32 devices in a mesh: row: 8 (over y, x, core), col: 4 (over z).
Axes of the slice: x: 2, y: 2, z: 4, core: 2. Of those that a mesh axis runs over, the one named last changes fastest.
Arguments:
- prior_voltage: float32 [4, 1024, 2048], P(None, 'row', 'col'), may hold values from 0.5 to 1.5
- baseline_admittance: float32 [4, 1024, 2048], P(None, 'row', 'col'), may hold values from 0.5 to 2
- block_warmth: float32 [4, 256, 512], P(None, 'row', 'col'), may hold values from 0 to 2
- interlayer_indicator: int32 [3, 1024, 2048], P(None, 'row', 'col'), may hold values 0 or 1
- feeder_indicator: int32 [4, 1024, 2048], P(None, 'row', 'col'), may hold values 0 or 1
- injected_amperes: float32 [4, 1024, 2048], P(None, 'row', 'col'), may hold values from 0.5 to 4
Outputs:
- revised_voltage: float32 [4, 1024, 2048], P(None, 'row', 'col')
- revised_warmth: float32 [4, 256, 512], P(None, 'row', 'col')
The draws below stay inside these ranges and needn't reach their ends.
All inputs are finite; a program needn't handle non-finite values. No bound on the sum of `interlayer_indicator` or of `feeder_indicator` on one device may be relied on, other than what follows from the above.
Results may differ from the reference program's by a relative error of at most 0.00002.
Values sent between devices are 32-bit elements; how exact they have to be, the bound alone decides.
No kernel may reach another device: no remote copies, remote signals or barrier semaphores. Data moves between devices by JAX's collectives and lax.ppermute only.
A program may use at most 128 MiB of HBM per device.

```python
import math
import jax
import jax.numpy as jnp
from jax import lax

LAYER_COUNT = 4
BLOCK_REFINE = 4
SWEEPS = 3
HEAT_SWEEPS = 4
NR = 1024
NC = 2048
BLOCK_HEIGHTWISE = 256
BLOCK_WIDTHWISE = 512


def touch_ends(result, rng, smallest, high):
    extent = result.shape
    index_at = [jax.random.randint(jax.random.fold_in(rng, axis), (), 0, extent[axis]) for axis in range(len(extent))]
    result = result.at[tuple(index_at)].set(smallest)
    longest = extent.index(max(extent))
    index_at[longest] = (index_at[longest] + 1) % extent[longest]
    return result.at[tuple(index_at)].set(high)


def levels(rng, extent, cuts, low, top_value):
    def one(position, parts):
        draws = jax.random.uniform(jax.random.fold_in(jax.random.fold_in(rng, 6), position), (parts,), jnp.float32, low / len(cuts), top_value / len(cuts))
        return jnp.repeat(jnp.exp(draws), extent[position] // parts).reshape((-1,) + (1,) * (len(extent) - position - 1))

    factor_of = one(*cuts[0])
    for cut in cuts[1:]:
        factor_of = factor_of * one(*cut)
    return factor_of


def setup_inputs(seed: int = 0) -> dict:
    key_list = jax.random.split(jax.random.key(seed), 7)
    prior_voltage = jnp.clip(0.5 + 1.0 * jax.random.uniform(key_list[0], (LAYER_COUNT, NR, NC), jnp.float32) ** levels(key_list[0], (LAYER_COUNT, NR, NC), ((1, 8), (2, 4)), -0.2, 0.2), 0.5, 1.5)
    baseline_admittance = jnp.clip(jnp.exp(math.log(2.0) - 1.3862944 * jax.random.uniform(key_list[1], (LAYER_COUNT, NR, NC), jnp.float32) ** levels(key_list[1], (LAYER_COUNT, NR, NC), ((1, 8), (2, 4)), -0.2, 0.2)), 0.5, 2.0)
    block_warmth = jnp.clip(2.0 * jax.random.uniform(key_list[2], (LAYER_COUNT, BLOCK_HEIGHTWISE, BLOCK_WIDTHWISE), jnp.float32) ** levels(key_list[2], (LAYER_COUNT, BLOCK_HEIGHTWISE, BLOCK_WIDTHWISE), ((1, 8), (2, 4)), -0.2, 0.2), 0.0, 2.0)
    interlayer_indicator = touch_ends((jax.random.randint(key_list[3], (LAYER_COUNT - 1, NR, NC), 0, 2) < 1).astype(jnp.int32), jax.random.fold_in(key_list[3], 1), 0, 1)
    feeder_indicator = touch_ends((jax.random.randint(key_list[4], (LAYER_COUNT, NR, NC), 0, 4) < 1).astype(jnp.int32), jax.random.fold_in(key_list[4], 1), 0, 1)
    injected_amperes = jnp.clip(jnp.exp(math.log(4.0) - 2.0794415 * jax.random.uniform(key_list[5], (LAYER_COUNT, NR, NC), jnp.float32) ** levels(key_list[5], (LAYER_COUNT, NR, NC), ((1, 8), (2, 4)), -0.2, 0.2)), 0.5, 4.0)
    return dict(prior_voltage=prior_voltage, baseline_admittance=baseline_admittance, block_warmth=block_warmth, interlayer_indicator=interlayer_indicator, feeder_indicator=feeder_indicator, injected_amperes=injected_amperes)


warmth_sensitivity = 0.5
via_cond = 1.0
leak_cond = 0.2
spectrum_low = 0.05
spectrum_high = 1.95
warming_weight = 0.3
layer_admittance = 1.0
drain_admittance = 1.0
heat_gain = 0.0625
interval_length = 0.12

def bordered_array(voltage_grid):
    return jnp.pad(voltage_grid, ((0, 0), (1, 1), (1, 1)))

def neighbours(voltage_grid):
    return (voltage_grid[:, :-2, 1:-1], voltage_grid[:, 2:, 1:-1], voltage_grid[:, 1:-1, :-2], voltage_grid[:, 1:-1, 2:])

def planar_edges(cond_pad):
    center = cond_pad[:, 1:-1, 1:-1]
    return tuple((jnp.sqrt(center * other) for other in neighbours(cond_pad)))

def vertical(voltage_grid, vias):
    nought_value = jnp.zeros_like(voltage_grid[:1])
    return jnp.concatenate([vias * voltage_grid[1:], nought_value], 0) + jnp.concatenate([nought_value, vias * voltage_grid[:-1]], 0)

def via_total(vias):
    nought_value = jnp.zeros_like(vias[:1])
    return jnp.concatenate([vias, nought_value], 0) + jnp.concatenate([nought_value, vias], 0)

def operate(field_pad, edges, vias, diag):
    center = field_pad[:, 1:-1, 1:-1]
    near = jnp.zeros_like(center)
    for edge, other in zip(edges, neighbours(field_pad)):
        near = near + edge * other
    return diag * center - near - vertical(center, vias)

def joule_power(field_pad, edges, vias):
    center = field_pad[:, 1:-1, 1:-1]
    total = leak_cond * center * center
    for edge, other in zip(edges, neighbours(field_pad)):
        total = total + 0.5 * edge * (center - other) ** 2
    drop = vias * (center[:-1] - center[1:]) ** 2
    nought_value = jnp.zeros_like(center[:1])
    return total + 0.5 * (jnp.concatenate([drop, nought_value], 0) + jnp.concatenate([nought_value, drop], 0))

def warming_increment(warmth_excess, diffusivity, warmth_border, diffusivity_border, warming_load):
    energy_flow = jnp.zeros_like(warmth_excess)
    for partner_warmth, partner_diffusivity in zip(neighbours(warmth_border), neighbours(diffusivity_border)):
        energy_flow = energy_flow + jnp.sqrt(diffusivity * partner_diffusivity) * (partner_warmth - warmth_excess)
    nought_value = jnp.zeros_like(warmth_excess[:1])
    upright_flow = layer_admittance * (jnp.concatenate([warmth_excess[1:] - warmth_excess[:-1], nought_value], 0) + jnp.concatenate([nought_value, warmth_excess[:-1] - warmth_excess[1:]], 0))
    layer_total = warmth_excess.shape[0]
    upper_layer = (lax.broadcasted_iota(jnp.int32, (layer_total, 1, 1), 0) == layer_total - 1).astype(jnp.float32)
    return warmth_excess + interval_length * (energy_flow + upright_flow + warming_load - drain_admittance * upper_layer * warmth_excess)

def reference(prior_voltage, baseline_admittance, block_warmth, interlayer_indicator, feeder_indicator, injected_amperes):
    warmth_on_points = jnp.repeat(jnp.repeat(block_warmth, BLOCK_REFINE, axis=1), BLOCK_REFINE, axis=2)
    admittance = baseline_admittance * jnp.exp(-warmth_sensitivity * warmth_on_points)
    vias = via_cond * interlayer_indicator.astype(jnp.float32)
    inject = feeder_indicator.astype(jnp.float32) * injected_amperes
    edges = planar_edges(bordered_array(admittance))
    diag = leak_cond + edges[0] + edges[1] + edges[2] + edges[3] + via_total(vias)
    center_c = 0.5 * (spectrum_high + spectrum_low)
    half = 0.5 * (spectrum_high - spectrum_low)
    sigma = center_c / half
    rho = 1.0 / sigma
    voltage_grid = prior_voltage
    resid = inject - operate(bordered_array(voltage_grid), edges, vias, diag)
    step = resid / (diag * center_c)
    for sweep in range(SWEEPS):
        voltage_grid = voltage_grid + step
        if sweep < SWEEPS - 1:
            resid = inject - operate(bordered_array(voltage_grid), edges, vias, diag)
            rho_new = 1.0 / (2.0 * sigma - rho)
            step = rho_new * rho * step + 2.0 * rho_new / half * (resid / diag)
            rho = rho_new
    power = joule_power(bordered_array(voltage_grid), edges, vias)
    layer_total, rows, cols = power.shape
    warming_load = power.reshape(layer_total, rows // BLOCK_REFINE, BLOCK_REFINE, cols // BLOCK_REFINE, BLOCK_REFINE).sum(axis=(2, 4)) * heat_gain
    warmth_excess = block_warmth
    for sweep in range(HEAT_SWEEPS):
        diffusivity = jnp.exp(-warming_weight * warmth_excess)
        warmth_excess = warming_increment(warmth_excess, diffusivity, bordered_array(warmth_excess), bordered_array(diffusivity), warming_load)
    return (voltage_grid, warmth_excess)
```

```python
import jax
import jax.numpy as jnp
from jax import lax
from jax.experimental import pallas as pl
from jax.experimental.pallas import tpu as pltpu
from jax.sharding import PartitionSpec as P

REFINE = 4
SWEEPS = 3
HEAT_SWEEPS = 4

warmth_sensitivity = 0.5
leak_cond = 0.2
spectrum_low = 0.05
spectrum_high = 1.95
warming_weight = 0.3
heat_gain = 0.0625
interval_length = 0.12

SUB = 8
LANE = 128
REACH = 4
BOTH = ("row", "col")
HIGHEST = lax.Precision.HIGHEST


def row_swaps(rows, cols, first):
    pairs = []
    for r in range(rows):
        for c in range(cols):
            p = r + 1 if (r - first) % 2 == 0 else r - 1
            if 0 <= p < rows:
                pairs.append((r * cols + c, p * cols + c))
            elif c ^ 1 < cols:
                pairs.append((r * cols + c, r * cols + (c ^ 1)))
    return pairs


def col_swaps(rows, cols, first):
    pairs = []
    for r in range(rows):
        for c in range(cols):
            p = c + 1 if (c - first) % 2 == 0 else c - 1
            if 0 <= p < cols:
                pairs.append((r * cols + c, r * cols + p))
            elif r ^ 1 < rows:
                pairs.append((r * cols + c, (r ^ 1) * cols + c))
    return pairs


def iota(shape, dim):
    return lax.broadcasted_iota(jnp.int32, shape, dim)


def uniform(flag, shape):
    return jnp.full(shape, flag.astype(jnp.int32), jnp.int32) == 1


def place(axis):
    at = lax.axis_index(axis)
    return at % 2 == 0, at > 0, at < lax.axis_size(axis) - 1


def dot(a, b):
    return jnp.dot(a, b, precision=HIGHEST, preferred_element_type=jnp.float32)


def spread_lanes(cells, nodes):
    same = lax.shift_right_logical(iota((cells, nodes), 1), 2) == iota((cells, nodes), 0)
    return same.astype(jnp.float32)


def gather_lanes(nodes, cells):
    same = lax.shift_right_logical(iota((nodes, cells), 0), 2) == iota((nodes, cells), 1)
    return same.astype(jnp.float32)


def pack_rows_kernel(x_t, x_b, b_t, b_b, w_t, w_b, v_t, v_b, f_t, f_b, a_t, a_b, e_ref, o_ref):
    layers, _, cols = x_t.shape
    cells = w_t.shape[2]
    even, _, _ = place("row")
    low = iota((SUB, cols), 0) < REACH
    spread = spread_lanes(cells, cols)

    def planes(x, b, w, v, f, a, cell_row):
        warm = jnp.concatenate([w[l, cell_row : cell_row + 1, :] for l in range(layers)] * 2, 0)
        warm = dot(jnp.exp(-0.5 * warmth_sensitivity * warm), spread)
        xs = [x[l] for l in range(layers)]
        gs = [jnp.sqrt(b[l]) * warm[l : l + 1] for l in range(layers)]
        js = [f[l].astype(jnp.float32) * a[l] for l in range(layers)]
        vs = [v[l].astype(jnp.float32) for l in range(layers - 1)]
        ws = [jnp.concatenate([w[l] for l in range(layers)], axis=1)]
        return xs + gs, js + vs + ws

    top_a, top_b = planes(x_t, b_t, w_t, v_t, f_t, a_t, 0)
    bot_a, bot_b = planes(x_b, b_b, w_b, v_b, f_b, a_b, SUB - 1)
    pick = uniform(even, (SUB, cols))
    for k in range(2 * layers):
        top = jnp.where(low, top_a[k], pltpu.roll(top_b[k], REACH, 0))
        bot = jnp.where(low, pltpu.roll(bot_a[k], REACH, 0), bot_b[k])
        e_ref[k] = jnp.where(pick, bot, top)
        o_ref[k] = jnp.where(pick, top, bot)


def row_margin(e_ref, o_ref, plane, cols, half):
    even, above, below = place("row")
    k = plane % half
    e, o = e_ref[k, :, cols], o_ref[k, :, cols]
    pick = uniform(even, e.shape)
    top, bot = jnp.where(pick, o, e), jnp.where(pick, e, o)
    if plane < half:
        top = pltpu.roll(top, REACH, 0)
    else:
        bot = pltpu.roll(bot, REACH, 0)
    return (
        jnp.where(uniform(above, top.shape), top, 0.0),
        jnp.where(uniform(below, bot.shape), bot, 0.0),
    )


def fields_kernel(b_ref, w_ref, f_ref, a_ref, g_ref, j_ref):
    _, rows, cols = b_ref.shape
    _, cell_rows, cells = w_ref.shape
    warm = jnp.exp(-0.5 * warmth_sensitivity * w_ref[0])
    warm = dot(gather_lanes(rows, cell_rows), dot(warm, spread_lanes(cells, cols)))
    g_ref[0] = jnp.sqrt(b_ref[0]) * warm
    j_ref[0] = f_ref[0].astype(jnp.float32) * a_ref[0]


def pack_cols_kernel(
    x_l, x_r, g_l, g_r, j_l, j_r, v_l, v_r, w_ref, re_ref, ro_ref, e_ref, o_ref
):
    layers, rows, _ = x_l.shape
    cols = re_ref.shape[2]
    half = 2 * layers
    cell_rows, cells = w_ref.shape[1:]
    height, cell_height = rows + 2 * SUB, cell_rows + 2 * SUB
    even, _, _ = place("col")
    lane = iota((height, LANE), 1)
    slot, low = lax.shift_right_logical(lane, 3), lane % 8 < REACH
    cell_lane = iota((cell_height, LANE), 1)
    cell_slot, cell_high = lax.shift_right_logical(cell_lane, 3), cell_lane % 8 >= REACH
    sides = []
    for side, refs in enumerate(((x_l, g_l, j_l, v_l), (x_r, g_r, j_r, v_r))):
        tile = slice(0, LANE) if side == 0 else slice(cols - LANE, cols)
        own = [ref[l] for ref in refs for l in range(ref.shape[0])]
        out = jnp.zeros((height, LANE), jnp.float32)
        for p, value in enumerate(own):
            top, bot = row_margin(re_ref, ro_ref, p, tile, half)
            value = jnp.concatenate([top, value.astype(jnp.float32), bot], axis=0)
            value = pltpu.roll(value, (8 * p + REACH * side) % LANE, 1)
            out = jnp.where((slot == p) & low, value, out)
        head = out[:cell_height]
        for l in range(layers):
            tile = slice(l * cells, (l + 1) * cells)
            top, bot = row_margin(re_ref, ro_ref, 2 * half - 1, tile, half)
            value = jnp.concatenate([top, w_ref[l], bot], axis=0)
            value = pltpu.roll(value, (8 * l + REACH + REACH * side) % LANE, 1)
            head = jnp.where((cell_slot == l) & cell_high, value, head)
        sides.append(jnp.concatenate([head, out[cell_height:]], axis=0))
    left, right = sides
    pick = uniform(even, (height, LANE))
    e_ref[...] = jnp.where(pick, right, left)
    o_ref[...] = jnp.where(pick, left, right)


def col_margin(e, o, high):
    even, before, after = place("col")
    lane = iota(e.shape, 1)
    pick = uniform(even, e.shape)
    right, left = jnp.where(pick, e, o), jnp.where(pick, o, e)
    right = jnp.where(uniform(after, e.shape), right, 0.0)
    left = jnp.where(uniform(before, e.shape), left, 0.0)
    own_half = lane % 8 >= REACH if high else lane % 8 < REACH
    return jnp.where(own_half, right, pltpu.roll(left, LANE - REACH, 1))


def margin_tile(mixed, shift):
    lane = iota(mixed.shape, 1)
    value = mixed if shift == 0 else pltpu.roll(mixed, LANE - shift, 1)
    return jnp.where((lane < REACH) | (lane >= LANE - REACH), value, 0.0)


def rows_of(i):
    return pl.ds(pl.multiple_of(i * SUB, SUB), SUB)


def above_below(before, here, after):
    sub = iota(here.shape, 0)
    up = jnp.where(sub == 0, pltpu.roll(before, 1, 0), pltpu.roll(here, 1, 0))
    down = jnp.where(sub == SUB - 1, pltpu.roll(after, SUB - 1, 0), pltpu.roll(here, SUB - 1, 0))
    return up, down


def around(ref, l, i):
    here = ref[l, rows_of(i + 1), :]
    up, down = above_below(ref[l, rows_of(i), :], here, ref[l, rows_of(i + 2), :])
    width = here.shape[1]
    return (up + down) + (pltpu.roll(here, 1, 1) + pltpu.roll(here, width - 1, 1))


def sweeps_kernel(
    x_ref, g_ref, j_ref, v_ref, re_ref, ro_ref, ce_ref, co_ref,
    xo_ref, h_ref, he_ref, ho_ref,
    X, G, J, V, W0, W1, D, DI, GD, PW,
):
    layers, rows, cols = x_ref.shape
    half = 2 * layers
    groups = rows // SUB + 2
    own_rows = pl.ds(2 * SUB, rows)
    mixed = col_margin(ce_ref[...], co_ref[...], False)
    plane = 0
    for ref, pad in ((x_ref, X), (g_ref, G), (j_ref, J), (v_ref, V)):
        for l in range(ref.shape[0]):
            top, bot = row_margin(re_ref, ro_ref, plane, slice(0, cols), half)
            pad[l, SUB : 2 * SUB, 0:cols] = top
            pad[l, rows + 2 * SUB : rows + 3 * SUB, 0:cols] = bot
            pad[l, own_rows, 0:cols] = ref[l].astype(jnp.float32)
            pad[l, SUB : rows + 3 * SUB, cols : cols + LANE] = margin_tile(mixed, 8 * plane)
            plane += 1

    def each(body, first, last, unroll):
        lax.fori_loop(first, last, lambda i, c: (body(i), c)[1], 0, unroll=unroll)

    def start(i):
        r = rows_of(i + 1)
        for l in range(layers):
            W0[l, r, :] = G[l, r, :] * X[l, r, :]

    each(start, 0, groups, 3)

    center_c = 0.5 * (spectrum_high + spectrum_low)
    half_c = 0.5 * (spectrum_high - spectrum_low)
    sigma = center_c / half_c
    rho = 1.0 / sigma

    def upright(l, xs, vs):
        if l == 0:
            return vs[0] * xs[1]
        if l == layers - 1:
            return vs[l - 1] * xs[l - 1]
        return vs[l] * xs[l + 1] + vs[l - 1] * xs[l - 1]

    def first(i):
        r = rows_of(i + 1)
        xs = [X[l, r, :] for l in range(layers)]
        vs = [V[l, r, :] for l in range(layers - 1)]
        for l in range(layers):
            g = G[l, r, :]
            diag = leak_cond + g * around(G, l, i)
            if l < layers - 1:
                diag = diag + vs[l]
            if l > 0:
                diag = diag + vs[l - 1]
            inverse = 1.0 / diag
            gd = g * inverse
            jd = J[l, r, :] * inverse
            d = (jd + gd * around(W0, l, i) + inverse * upright(l, xs, vs) - xs[l]) / center_c
            x = xs[l] + d
            DI[l, r, :] = inverse
            GD[l, r, :] = gd
            J[l, r, :] = jd
            D[l, r, :] = d
            X[l, r, :] = x
            W1[l, r, :] = g * x

    each(first, 0, groups, 3)

    source, target = W1, W0
    for sweep in range(SWEEPS - 1):
        rho_new = 1.0 / (2.0 * sigma - rho)
        keep, gain = rho_new * rho, 2.0 * rho_new / half_c
        rho = rho_new
        last = sweep == SWEEPS - 2

        def later(i, source=source, target=target, keep=keep, gain=gain, last=last):
            r = rows_of(i + 1)
            xs = [X[l, r, :] for l in range(layers)]
            vs = [V[l, r, :] for l in range(layers - 1)]
            for l in range(layers):
                resid = (
                    J[l, r, :]
                    + GD[l, r, :] * around(source, l, i)
                    + DI[l, r, :] * upright(l, xs, vs)
                    - xs[l]
                )
                d = keep * D[l, r, :] + gain * resid
                x = xs[l] + d
                X[l, r, :] = x
                if not last:
                    D[l, r, :] = d
                    target[l, r, :] = G[l, r, :] * x

        each(later, 0, groups, 3)
        source, target = target, source

    def power(i):
        r = rows_of(i + 1)
        width = cols + LANE
        xs = [X[l, r, :] for l in range(layers)]
        drops = [
            V[l, r, 0:cols] * (xs[l][:, :cols] - xs[l + 1][:, :cols]) ** 2
            for l in range(layers - 1)
        ]
        for l in range(layers):
            x, g = xs[l], G[l, r, :]
            step = x - pltpu.roll(x, width - 1, 1)
            edge = (g * pltpu.roll(g, width - 1, 1)) * (step * step)
            flat = (edge + pltpu.roll(edge, 1, 1))[:, :cols]
            x, g = x[:, :cols], g[:, :cols]
            x_up, x_down = above_below(X[l, rows_of(i), 0:cols], x, X[l, rows_of(i + 2), 0:cols])
            g_up, g_down = above_below(G[l, rows_of(i), 0:cols], g, G[l, rows_of(i + 2), 0:cols])
            total = flat + g * (g_up * (x - x_up) ** 2 + g_down * (x - x_down) ** 2)
            if l < layers - 1:
                total = total + drops[l]
            if l > 0:
                total = total + drops[l - 1]
            PW[l, rows_of(i - 1), :] = leak_cond * (x * x) + 0.5 * total

    each(power, 1, groups - 1, 3)
    even, _, _ = place("row")
    cell_rows, cells = h_ref.shape[1:]
    fold_rows = spread_lanes(cell_rows, rows)
    fold_cols = gather_lanes(cols, cells)
    pick = uniform(even, (SUB, cells))
    for l in range(layers):
        xo_ref[l] = X[l, own_rows, 0:cols]
        heat = dot(dot(fold_rows, PW[l]), fold_cols) * heat_gain
        h_ref[l] = heat
        top, bot = heat[:SUB], heat[cell_rows - SUB :]
        he_ref[l] = jnp.where(pick, bot, top)
        ho_ref[l] = jnp.where(pick, top, bot)


def heat_rows(h_ref, e_ref, o_ref, l):
    even, above, below = place("row")
    e, o = e_ref[l], o_ref[l]
    pick = uniform(even, e.shape)
    top = jnp.where(uniform(above, e.shape), jnp.where(pick, o, e), 0.0)
    bot = jnp.where(uniform(below, e.shape), jnp.where(pick, e, o), 0.0)
    return jnp.concatenate([top, h_ref[l], bot], axis=0)


def pack_heat_kernel(h_ref, re_ref, ro_ref, e_ref, o_ref):
    layers, cell_rows, cells = h_ref.shape
    height = cell_rows + 2 * SUB
    even, _, _ = place("col")
    lane = iota((height, LANE), 1)
    slot, low = lax.shift_right_logical(lane, 3), lane % 8 < REACH
    left = right = jnp.zeros((height, LANE), jnp.float32)
    for l in range(layers):
        value = heat_rows(h_ref, re_ref, ro_ref, l)
        mine = (slot == l) & low
        left = jnp.where(mine, pltpu.roll(value[:, :LANE], 8 * l, 1) if l else value[:, :LANE], left)
        right = jnp.where(mine, pltpu.roll(value[:, cells - LANE :], 8 * l + REACH, 1), right)
    pick = uniform(even, (height, LANE))
    e_ref[...] = jnp.where(pick, right, left)
    o_ref[...] = jnp.where(pick, left, right)


def warm_kernel(
    w_ref, h_ref, re_ref, ro_ref, ce_ref, co_ref, hre_ref, hro_ref, hce_ref, hco_ref, out_ref
):
    layers, cell_rows, cells = w_ref.shape
    half = 2 * layers
    height, width = cell_rows + 2 * SUB, cells + LANE
    warm_mixed = col_margin(ce_ref[0:height, :], co_ref[0:height, :], True)
    heat_mixed = col_margin(hce_ref[...], hco_ref[...], False)
    theta, heat = [], []
    for l in range(layers):
        top, bot = row_margin(
            re_ref, ro_ref, 2 * half - 1, slice(l * cells, (l + 1) * cells), half
        )
        own = jnp.concatenate([top, w_ref[l], bot], axis=0)
        theta.append(jnp.concatenate([own, margin_tile(warm_mixed, 8 * l + REACH)], axis=1))
        own = heat_rows(h_ref, hre_ref, hro_ref, l)
        heat.append(jnp.concatenate([own, margin_tile(heat_mixed, 8 * l)], axis=1))
    _, above, below = place("row")
    _, before, after = place("col")
    shape = (height, width)
    r, c = iota(shape, 0), iota(shape, 1)
    inside = (uniform(above, shape) | (r >= SUB)) & (uniform(below, shape) | (r < height - SUB))
    inside = inside & (uniform(after, shape) | (c < cells) | (c >= cells + LANE // 2))
    inside = inside & (uniform(before, shape) | (c < cells + LANE // 2))

    def around_cells(v):
        return (pltpu.roll(v, 1, 0) + pltpu.roll(v, height - 1, 0)) + (
            pltpu.roll(v, 1, 1) + pltpu.roll(v, width - 1, 1)
        )

    for _ in range(HEAT_SWEEPS):
        later = []
        for l in range(layers):
            t = theta[l]
            q = jnp.where(inside, jnp.exp(-0.5 * warming_weight * t), 0.0)
            change = q * (around_cells(q * t) - t * around_cells(q)) + heat[l]
            if l < layers - 1:
                change = change + (theta[l + 1] - t)
            if l > 0:
                change = change + (theta[l - 1] - t)
            if l == layers - 1:
                change = change - t
            later.append(t + interval_length * change)
        theta = later
    for l in range(layers):
        out_ref[l] = theta[l][SUB : SUB + cell_rows, :cells]


def on_device(x, base, warm, via, feeder, amps):
    layers, rows, cols = x.shape
    _, cell_rows, cells = warm.shape
    f32 = jnp.float32
    mesh_rows, mesh_cols = lax.axis_size("row"), lax.axis_size("col")
    last_row, last_cell_row, last_col = rows // SUB - 1, cell_rows // SUB - 1, cols // LANE - 1

    def shape(*dims):
        return jax.ShapeDtypeStruct(dims, f32)

    def edge_rows(a, at):
        return pl.BlockSpec((a.shape[0], SUB, a.shape[2]), lambda _, at=at: (0, at, 0))

    def edge_cols(a, at):
        return pl.BlockSpec((a.shape[0], a.shape[1], LANE), lambda _, at=at: (0, 0, at))

    def full(a):
        return pl.BlockSpec(a.shape, lambda _, n=len(a.shape): (0,) * n)

    def swap(e, o, tables):
        return tuple(
            lax.ppermute(m, BOTH, tables(mesh_rows, mesh_cols, first)) for first, m in enumerate((e, o))
        )

    params = pltpu.CompilerParams(vmem_limit_bytes=40 * 1024 * 1024)
    row_args, row_specs = [], []
    for a in (x, base, warm, via, feeder, amps):
        end = last_cell_row if a is warm else last_row
        row_args += [a, a]
        row_specs += [edge_rows(a, 0), edge_rows(a, end)]
    message = shape(2 * layers, SUB, cols)
    e, o = pl.pallas_call(
        pack_rows_kernel,
        grid=(1,),
        in_specs=row_specs,
        out_specs=(full(message), full(message)),
        out_shape=(message, message),
        compiler_params=pltpu.CompilerParams(vmem_limit_bytes=60 * 1024 * 1024),
        name="pack_rows",
    )(*row_args)
    row_e, row_o = swap(e, o, row_swaps)

    fine = pl.BlockSpec((1, rows, cols), lambda l: (l, 0, 0))
    coarse = pl.BlockSpec((1, cell_rows, cells), lambda l: (l, 0, 0))
    g, inject = pl.pallas_call(
        fields_kernel,
        grid=(layers,),
        in_specs=[fine, coarse, fine, fine],
        out_specs=(fine, fine),
        out_shape=(shape(layers, rows, cols),) * 2,
        compiler_params=params,
        name="fields",
        cost_estimate=pl.CostEstimate(flops=8 * x.size, bytes_accessed=20 * x.size, transcendentals=x.size),
    )(base, warm, feeder, amps)

    col_args, col_specs = [], []
    for a in (x, g, inject, via):
        col_args += [a, a]
        col_specs += [edge_cols(a, 0), edge_cols(a, last_col)]
    message = shape(rows + 2 * SUB, LANE)
    e, o = pl.pallas_call(
        pack_cols_kernel,
        grid=(1,),
        in_specs=col_specs + [full(warm), full(row_e), full(row_o)],
        out_specs=(full(message), full(message)),
        out_shape=(message, message),
        compiler_params=params,
        name="pack_cols",
    )(*col_args, warm, row_e, row_o)
    col_e, col_o = swap(e, o, col_swaps)

    pad = pltpu.VMEM((layers, rows + 4 * SUB, cols + LANE), f32)
    pad_via = pltpu.VMEM((layers - 1, rows + 4 * SUB, cols + LANE), f32)
    edge = shape(layers, SUB, cells)
    voltage, heat, e, o = pl.pallas_call(
        sweeps_kernel,
        out_shape=(shape(layers, rows, cols), shape(layers, cell_rows, cells), edge, edge),
        scratch_shapes=[pad, pad, pad, pad_via, pad, pad, pad, pad, pad, pltpu.VMEM((layers, rows, cols), f32)],
        compiler_params=params,
        name="sweeps",
    )(x, g, inject, via, row_e, row_o, col_e, col_o)
    heat_row_e, heat_row_o = swap(e, o, row_swaps)

    message = shape(cell_rows + 2 * SUB, LANE)
    e, o = pl.pallas_call(
        pack_heat_kernel,
        out_shape=(message, message),
        compiler_params=params,
        name="pack_heat",
    )(heat, heat_row_e, heat_row_o)
    heat_col_e, heat_col_o = swap(e, o, col_swaps)

    warmth = pl.pallas_call(
        warm_kernel,
        out_shape=shape(layers, cell_rows, cells),
        compiler_params=params,
        name="warm",
    )(warm, heat, row_e, row_o, col_e, col_o, heat_row_e, heat_row_o, heat_col_e, heat_col_o)
    return voltage, warmth


def solution(mesh):
    placed = P(None, "row", "col")
    return jax.shard_map(
        on_device,
        mesh=mesh,
        in_specs=(placed,) * 6,
        out_specs=(placed, placed),
        check_vma=False,
    )
```

```python
import jax
import jax.numpy as jnp
from jax import lax
from jax.experimental import pallas as pl
from jax.experimental.pallas import tpu as pltpu
from jax.sharding import PartitionSpec as P

REFINE = 4
SWEEPS = 3
HEAT_SWEEPS = 4

warmth_sensitivity = 0.5
leak_cond = 0.2
spectrum_low = 0.05
spectrum_high = 1.95
warming_weight = 0.3
heat_gain = 0.0625
interval_length = 0.12

SUB = 8
LANE = 128
REACH = 4
BOTH = ("row", "col")
HIGHEST = lax.Precision.HIGHEST


def row_swaps(rows, cols, first):
    pairs = []
    for r in range(rows):
        for c in range(cols):
            p = r + 1 if (r - first) % 2 == 0 else r - 1
            if 0 <= p < rows:
                pairs.append((r * cols + c, p * cols + c))
            elif c ^ 1 < cols:
                pairs.append((r * cols + c, r * cols + (c ^ 1)))
    return pairs


def col_swaps(rows, cols, first):
    pairs = []
    for r in range(rows):
        for c in range(cols):
            p = c + 1 if (c - first) % 2 == 0 else c - 1
            if 0 <= p < cols:
                pairs.append((r * cols + c, r * cols + p))
            elif r ^ 1 < rows:
                pairs.append((r * cols + c, (r ^ 1) * cols + c))
    return pairs


def iota(shape, dim):
    return lax.broadcasted_iota(jnp.int32, shape, dim)


def uniform(flag, shape):
    return jnp.full(shape, flag.astype(jnp.int32), jnp.int32) == 1


def place(axis):
    at = lax.axis_index(axis)
    return at % 2 == 0, at > 0, at < lax.axis_size(axis) - 1


def dot(a, b):
    return jnp.dot(a, b, precision=HIGHEST, preferred_element_type=jnp.float32)


def spread_lanes(cells, nodes):
    same = lax.shift_right_logical(iota((cells, nodes), 1), 2) == iota((cells, nodes), 0)
    return same.astype(jnp.float32)


def gather_lanes(nodes, cells):
    same = lax.shift_right_logical(iota((nodes, cells), 0), 2) == iota((nodes, cells), 1)
    return same.astype(jnp.float32)


def pack_rows_kernel(x_t, x_b, b_t, b_b, w_t, w_b, v_t, v_b, f_t, f_b, a_t, a_b, e_ref, o_ref):
    layers, _, cols = x_t.shape
    cells = w_t.shape[2]
    even, _, _ = place("row")
    low = iota((SUB, cols), 0) < REACH
    spread = spread_lanes(cells, cols)

    def planes(x, b, w, v, f, a, cell_row):
        warm = jnp.concatenate([w[l, cell_row : cell_row + 1, :] for l in range(layers)] * 2, 0)
        warm = dot(jnp.exp(-0.5 * warmth_sensitivity * warm), spread)
        xs = [x[l] for l in range(layers)]
        gs = [jnp.sqrt(b[l]) * warm[l : l + 1] for l in range(layers)]
        js = [f[l].astype(jnp.float32) * a[l] for l in range(layers)]
        vs = [v[l].astype(jnp.float32) for l in range(layers - 1)]
        ws = [jnp.concatenate([w[l] for l in range(layers)], axis=1)]
        return xs + gs, js + vs + ws

    top_a, top_b = planes(x_t, b_t, w_t, v_t, f_t, a_t, 0)
    bot_a, bot_b = planes(x_b, b_b, w_b, v_b, f_b, a_b, SUB - 1)
    pick = uniform(even, (SUB, cols))
    for k in range(2 * layers):
        top = jnp.where(low, top_a[k], pltpu.roll(top_b[k], REACH, 0))
        bot = jnp.where(low, pltpu.roll(bot_a[k], REACH, 0), bot_b[k])
        e_ref[k] = jnp.where(pick, bot, top)
        o_ref[k] = jnp.where(pick, top, bot)


def row_margin(e_ref, o_ref, plane, cols, half):
    even, above, below = place("row")
    k = plane % half
    e, o = e_ref[k, :, cols], o_ref[k, :, cols]
    pick = uniform(even, e.shape)
    top, bot = jnp.where(pick, o, e), jnp.where(pick, e, o)
    if plane < half:
        top = pltpu.roll(top, REACH, 0)
    else:
        bot = pltpu.roll(bot, REACH, 0)
    return (
        jnp.where(uniform(above, top.shape), top, 0.0),
        jnp.where(uniform(below, bot.shape), bot, 0.0),
    )


def pack_cols_kernel(
    x_l, x_r, g_l, g_r, j_l, j_r, v_l, v_r, w_ref, re_ref, ro_ref, e_ref, o_ref
):
    layers, rows, _ = x_l.shape
    cols = re_ref.shape[2]
    half = 2 * layers
    cell_rows, cells = w_ref.shape[1:]
    height, cell_height = rows + 2 * SUB, cell_rows + 2 * SUB
    even, _, _ = place("col")
    lane = iota((height, LANE), 1)
    slot, low = lax.shift_right_logical(lane, 3), lane % 8 < REACH
    cell_lane = iota((cell_height, LANE), 1)
    cell_slot, cell_high = lax.shift_right_logical(cell_lane, 3), cell_lane % 8 >= REACH
    sides = []
    for side, refs in enumerate(((x_l, g_l, j_l, v_l), (x_r, g_r, j_r, v_r))):
        tile = slice(0, LANE) if side == 0 else slice(cols - LANE, cols)
        own = [ref[l] for ref in refs for l in range(ref.shape[0])]
        out = jnp.zeros((height, LANE), jnp.float32)
        for p, value in enumerate(own):
            top, bot = row_margin(re_ref, ro_ref, p, tile, half)
            value = jnp.concatenate([top, value.astype(jnp.float32), bot], axis=0)
            value = pltpu.roll(value, (8 * p + REACH * side) % LANE, 1)
            out = jnp.where((slot == p) & low, value, out)
        head = out[:cell_height]
        for l in range(layers):
            tile = slice(l * cells, (l + 1) * cells)
            top, bot = row_margin(re_ref, ro_ref, 2 * half - 1, tile, half)
            value = jnp.concatenate([top, w_ref[l], bot], axis=0)
            value = pltpu.roll(value, (8 * l + REACH + REACH * side) % LANE, 1)
            head = jnp.where((cell_slot == l) & cell_high, value, head)
        sides.append(jnp.concatenate([head, out[cell_height:]], axis=0))
    left, right = sides
    pick = uniform(even, (height, LANE))
    e_ref[...] = jnp.where(pick, right, left)
    o_ref[...] = jnp.where(pick, left, right)


def col_margin(e, o, high, back):
    even, before, after = place("col")
    lane = iota(e.shape, 1)
    pick = uniform(even, e.shape)
    right, left = jnp.where(pick, e, o), jnp.where(pick, o, e)
    right = jnp.where(uniform(after, e.shape), right, 0.0)
    left = jnp.where(uniform(before, e.shape), left, 0.0)
    own_half = lane % 8 >= REACH if high else lane % 8 < REACH
    return jnp.where(own_half, right, pltpu.roll(left, LANE - back, 1))


def margin_tile(mixed, shift):
    lane = iota(mixed.shape, 1)
    value = mixed if shift == 0 else pltpu.roll(mixed, LANE - shift, 1)
    return jnp.where((lane < REACH) | (lane >= LANE - REACH), value, 0.0)


CENTER = 0.5 * (spectrum_high + spectrum_low)
HALF = 0.5 * (spectrum_high - spectrum_low)
SIGMA = CENTER / HALF


def sweep_gains():
    rho, gains = 1.0 / SIGMA, []
    for _ in range(SWEEPS - 1):
        rho_new = 1.0 / (2.0 * SIGMA - rho)
        gains.append((rho_new * rho, 2.0 * rho_new / HALF))
        rho = rho_new
    return gains


def tile_rows(i):
    return pl.ds(pl.multiple_of(i * SUB, SUB), SUB)


def each(first, last, unroll, body):
    if unroll >= last - first:
        for i in range(first, last):
            body(i)
    else:
        lax.fori_loop(first, last, lambda i, c: (body(i), c)[1], 0, unroll=unroll)


def before(i):
    return max(i - 1, 0) if isinstance(i, int) else jnp.maximum(i - 1, 0)


def after(i, groups):
    return min(i + 1, groups - 1) if isinstance(i, int) else jnp.minimum(i + 1, groups - 1)


def shifted_down(here, nxt):
    return jnp.where(
        iota(here.shape, 0) == SUB - 1, pltpu.roll(nxt, SUB - 1, 0), pltpu.roll(here, SUB - 1, 0)
    )


def shifted_up(prev, here):
    return jnp.where(iota(here.shape, 0) == 0, pltpu.roll(prev, 1, 0), pltpu.roll(here, 1, 0))


def around(ref, l, i, groups):
    here = ref[l, tile_rows(i), :]
    width = here.shape[1]
    up = shifted_up(ref[l, tile_rows(before(i)), :], here)
    down = shifted_down(here, ref[l, tile_rows(after(i, groups)), :])
    return up, down, pltpu.roll(here, 1, 1), pltpu.roll(here, width - 1, 1)


def added(four):
    return (four[0] + four[1]) + (four[2] + four[3])


def upright(l, xs, vs):
    layers = len(xs)
    if l == 0:
        return vs[0] * xs[1]
    if l == layers - 1:
        return vs[l - 1] * xs[l - 1]
    return vs[l] * xs[l + 1] + vs[l - 1] * xs[l - 1]


def load_vias(V, r):
    return [V[l, r, :].astype(jnp.float32) for l in range(V.shape[0])]


def first_sweep(unroll, X, G, J, V, W0, XN, WN, D, DI, GD, JD, EH, EV):
    layers, height, _ = X.shape
    groups = height // SUB

    def start(i):
        r = tile_rows(i)
        for l in range(layers):
            W0[l, r, :] = G[l, r, :] * X[l, r, :]

    each(0, groups, unroll, start)

    def body(i):
        r = tile_rows(i)
        xs = [X[l, r, :] for l in range(layers)]
        vs = load_vias(V, r)
        for l in range(layers):
            g = G[l, r, :]
            four = around(G, l, i, groups)
            diag = leak_cond + g * added(four)
            EV[l, r, :] = g * four[1]
            EH[l, r, :] = g * four[3]
            if l < layers - 1:
                diag = diag + vs[l]
            if l > 0:
                diag = diag + vs[l - 1]
            inverse = 1.0 / diag
            gd, jd = g * inverse, J[l, r, :] * inverse
            near = added(around(W0, l, i, groups))
            d = (jd + gd * near + inverse * upright(l, xs, vs) - xs[l]) / CENTER
            x = xs[l] + d
            DI[l, r, :], GD[l, r, :], JD[l, r, :], D[l, r, :] = inverse, gd, jd, d
            XN[l, r, :] = x
            WN[l, r, :] = g * x

    each(0, groups, unroll, body)


def next_sweep(unroll, keep, gain, X, V, W, D, DI, GD, JD, G, XN, WN=None, DN=None):
    layers, height, _ = X.shape
    groups = height // SUB

    def body(i):
        r = tile_rows(i)
        xs = [X[l, r, :] for l in range(layers)]
        vs = load_vias(V, r)
        for l in range(layers):
            near = added(around(W, l, i, groups))
            resid = (
                JD[l, r, :] + GD[l, r, :] * near + DI[l, r, :] * upright(l, xs, vs) - xs[l]
            )
            d = keep * D[l, r, :] + gain * resid
            x = xs[l] + d
            XN[l, r, :] = x
            if WN is not None:
                DN[l, r, :] = d
                WN[l, r, :] = G[l, r, :] * x

    each(0, groups, unroll, body)


def later_sweeps(unroll, X, V, W, D, DI, GD, JD, G, WN, XN, DN):
    gains = sweep_gains()
    x, w, d, other = X, W, D, WN
    for at, (keep, gain) in enumerate(gains):
        if at == len(gains) - 1:
            next_sweep(unroll, keep, gain, x, V, w, d, DI, GD, JD, G, XN)
        else:
            next_sweep(unroll, keep, gain, x, V, w, d, DI, GD, JD, G, XN, other, DN)
            assert len(gains) <= 2
            x, w, d = XN, other, DN


def power_rows(first, last, unroll, X, V, EH, EV, PA, PB, PD):
    layers, height, width = X.shape
    groups = height // SUB
    share = jnp.where(iota((SUB, width), 0) % REFINE == REFINE - 1, 0.5, 1.0)
    lane_share = jnp.where(iota((SUB, width), 1) % REFINE == REFINE - 1, 1.0, 2.0)

    def fold(v):
        v = v + pltpu.roll(v, SUB - 1, 0)
        return v + pltpu.roll(v, SUB - 2, 0)

    def body(i):
        r = tile_rows(i)
        out = tile_rows(i + 1)
        xs = [X[l, r, :] for l in range(layers)]
        vs = load_vias(V, r)
        drops = [0.5 * vs[l] * (xs[l] - xs[l + 1]) ** 2 for l in range(layers - 1)]
        for l in range(layers):
            x = xs[l]
            across = x - pltpu.roll(x, width - 1, 1)
            down = x - shifted_down(x, X[l, tile_rows(after(i, groups)), :])
            across = 0.5 * EH[l, r, :] * (across * across)
            down = EV[l, r, :] * (down * down)
            total = leak_cond * (x * x) + share * down + lane_share * across
            if l < layers - 1:
                total = total + drops[l]
            if l > 0:
                total = total + drops[l - 1]
            total, across = fold(total), fold(across)
            for t in range(width // LANE):
                tile = slice(t * LANE, (t + 1) * LANE)
                PA[l, t, out, :] = total[:, tile]
                PB[l, t, out, :] = across[:, tile]
                PD[l, t, out, :] = down[:, tile]

    each(first, last, unroll, body)


def fold_power(row, cells, PA, PB, PD, same, left):
    layers = PA.shape[0]
    at = pl.ds(row + SUB, cells, stride=REFINE)
    up = pl.ds(row + SUB - 1, cells, stride=REFINE)
    tiles = range(PA.shape[1])
    a = [
        jnp.concatenate([PA[l, t, at, :] + 0.5 * PD[l, t, up, :] for t in tiles], 1)
        for l in range(layers)
    ]
    b = [jnp.concatenate([PB[l, t, at, :] for t in tiles], 1) for l in range(layers)]
    a, b = jnp.concatenate(a, 0), jnp.concatenate(b, 0)
    heat = (dot(a, same) + dot(b, left)) * heat_gain
    return [heat[l * cells : (l + 1) * cells] for l in range(layers)]


def fold_matrices(nodes, cells):
    n, c = iota((nodes, cells), 0), iota((nodes, cells), 1)
    same = lax.shift_right_logical(n, 2) == c
    return same.astype(jnp.float32), (n == REFINE * c - 1).astype(jnp.float32)


def bulk_first_kernel(
    x_ref, b_ref, w_ref, v_ref, f_ref, a_ref,
    g_ref, j_ref, XN, WN, D, DI, GD, JD, EH, EV,
    W0,
):
    layers, rows, cols = x_ref.shape
    _, cell_rows, cells = w_ref.shape
    spread_rows = gather_lanes(rows, cell_rows)
    spread = spread_lanes(cells, cols)
    for l in range(layers):
        warm = jnp.exp(-0.5 * warmth_sensitivity * w_ref[l])
        g_ref[l] = jnp.sqrt(b_ref[l]) * dot(spread_rows, dot(warm, spread))
        j_ref[l] = f_ref[l].astype(jnp.float32) * a_ref[l]
    first_sweep(2, x_ref, g_ref, j_ref, v_ref, W0, XN, WN, D, DI, GD, JD, EH, EV)


def bulk_mid_kernel(X, V, W, D, DI, GD, JD, G, XN, WN, DN):
    keep, gain = sweep_gains()[0]
    next_sweep(2, keep, gain, X, V, W, D, DI, GD, JD, G, XN, WN, DN)


def bulk_last_kernel(
    X, V, W, D, DI, GD, JD, EH, EV, xr_ref, xc_ref,
    x_hbm, h_ref,
    XN, PA, PB, PD, out, sem,
):
    layers, rows, cols = X.shape
    cell_rows, cells = h_ref.shape[1:]
    groups = rows // SUB
    keep, gain = sweep_gains()[-1]
    next_sweep(2, keep, gain, X, V, W, D, DI, GD, JD, None, XN)
    lane = iota((rows, LANE), 1)
    for l in range(layers):
        for t in range(cols // LANE):
            tile = slice(t * LANE, (t + 1) * LANE)
            x = jnp.concatenate(
                [xr_ref[l, 0:SUB, tile], XN[l, SUB : rows - SUB, tile], xr_ref[l, SUB : 2 * SUB, tile]], 0
            )
            if t == 0:
                x = jnp.where(lane < SUB, xc_ref[l], x)
            if t == cols // LANE - 1:
                x = jnp.where(lane >= LANE - SUB, xc_ref[l], x)
            out[l, :, tile] = x
    copy = pltpu.make_async_copy(out, x_hbm, sem)
    copy.start()
    PD[:, :, 0:SUB, :] = jnp.zeros((layers, cols // LANE, SUB, LANE), jnp.float32)
    power_rows(0, groups, 2, XN, V, EH, EV, PA, PB, PD)
    heat = fold_power(0, cell_rows, PA, PB, PD, *fold_matrices(cols, cells))
    for l in range(layers):
        h_ref[l] = heat[l]
    copy.wait()


def row_strip_kernel(
    x_t, x_b, g_t, g_b, j_t, j_b, v_t, v_b,
    x_l, x_r, g_l, g_r, j_l, j_r, v_l, v_r,
    re_ref, ro_ref,
    xr_ref, h_ref, strip_ref,
    X, G, J, V, W0, XN, WN, D, DI, GD, JD, EH, EV, PA, PB, PD, DN, XL,
):
    layers, deep, cols = x_t.shape
    rows = x_l.shape[1]
    cells = h_ref.shape[2]
    half = 2 * layers
    height = 2 * (SUB + deep)
    plane = 0
    lane = iota((rows + 2 * SUB, LANE), 1)
    for top_ref, bot_ref, left_ref, right_ref, pad in (
        (x_t, x_b, x_l, x_r, X), (g_t, g_b, g_l, g_r, G), (j_t, j_b, j_l, j_r, J), (v_t, v_b, v_l, v_r, V),
    ):
        for l in range(top_ref.shape[0]):
            top, bot = row_margin(re_ref, ro_ref, plane, slice(0, cols), half)
            pad[l, 0:SUB, :] = top
            pad[l, SUB : SUB + deep, :] = top_ref[l].astype(jnp.float32)
            pad[l, SUB + deep : SUB + 2 * deep, :] = bot_ref[l].astype(jnp.float32)
            pad[l, SUB + 2 * deep : height, :] = bot
            left = jnp.concatenate([top[:, :LANE], left_ref[l].astype(jnp.float32), bot[:, :LANE]], 0)
            right = jnp.concatenate(
                [top[:, cols - LANE :], right_ref[l].astype(jnp.float32), bot[:, cols - LANE :]], 0
            )
            strip_ref[plane] = jnp.where(lane < LANE // 4, left, pltpu.roll(right, LANE // 2, 1))
            plane += 1
    first_sweep(6, X, G, J, V, W0, XN, WN, D, DI, GD, JD, EH, EV)
    later_sweeps(6, XN, V, WN, D, DI, GD, JD, G, W0, XL, DN)
    groups = height // SUB
    power_rows(0, groups - 1, 6, XL, V, EH, EV, PA, PB, PD)
    heat = fold_power(SUB, 2 * SUB // 2, PA, PB, PD, *fold_matrices(cols, cells))
    for l in range(layers):
        h_ref[l] = heat[l]
        xr_ref[l, 0:SUB, :] = XL[l, SUB : 2 * SUB, :]
        xr_ref[l, SUB : 2 * SUB, :] = XL[l, height - 2 * SUB : height - SUB, :]


def col_strip_kernel(
    strip_ref, ce_ref, co_ref, hr_ref,
    xc_ref, hc_ref, hm_ref,
    X, G, J, V, W0, XN, WN, D, DI, GD, JD, EH, EV, PA, PB, PD, DN, XL,
):
    layers, rows, _ = xc_ref.shape
    cell_rows, cells = hc_ref.shape[1:]
    height = rows + 2 * SUB
    mixed = col_margin(ce_ref[...], co_ref[...], False, LANE // 2 + REACH)
    lane = iota((height, LANE), 1)
    from_right = (lane >= LANE // 2) & (lane < LANE // 2 + REACH)
    margin = from_right | (lane >= LANE - REACH)
    plane = 0
    for pad in (X, G, J, V):
        for l in range(pad.shape[0]):
            shift = (LANE // 2 - 8 * plane) % LANE
            value = pltpu.roll(mixed, shift, 1) if shift else mixed
            pad[l] = jnp.where(margin, value, strip_ref[plane])
            plane += 1
    groups = height // SUB
    first_sweep(9, X, G, J, V, W0, XN, WN, D, DI, GD, JD, EH, EV)
    later_sweeps(9, XN, V, WN, D, DI, GD, JD, G, W0, XL, DN)
    power_rows(0, groups - 1, 17, XL, V, EH, EV, PA, PB, PD)
    n, c = iota((LANE, cells), 0), iota((LANE, cells), 1)
    near = lax.shift_right_logical(n, 2) == jnp.where(c < cells // 2, c, c - cells + LANE // 8)
    before_it = n == (REFINE * jnp.where(c < cells // 2, c, c - cells + LANE // 8) - 1) % LANE
    at_edge = (c < REACH) | (c >= cells - REACH)
    heat = fold_power(
        SUB, cell_rows, PA, PB, PD,
        (near & at_edge).astype(jnp.float32), (before_it & at_edge).astype(jnp.float32),
    )
    lane = iota((rows, LANE), 1)
    cell = iota((SUB, cells), 1)
    edge = (cell < REACH - 1) | (cell > cells - REACH)
    for l in range(layers):
        hc_ref[l] = heat[l]
        x = XL[l, SUB : SUB + rows, :]
        xc_ref[l] = jnp.where(lane < LANE // 2, x, pltpu.roll(x, LANE // 2, 1))
        own = jnp.concatenate([heat[l][:REACH], heat[l][cell_rows - REACH :]], 0)
        hm_ref[l] = jnp.where(edge, own, hr_ref[l])


def heat_rows(own, e_ref, o_ref, l):
    even, above, below = place("row")
    e, o = e_ref[l], o_ref[l]
    pick = uniform(even, e.shape)
    top = jnp.where(uniform(above, e.shape), jnp.where(pick, o, e), 0.0)
    bot = jnp.where(uniform(below, e.shape), jnp.where(pick, e, o), 0.0)
    return jnp.concatenate([top, own, bot], axis=0)


def pack_heat_kernel(h_ref, re_ref, ro_ref, _, e_ref, o_ref):
    layers, cell_rows, cells = h_ref.shape
    height = cell_rows + 2 * SUB
    even, _, _ = place("col")
    lane = iota((height, LANE), 1)
    slot, low = lax.shift_right_logical(lane, 3), lane % 8 < REACH
    left = right = jnp.zeros((height, LANE), jnp.float32)
    for l in range(layers):
        value = heat_rows(h_ref[l], re_ref, ro_ref, l)
        mine = (slot == l) & low
        left = jnp.where(mine, pltpu.roll(value[:, :LANE], 8 * l, 1) if l else value[:, :LANE], left)
        right = jnp.where(mine, pltpu.roll(value[:, cells - LANE :], 8 * l + REACH, 1), right)
    pick = uniform(even, (height, LANE))
    e_ref[...] = jnp.where(pick, right, left)
    o_ref[...] = jnp.where(pick, left, right)


def warm_kernel(
    w_ref, h_ref, hm_ref, hc_ref, re_ref, ro_ref, ce_ref, co_ref,
    hre_ref, hro_ref, hce_ref, hco_ref, out_ref,
):
    layers, cell_rows, cells = w_ref.shape
    half = 2 * layers
    height, width = cell_rows + 2 * SUB, cells + LANE
    warm_mixed = col_margin(ce_ref[0:height, :], co_ref[0:height, :], True, REACH)
    heat_mixed = col_margin(hce_ref[...], hco_ref[...], False, REACH)
    cell = iota((cell_rows, cells), 1)
    edge = (cell < REACH - 1) | (cell > cells - REACH)
    cell_row = iota((SUB, cells), 0)
    theta, heat = [], []
    for l in range(layers):
        top, bot = row_margin(
            re_ref, ro_ref, 2 * half - 1, slice(l * cells, (l + 1) * cells), half
        )
        own = jnp.concatenate([top, w_ref[l], bot], axis=0)
        theta.append(jnp.concatenate([own, margin_tile(warm_mixed, 8 * l + REACH)], axis=1))
        own = jnp.where(edge, hc_ref[l], h_ref[l])
        first, final = own[:SUB], own[cell_rows - SUB :]
        first = jnp.where(cell_row < REACH - 1, hm_ref[l], first)
        final = jnp.where(cell_row > SUB - REACH, hm_ref[l], final)
        own = jnp.concatenate([first, own[SUB : cell_rows - SUB], final], axis=0)
        own = heat_rows(own, hre_ref, hro_ref, l)
        heat.append(jnp.concatenate([own, margin_tile(heat_mixed, 8 * l)], axis=1))
    _, above, below = place("row")
    _, before, after = place("col")
    shape = (height, width)
    r, c = iota(shape, 0), iota(shape, 1)
    inside = (uniform(above, shape) | (r >= SUB)) & (uniform(below, shape) | (r < height - SUB))
    inside = inside & (uniform(after, shape) | (c < cells) | (c >= cells + LANE // 2))
    inside = inside & (uniform(before, shape) | (c < cells + LANE // 2))

    def around_cells(v):
        return (pltpu.roll(v, 1, 0) + pltpu.roll(v, height - 1, 0)) + (
            pltpu.roll(v, 1, 1) + pltpu.roll(v, width - 1, 1)
        )

    for _ in range(HEAT_SWEEPS):
        later = []
        for l in range(layers):
            t = theta[l]
            q = jnp.where(inside, jnp.exp(-0.5 * warming_weight * t), 0.0)
            change = q * (around_cells(q * t) - t * around_cells(q)) + heat[l]
            if l < layers - 1:
                change = change + (theta[l + 1] - t)
            if l > 0:
                change = change + (theta[l - 1] - t)
            if l == layers - 1:
                change = change - t
            later.append(t + interval_length * change)
        theta = later
    for l in range(layers):
        out_ref[l] = theta[l][SUB : SUB + cell_rows, :cells]


def on_device(x, base, warm, via, feeder, amps):
    layers, rows, cols = x.shape
    _, cell_rows, cells = warm.shape
    f32 = jnp.float32
    mesh_rows, mesh_cols = lax.axis_size("row"), lax.axis_size("col")
    last_row, last_cell_row, last_col = rows // SUB - 1, cell_rows // SUB - 1, cols // LANE - 1

    def shape(*dims):
        return jax.ShapeDtypeStruct(dims, f32)

    def edge_rows(a, at):
        return pl.BlockSpec((a.shape[0], SUB, a.shape[2]), lambda _, at=at: (0, at, 0))

    def edge_cols(a, at):
        return pl.BlockSpec((a.shape[0], a.shape[1], LANE), lambda _, at=at: (0, 0, at))

    def full(a):
        return pl.BlockSpec(a.shape, lambda _, n=len(a.shape): (0,) * n)

    def swap(e, o, tables):
        return tuple(
            lax.ppermute(m, BOTH, tables(mesh_rows, mesh_cols, first)) for first, m in enumerate((e, o))
        )

    params = pltpu.CompilerParams(vmem_limit_bytes=24 * 1024 * 1024)
    row_args, row_specs = [], []
    for a in (x, base, warm, via, feeder, amps):
        end = last_cell_row if a is warm else last_row
        row_args += [a, a]
        row_specs += [edge_rows(a, 0), edge_rows(a, end)]
    message = shape(2 * layers, SUB, cols)
    e, o = pl.pallas_call(
        pack_rows_kernel,
        grid=(1,),
        in_specs=row_specs,
        out_specs=(full(message), full(message)),
        out_shape=(message, message),
        compiler_params=pltpu.CompilerParams(vmem_limit_bytes=58 * 1024 * 1024),
        name="pack_rows",
    )(*row_args)
    row_e, row_o = swap(e, o, row_swaps)

    fields = (shape(layers, rows, cols),) * 10
    node_scratch = pltpu.VMEM((layers, rows, cols), f32)
    g, inject, *mid = pl.pallas_call(
        bulk_first_kernel,
        out_shape=fields,
        scratch_shapes=[node_scratch],
        compiler_params=params,
        name="bulk_first",
        cost_estimate=pl.CostEstimate(flops=40 * x.size, bytes_accessed=60 * x.size, transcendentals=0),
    )(x, base, warm, via, feeder, amps)
    x_mid, w_mid, d_mid, inv_diag, g_diag, j_diag, edge_h, edge_v = mid

    col_args, col_specs = [], []
    for a in (x, g, inject, via):
        col_args += [a, a]
        col_specs += [edge_cols(a, 0), edge_cols(a, last_col)]
    message = shape(rows + 2 * SUB, LANE)
    e, o = pl.pallas_call(
        pack_cols_kernel,
        grid=(1,),
        in_specs=col_specs + [full(warm), full(row_e), full(row_o)],
        out_specs=(full(message), full(message)),
        out_shape=(message, message),
        compiler_params=params,
        name="pack_cols",
    )(*col_args, warm, row_e, row_o)
    col_e, col_o = swap(e, o, col_swaps)

    def strip_scratch(height, width):
        node = pltpu.VMEM((layers, height, width), f32)
        taller = pltpu.VMEM((layers, width // LANE, height + SUB, LANE), f32)
        return [node] * 3 + [pltpu.VMEM((layers - 1, height, width), f32)] + [node] * 9 + [taller] * 3 + [node] * 2

    def edge_deep(a, at):
        return pl.BlockSpec((a.shape[0], 2 * SUB, a.shape[2]), lambda _, at=at: (0, at, 0))

    deep_args, deep_specs = [], []
    for a in (x, g, inject, via):
        deep_args += [a, a]
        deep_specs += [edge_deep(a, 0), edge_deep(a, rows // (2 * SUB) - 1)]
    edge_x, edge_h2 = shape(layers, 2 * SUB, cols), shape(layers, SUB, cells)
    strip = shape(4 * layers - 1, rows + 2 * SUB, LANE)
    x_rows, heat_strip, strip = pl.pallas_call(
        row_strip_kernel,
        grid=(1,),
        in_specs=deep_specs + col_specs + [full(row_e), full(row_o)],
        out_specs=(full(edge_x), full(edge_h2), full(strip)),
        out_shape=(edge_x, edge_h2, strip),
        scratch_shapes=strip_scratch(6 * SUB, cols),
        compiler_params=params,
        name="row_strip",
        cost_estimate=pl.CostEstimate(flops=40 * x.size, bytes_accessed=20 * x.size, transcendentals=0),
    )(*deep_args, *col_args, row_e, row_o)

    x_cols, heat_cols, heat_edge = pl.pallas_call(
        col_strip_kernel,
        out_shape=(shape(layers, rows, LANE), shape(layers, cell_rows, cells), edge_h2),
        scratch_shapes=strip_scratch(rows + 2 * SUB, LANE),
        compiler_params=params,
        name="col_strip",
    )(strip, col_e, col_o, heat_strip)
    heat_row_e, heat_row_o = swap(heat_edge, heat_edge, row_swaps)

    assert SWEEPS == 3
    x_next, w_next, d_next = pl.pallas_call(
        bulk_mid_kernel,
        out_shape=(shape(layers, rows, cols),) * 3,
        compiler_params=params,
        name="bulk_mid",
        cost_estimate=pl.CostEstimate(flops=20 * x.size, bytes_accessed=20 * x.size, transcendentals=0),
    )(x_mid, via, w_mid, d_mid, inv_diag, g_diag, j_diag, g)

    message = shape(cell_rows + 2 * SUB, LANE)
    e, o = pl.pallas_call(
        pack_heat_kernel,
        in_specs=[pl.BlockSpec(memory_space=pltpu.VMEM)] * 3 + [pl.BlockSpec(memory_space=pl.ANY)],
        out_shape=(message, message),
        compiler_params=params,
        name="pack_heat",
    )(heat_cols, heat_row_e, heat_row_o, x_next)
    heat_col_e, heat_col_o = swap(e, o, col_swaps)

    tall = pltpu.VMEM((layers, cols // LANE, rows + SUB, LANE), f32)
    voltage, heat = pl.pallas_call(
        bulk_last_kernel,
        out_shape=(shape(layers, rows, cols), shape(layers, cell_rows, cells)),
        out_specs=(pl.BlockSpec(memory_space=pl.ANY), pl.BlockSpec(memory_space=pltpu.VMEM)),
        scratch_shapes=[node_scratch] + [tall] * 3 + [node_scratch, pltpu.SemaphoreType.DMA],
        compiler_params=params,
        name="bulk_last",
        cost_estimate=pl.CostEstimate(flops=40 * x.size, bytes_accessed=60 * x.size, transcendentals=0),
    )(x_next, via, w_next, d_next, inv_diag, g_diag, j_diag, edge_h, edge_v, x_rows, x_cols)

    warmth = pl.pallas_call(
        warm_kernel,
        out_shape=shape(layers, cell_rows, cells),
        compiler_params=params,
        name="warm",
    )(warm, heat, heat_edge, heat_cols, row_e, row_o, col_e, col_o, heat_row_e, heat_row_o, heat_col_e, heat_col_o)
    return voltage, warmth


def solution(mesh):
    placed = P(None, "row", "col")
    return jax.shard_map(
        on_device,
        mesh=mesh,
        in_specs=(placed,) * 6,
        out_specs=(placed, placed),
        check_vma=False,
    )
```

```python
import jax
import jax.numpy as jnp
from jax import lax
from jax.experimental import pallas as pl
from jax.experimental.pallas import tpu as pltpu
from jax.sharding import PartitionSpec as P

REFINE = 4
SWEEPS = 3
HEAT_SWEEPS = 4

warmth_sensitivity = 0.5
leak_cond = 0.2
spectrum_low = 0.05
spectrum_high = 1.95
warming_weight = 0.3
heat_gain = 0.0625
interval_length = 0.12

SUB = 8
LANE = 128
REACH = 4
BOTH = ("row", "col")
HIGHEST = lax.Precision.HIGHEST


def row_swaps(rows, cols, first):
    pairs = []
    for r in range(rows):
        for c in range(cols):
            p = r + 1 if (r - first) % 2 == 0 else r - 1
            if 0 <= p < rows:
                pairs.append((r * cols + c, p * cols + c))
            elif c ^ 1 < cols:
                pairs.append((r * cols + c, r * cols + (c ^ 1)))
    return pairs


def col_swaps(rows, cols, first):
    pairs = []
    for r in range(rows):
        for c in range(cols):
            p = c + 1 if (c - first) % 2 == 0 else c - 1
            if 0 <= p < cols:
                pairs.append((r * cols + c, r * cols + p))
            elif r ^ 1 < rows:
                pairs.append((r * cols + c, (r ^ 1) * cols + c))
    return pairs


def iota(shape, dim):
    return lax.broadcasted_iota(jnp.int32, shape, dim)


def uniform(flag, shape):
    return jnp.full(shape, flag.astype(jnp.int32), jnp.int32) == 1


def place(axis):
    at = lax.axis_index(axis)
    return at % 2 == 0, at > 0, at < lax.axis_size(axis) - 1


def dot(a, b):
    return jnp.dot(a, b, precision=HIGHEST, preferred_element_type=jnp.float32)


def spread_lanes(cells, nodes):
    same = lax.shift_right_logical(iota((cells, nodes), 1), 2) == iota((cells, nodes), 0)
    return same.astype(jnp.float32)


def gather_lanes(nodes, cells):
    same = lax.shift_right_logical(iota((nodes, cells), 0), 2) == iota((nodes, cells), 1)
    return same.astype(jnp.float32)


def pack_rows_kernel(x_t, x_b, b_t, b_b, w_t, w_b, v_t, v_b, f_t, f_b, a_t, a_b, e_ref, o_ref):
    layers, _, cols = x_t.shape
    cells = w_t.shape[2]
    even, _, _ = place("row")
    low = iota((SUB, cols), 0) < REACH
    spread = spread_lanes(cells, cols)

    def planes(x, b, w, v, f, a, cell_row):
        warm = jnp.concatenate([w[l, cell_row : cell_row + 1, :] for l in range(layers)] * 2, 0)
        warm = dot(jnp.exp(-0.5 * warmth_sensitivity * warm), spread)
        xs = [x[l] for l in range(layers)]
        gs = [jnp.sqrt(b[l]) * warm[l : l + 1] for l in range(layers)]
        js = [f[l].astype(jnp.float32) * a[l] for l in range(layers)]
        vs = [v[l].astype(jnp.float32) for l in range(layers - 1)]
        ws = [jnp.concatenate([w[l] for l in range(layers)], axis=1)]
        return xs + gs, js + vs + ws

    top_a, top_b = planes(x_t, b_t, w_t, v_t, f_t, a_t, 0)
    bot_a, bot_b = planes(x_b, b_b, w_b, v_b, f_b, a_b, SUB - 1)
    pick = uniform(even, (SUB, cols))
    for k in range(2 * layers):
        top = jnp.where(low, top_a[k], pltpu.roll(top_b[k], REACH, 0))
        bot = jnp.where(low, pltpu.roll(bot_a[k], REACH, 0), bot_b[k])
        e_ref[k] = jnp.where(pick, bot, top)
        o_ref[k] = jnp.where(pick, top, bot)


def row_margin(e_ref, o_ref, plane, cols, half):
    even, above, below = place("row")
    k = plane % half
    e, o = e_ref[k, :, cols], o_ref[k, :, cols]
    pick = uniform(even, e.shape)
    top, bot = jnp.where(pick, o, e), jnp.where(pick, e, o)
    if plane < half:
        top = pltpu.roll(top, REACH, 0)
    else:
        bot = pltpu.roll(bot, REACH, 0)
    return (
        jnp.where(uniform(above, top.shape), top, 0.0),
        jnp.where(uniform(below, bot.shape), bot, 0.0),
    )


def packed(values, side, high, out):
    lane = iota(out.shape, 1)
    slot, upper = lax.shift_right_logical(lane, 3), lane % 8 >= REACH
    for p, value in enumerate(values):
        shift = (8 * p + REACH * (side + high)) % LANE
        value = pltpu.roll(value.astype(jnp.float32), shift, 1) if shift else value
        out = jnp.where((slot == p) & (upper if high else ~upper), value, out)
    return out


def end_tiles(width):
    return slice(0, LANE), slice(width - LANE, width)


def pack_own_columns(fields, w_ref, e_ref, o_ref):
    rows, cols = fields[0].shape[1:]
    layers, cell_rows, cells = w_ref.shape
    sides = []
    for side in range(2):
        tile, cell_tile = end_tiles(cols)[side], end_tiles(cells)[side]
        values = [ref[l, :, tile] for ref in fields for l in range(ref.shape[0])]
        out = packed(values, side, False, jnp.zeros((rows, LANE), jnp.float32))
        head = packed([w_ref[l, :, cell_tile] for l in range(layers)], side, True, out[:cell_rows])
        sides.append(jnp.concatenate([head, out[cell_rows:]], axis=0))
    even, _, _ = place("col")
    pick = uniform(even, (rows, LANE))
    e_ref[...] = jnp.where(pick, sides[1], sides[0])
    o_ref[...] = jnp.where(pick, sides[0], sides[1])


def pack_cols_kernel(re_ref, ro_ref, own_e, own_o, w_ref, e_ref, o_ref):
    rows, cols = own_e.shape[0], re_ref.shape[2]
    layers, cell_rows, cells = w_ref.shape
    half = 2 * layers
    even, _, _ = place("col")
    pick = uniform(even, (SUB, LANE))
    zero = jnp.zeros((SUB, LANE), jnp.float32)
    tops, bots, lows = [], [], []
    for side in range(2):
        tile, cell_tile = end_tiles(cols)[side], end_tiles(cells)[side]
        margins = [row_margin(re_ref, ro_ref, p, tile, half) for p in range(2 * half - 1)]
        warm = [
            row_margin(
                re_ref, ro_ref, 2 * half - 1,
                slice(l * cells + cell_tile.start, l * cells + cell_tile.stop), half,
            )
            for l in range(layers)
        ]
        tops.append(packed([m[0] for m in warm], side, True, packed([m[0] for m in margins], side, False, zero)))
        bots.append(packed([m[1] for m in margins], side, False, zero))
        lows.append(packed([m[1] for m in warm], side, True, zero))
    high = iota((SUB, LANE), 1) % 8 >= REACH
    at = SUB + cell_rows
    for ref, own, first in ((e_ref, own_e, 1), (o_ref, own_o, 0)):
        ref[SUB : SUB + rows, :] = own[...]
        ref[0:SUB, :] = jnp.where(pick, tops[first], tops[1 - first])
        ref[SUB + rows : 2 * SUB + rows, :] = jnp.where(pick, bots[first], bots[1 - first])
        low = jnp.where(pick, lows[first], lows[1 - first])
        ref[at : at + SUB, :] = jnp.where(high, low, own[cell_rows : cell_rows + SUB, :])


def col_margin(e, o, high, back):
    even, before, after = place("col")
    lane = iota(e.shape, 1)
    pick = uniform(even, e.shape)
    right, left = jnp.where(pick, e, o), jnp.where(pick, o, e)
    right = jnp.where(uniform(after, e.shape), right, 0.0)
    left = jnp.where(uniform(before, e.shape), left, 0.0)
    own_half = lane % 8 >= REACH if high else lane % 8 < REACH
    return jnp.where(own_half, right, pltpu.roll(left, LANE - back, 1))


def margin_tile(mixed, shift):
    lane = iota(mixed.shape, 1)
    value = mixed if shift == 0 else pltpu.roll(mixed, LANE - shift, 1)
    return jnp.where((lane < REACH) | (lane >= LANE - REACH), value, 0.0)


CENTER = 0.5 * (spectrum_high + spectrum_low)
HALF = 0.5 * (spectrum_high - spectrum_low)
SIGMA = CENTER / HALF


def sweep_gains():
    rho, gains = 1.0 / SIGMA, []
    for _ in range(SWEEPS - 1):
        rho_new = 1.0 / (2.0 * SIGMA - rho)
        gains.append((rho_new * rho, 2.0 * rho_new / HALF))
        rho = rho_new
    return gains


def tile_rows(i):
    return pl.ds(pl.multiple_of(i * SUB, SUB), SUB)


def each(first, last, unroll, body):
    if unroll >= last - first:
        for i in range(first, last):
            body(i)
    else:
        lax.fori_loop(first, last, lambda i, c: (body(i), c)[1], 0, unroll=unroll)


def before(i):
    return max(i - 1, 0) if isinstance(i, int) else jnp.maximum(i - 1, 0)


def after(i, groups):
    return min(i + 1, groups - 1) if isinstance(i, int) else jnp.minimum(i + 1, groups - 1)


def shifted_down(here, nxt):
    return jnp.where(
        iota(here.shape, 0) == SUB - 1, pltpu.roll(nxt, SUB - 1, 0), pltpu.roll(here, SUB - 1, 0)
    )


def shifted_up(prev, here):
    return jnp.where(iota(here.shape, 0) == 0, pltpu.roll(prev, 1, 0), pltpu.roll(here, 1, 0))


def around(ref, l, i, groups):
    here = ref[l, tile_rows(i), :]
    width = here.shape[1]
    up = shifted_up(ref[l, tile_rows(before(i)), :], here)
    down = shifted_down(here, ref[l, tile_rows(after(i, groups)), :])
    return up, down, pltpu.roll(here, 1, 1), pltpu.roll(here, width - 1, 1)


def added(four):
    return (four[0] + four[1]) + (four[2] + four[3])


def upright(l, xs, vs):
    layers = len(xs)
    if l == 0:
        return vs[0] * xs[1]
    if l == layers - 1:
        return vs[l - 1] * xs[l - 1]
    return vs[l] * xs[l + 1] + vs[l - 1] * xs[l - 1]


def load_vias(V, r):
    return [V[l, r, :].astype(jnp.float32) for l in range(V.shape[0])]


def first_sweep(unroll, skip, X, G, J, V, W0, XN, WN, D, DI, GD, JD, EH, EV):
    layers, height, _ = X.shape
    groups = height // SUB

    def start(i):
        r = tile_rows(i)
        for l in range(layers):
            W0[l, r, :] = G[l, r, :] * X[l, r, :]

    each(0, groups, unroll, start)

    def body(i):
        r = tile_rows(i)
        xs = [X[l, r, :] for l in range(layers)]
        vs = load_vias(V, r)
        for l in range(layers):
            g = G[l, r, :]
            four = around(G, l, i, groups)
            diag = leak_cond + g * added(four)
            EV[l, r, :] = g * four[1]
            EH[l, r, :] = g * four[3]
            if l < layers - 1:
                diag = diag + vs[l]
            if l > 0:
                diag = diag + vs[l - 1]
            inverse = 1.0 / diag
            gd, jd = g * inverse, J[l, r, :] * inverse
            near = added(around(W0, l, i, groups))
            d = (jd + gd * near + inverse * upright(l, xs, vs) - xs[l]) / CENTER
            x = xs[l] + d
            DI[l, r, :], GD[l, r, :], JD[l, r, :], D[l, r, :] = inverse, gd, jd, d
            XN[l, r, :] = x
            WN[l, r, :] = g * x

    each(skip, groups - skip, unroll, body)


def next_sweep(unroll, skip, keep, gain, X, V, W, D, DI, GD, JD, G, XN, WN=None, DN=None):
    layers, height, _ = X.shape
    groups = height // SUB

    def body(i):
        r = tile_rows(i)
        xs = [X[l, r, :] for l in range(layers)]
        vs = load_vias(V, r)
        for l in range(layers):
            near = added(around(W, l, i, groups))
            resid = (
                JD[l, r, :] + GD[l, r, :] * near + DI[l, r, :] * upright(l, xs, vs) - xs[l]
            )
            d = keep * D[l, r, :] + gain * resid
            x = xs[l] + d
            XN[l, r, :] = x
            if WN is not None:
                DN[l, r, :] = d
                WN[l, r, :] = G[l, r, :] * x

    each(skip, groups - skip, unroll, body)


def later_sweeps(unroll, X, V, W, D, DI, GD, JD, G, WN, XN, DN):
    gains = sweep_gains()
    x, w, d, other = X, W, D, WN
    for at, (keep, gain) in enumerate(gains):
        if at == len(gains) - 1:
            next_sweep(unroll, 0, keep, gain, x, V, w, d, DI, GD, JD, G, XN)
        else:
            next_sweep(unroll, 0, keep, gain, x, V, w, d, DI, GD, JD, G, XN, other, DN)
            assert len(gains) <= 2
            x, w, d = XN, other, DN


def power_rows(first, last, unroll, X, V, EH, EV, PA, PB, PD):
    layers, height, width = X.shape
    groups = height // SUB
    share = jnp.where(iota((SUB, width), 0) % REFINE == REFINE - 1, 0.5, 1.0)
    lane_share = jnp.where(iota((SUB, width), 1) % REFINE == REFINE - 1, 1.0, 2.0)

    def fold(v):
        v = v + pltpu.roll(v, SUB - 1, 0)
        return v + pltpu.roll(v, SUB - 2, 0)

    def body(i):
        r = tile_rows(i)
        out = tile_rows(i + 1)
        xs = [X[l, r, :] for l in range(layers)]
        vs = load_vias(V, r)
        drops = [0.5 * vs[l] * (xs[l] - xs[l + 1]) ** 2 for l in range(layers - 1)]
        for l in range(layers):
            x = xs[l]
            across = x - pltpu.roll(x, width - 1, 1)
            down = x - shifted_down(x, X[l, tile_rows(after(i, groups)), :])
            across = 0.5 * EH[l, r, :] * (across * across)
            down = EV[l, r, :] * (down * down)
            total = leak_cond * (x * x) + share * down + lane_share * across
            if l < layers - 1:
                total = total + drops[l]
            if l > 0:
                total = total + drops[l - 1]
            total, across = fold(total), fold(across)
            for t in range(width // LANE):
                tile = slice(t * LANE, (t + 1) * LANE)
                PA[l, t, out, :] = total[:, tile]
                PB[l, t, out, :] = across[:, tile]
                PD[l, t, out, :] = down[:, tile]

    each(first, last, unroll, body)


def fold_power(row, cells, PA, PB, PD, same, left):
    layers = PA.shape[0]
    at = pl.ds(row + SUB, cells, stride=REFINE)
    up = pl.ds(row + SUB - 1, cells, stride=REFINE)
    tiles = range(PA.shape[1])
    a = [
        jnp.concatenate([PA[l, t, at, :] + 0.5 * PD[l, t, up, :] for t in tiles], 1)
        for l in range(layers)
    ]
    b = [jnp.concatenate([PB[l, t, at, :] for t in tiles], 1) for l in range(layers)]
    a, b = jnp.concatenate(a, 0), jnp.concatenate(b, 0)
    heat = (dot(a, same) + dot(b, left)) * heat_gain
    return [heat[l * cells : (l + 1) * cells] for l in range(layers)]


def fold_matrices(nodes, cells):
    n, c = iota((nodes, cells), 0), iota((nodes, cells), 1)
    same = lax.shift_right_logical(n, 2) == c
    return same.astype(jnp.float32), (n == REFINE * c - 1).astype(jnp.float32)


def bulk_first_kernel(
    x_ref, b_ref, w_ref, v_ref, f_ref, a_ref,
    g_ref, j_ref, XN, WN, D, DI, GD, JD, EH, EV, own_e, own_o,
    W0,
):
    layers, rows, cols = x_ref.shape
    _, cell_rows, cells = w_ref.shape
    spread_rows = gather_lanes(rows, cell_rows)
    spread = spread_lanes(cells, cols)
    for l in range(layers):
        warm = jnp.exp(-0.5 * warmth_sensitivity * w_ref[l])
        g_ref[l] = jnp.sqrt(b_ref[l]) * dot(spread_rows, dot(warm, spread))
        j_ref[l] = f_ref[l].astype(jnp.float32) * a_ref[l]
    pack_own_columns((x_ref, g_ref, j_ref, v_ref), w_ref, own_e, own_o)
    first_sweep(2, 1, x_ref, g_ref, j_ref, v_ref, W0, XN, WN, D, DI, GD, JD, EH, EV)


def bulk_mid_kernel(X, V, W, D, DI, GD, JD, G, XL, WN, XN, DN):
    (keep, gain), (keep_last, gain_last) = sweep_gains()
    next_sweep(2, 1, keep, gain, X, V, W, D, DI, GD, JD, G, XN, WN, DN)
    next_sweep(2, 1, keep_last, gain_last, XN, V, WN, DN, DI, GD, JD, G, XL)


def bulk_last_kernel(
    XN, V, EH, EV, xr_ref, xc_ref,
    x_hbm, h_ref,
    PA, PB, PD, out, sem,
):
    layers, rows, cols = XN.shape
    cell_rows, cells = h_ref.shape[1:]
    groups = rows // SUB
    lane = iota((rows, LANE), 1)
    low = iota((SUB, LANE), 0) < REACH
    for l in range(layers):
        for t in range(cols // LANE):
            tile = slice(t * LANE, (t + 1) * LANE)
            x = jnp.concatenate(
                [
                    xr_ref[l, 0:SUB, tile],
                    jnp.where(low, xr_ref[l, SUB : 2 * SUB, tile], XN[l, SUB : 2 * SUB, tile]),
                    XN[l, 2 * SUB : rows - 2 * SUB, tile],
                    jnp.where(
                        low,
                        XN[l, rows - 2 * SUB : rows - SUB, tile],
                        xr_ref[l, 2 * SUB : 3 * SUB, tile],
                    ),
                    xr_ref[l, 3 * SUB : 4 * SUB, tile],
                ],
                0,
            )
            if t == 0:
                x = jnp.where(lane < SUB, xc_ref[l], x)
            if t == cols // LANE - 1:
                x = jnp.where(lane >= LANE - SUB, xc_ref[l], x)
            out[l, :, tile] = x
    copy = pltpu.make_async_copy(out, x_hbm, sem)
    copy.start()
    power_rows(1, groups - 1, 2, XN, V, EH, EV, PA, PB, PD)
    heat = fold_power(0, cell_rows, PA, PB, PD, *fold_matrices(cols, cells))
    for l in range(layers):
        h_ref[l] = heat[l]
    copy.wait()


def row_strip_kernel(
    x_t, x_b, g_t, g_b, j_t, j_b, v_t, v_b,
    x_l, x_r, g_l, g_r, j_l, j_r, v_l, v_r,
    re_ref, ro_ref,
    xr_ref, h_ref, strip_ref,
    X, G, J, V, W0, XN, WN, D, DI, GD, JD, EH, EV, PA, PB, PD, DN, XL,
):
    layers, deep, cols = x_t.shape
    rows = x_l.shape[1]
    cells = h_ref.shape[2]
    half = 2 * layers
    height = 2 * (SUB + deep)
    plane = 0
    lane = iota((rows + 2 * SUB, LANE), 1)
    for top_ref, bot_ref, left_ref, right_ref, pad in (
        (x_t, x_b, x_l, x_r, X), (g_t, g_b, g_l, g_r, G), (j_t, j_b, j_l, j_r, J), (v_t, v_b, v_l, v_r, V),
    ):
        for l in range(top_ref.shape[0]):
            top, bot = row_margin(re_ref, ro_ref, plane, slice(0, cols), half)
            pad[l, 0:SUB, :] = top
            pad[l, SUB : SUB + deep, :] = top_ref[l].astype(jnp.float32)
            pad[l, SUB + deep : SUB + 2 * deep, :] = bot_ref[l].astype(jnp.float32)
            pad[l, SUB + 2 * deep : height, :] = bot
            left = jnp.concatenate([top[:, :LANE], left_ref[l].astype(jnp.float32), bot[:, :LANE]], 0)
            right = jnp.concatenate(
                [top[:, cols - LANE :], right_ref[l].astype(jnp.float32), bot[:, cols - LANE :]], 0
            )
            strip_ref[plane] = jnp.where(lane < LANE // 4, left, pltpu.roll(right, LANE // 2, 1))
            plane += 1
    first_sweep(6, 0, X, G, J, V, W0, XN, WN, D, DI, GD, JD, EH, EV)
    later_sweeps(6, XN, V, WN, D, DI, GD, JD, G, W0, XL, DN)
    groups = height // SUB
    power_rows(0, groups - 1, 6, XL, V, EH, EV, PA, PB, PD)
    heat = fold_power(SUB, 2 * SUB // 2, PA, PB, PD, *fold_matrices(cols, cells))
    for l in range(layers):
        h_ref[l] = heat[l]
        xr_ref[l] = XL[l, SUB : height - SUB, :]


def col_strip_kernel(
    strip_ref, ce_ref, co_ref, hr_ref,
    xc_ref, hc_ref, hm_ref,
    X, G, J, V, W0, XN, WN, D, DI, GD, JD, EH, EV, PA, PB, PD, DN, XL,
):
    layers, rows, _ = xc_ref.shape
    cell_rows, cells = hc_ref.shape[1:]
    height = rows + 2 * SUB
    mixed = col_margin(ce_ref[...], co_ref[...], False, LANE // 2 + REACH)
    lane = iota((height, LANE), 1)
    from_right = (lane >= LANE // 2) & (lane < LANE // 2 + REACH)
    margin = from_right | (lane >= LANE - REACH)
    plane = 0
    for pad in (X, G, J, V):
        for l in range(pad.shape[0]):
            shift = (LANE // 2 - 8 * plane) % LANE
            value = pltpu.roll(mixed, shift, 1) if shift else mixed
            pad[l] = jnp.where(margin, value, strip_ref[plane])
            plane += 1
    groups = height // SUB
    first_sweep(9, 0, X, G, J, V, W0, XN, WN, D, DI, GD, JD, EH, EV)
    later_sweeps(9, XN, V, WN, D, DI, GD, JD, G, W0, XL, DN)
    power_rows(0, groups - 1, 17, XL, V, EH, EV, PA, PB, PD)
    n, c = iota((LANE, cells), 0), iota((LANE, cells), 1)
    near = lax.shift_right_logical(n, 2) == jnp.where(c < cells // 2, c, c - cells + LANE // 8)
    before_it = n == (REFINE * jnp.where(c < cells // 2, c, c - cells + LANE // 8) - 1) % LANE
    at_edge = (c < REACH) | (c >= cells - REACH)
    heat = fold_power(
        SUB, cell_rows, PA, PB, PD,
        (near & at_edge).astype(jnp.float32), (before_it & at_edge).astype(jnp.float32),
    )
    lane = iota((rows, LANE), 1)
    cell = iota((SUB, cells), 1)
    edge = (cell < REACH - 1) | (cell > cells - REACH)
    for l in range(layers):
        hc_ref[l] = heat[l]
        x = XL[l, SUB : SUB + rows, :]
        xc_ref[l] = jnp.where(lane < LANE // 2, x, pltpu.roll(x, LANE // 2, 1))
        own = jnp.concatenate([heat[l][:REACH], heat[l][cell_rows - REACH :]], 0)
        hm_ref[l] = jnp.where(edge, own, hr_ref[l])


def heat_rows(own, e_ref, o_ref, l):
    even, above, below = place("row")
    e, o = e_ref[l], o_ref[l]
    pick = uniform(even, e.shape)
    top = jnp.where(uniform(above, e.shape), jnp.where(pick, o, e), 0.0)
    bot = jnp.where(uniform(below, e.shape), jnp.where(pick, e, o), 0.0)
    return jnp.concatenate([top, own, bot], axis=0)


def pack_heat_kernel(h_ref, re_ref, ro_ref, _, e_ref, o_ref):
    layers, cell_rows, cells = h_ref.shape
    height = cell_rows + 2 * SUB
    even, _, _ = place("col")
    lane = iota((height, LANE), 1)
    slot, low = lax.shift_right_logical(lane, 3), lane % 8 < REACH
    left = right = jnp.zeros((height, LANE), jnp.float32)
    for l in range(layers):
        value = heat_rows(h_ref[l], re_ref, ro_ref, l)
        mine = (slot == l) & low
        left = jnp.where(mine, pltpu.roll(value[:, :LANE], 8 * l, 1) if l else value[:, :LANE], left)
        right = jnp.where(mine, pltpu.roll(value[:, cells - LANE :], 8 * l + REACH, 1), right)
    pick = uniform(even, (height, LANE))
    e_ref[...] = jnp.where(pick, right, left)
    o_ref[...] = jnp.where(pick, left, right)


def warm_kernel(
    w_ref, h_ref, hm_ref, hc_ref, re_ref, ro_ref, ce_ref, co_ref,
    hre_ref, hro_ref, hce_ref, hco_ref, out_ref,
):
    layers, cell_rows, cells = w_ref.shape
    half = 2 * layers
    height, width = cell_rows + 2 * SUB, cells + LANE
    warm_mixed = col_margin(ce_ref[0:height, :], co_ref[0:height, :], True, REACH)
    heat_mixed = col_margin(hce_ref[...], hco_ref[...], False, REACH)
    cell = iota((cell_rows, cells), 1)
    edge = (cell < REACH - 1) | (cell > cells - REACH)
    cell_row = iota((SUB, cells), 0)
    theta, heat = [], []
    for l in range(layers):
        top, bot = row_margin(
            re_ref, ro_ref, 2 * half - 1, slice(l * cells, (l + 1) * cells), half
        )
        own = jnp.concatenate([top, w_ref[l], bot], axis=0)
        theta.append(jnp.concatenate([own, margin_tile(warm_mixed, 8 * l + REACH)], axis=1))
        own = jnp.where(edge, hc_ref[l], h_ref[l])
        first, final = own[:SUB], own[cell_rows - SUB :]
        first = jnp.where(cell_row < REACH - 1, hm_ref[l], first)
        final = jnp.where(cell_row > SUB - REACH, hm_ref[l], final)
        own = jnp.concatenate([first, own[SUB : cell_rows - SUB], final], axis=0)
        own = heat_rows(own, hre_ref, hro_ref, l)
        heat.append(jnp.concatenate([own, margin_tile(heat_mixed, 8 * l)], axis=1))
    _, above, below = place("row")
    _, before, after = place("col")
    shape = (height, width)
    r, c = iota(shape, 0), iota(shape, 1)
    inside = (uniform(above, shape) | (r >= SUB)) & (uniform(below, shape) | (r < height - SUB))
    inside = inside & (uniform(after, shape) | (c < cells) | (c >= cells + LANE // 2))
    inside = inside & (uniform(before, shape) | (c < cells + LANE // 2))

    def around_cells(v):
        return (pltpu.roll(v, 1, 0) + pltpu.roll(v, height - 1, 0)) + (
            pltpu.roll(v, 1, 1) + pltpu.roll(v, width - 1, 1)
        )

    for _ in range(HEAT_SWEEPS):
        later = []
        for l in range(layers):
            t = theta[l]
            q = jnp.where(inside, jnp.exp(-0.5 * warming_weight * t), 0.0)
            change = q * (around_cells(q * t) - t * around_cells(q)) + heat[l]
            if l < layers - 1:
                change = change + (theta[l + 1] - t)
            if l > 0:
                change = change + (theta[l - 1] - t)
            if l == layers - 1:
                change = change - t
            later.append(t + interval_length * change)
        theta = later
    for l in range(layers):
        out_ref[l] = theta[l][SUB : SUB + cell_rows, :cells]


def on_device(x, base, warm, via, feeder, amps):
    layers, rows, cols = x.shape
    _, cell_rows, cells = warm.shape
    f32 = jnp.float32
    mesh_rows, mesh_cols = lax.axis_size("row"), lax.axis_size("col")
    last_row, last_cell_row, last_col = rows // SUB - 1, cell_rows // SUB - 1, cols // LANE - 1

    def shape(*dims):
        return jax.ShapeDtypeStruct(dims, f32)

    def edge_rows(a, at):
        return pl.BlockSpec((a.shape[0], SUB, a.shape[2]), lambda _, at=at: (0, at, 0))

    def edge_cols(a, at):
        return pl.BlockSpec((a.shape[0], a.shape[1], LANE), lambda _, at=at: (0, 0, at))

    def full(a):
        return pl.BlockSpec(a.shape, lambda _, n=len(a.shape): (0,) * n)

    def swap(e, o, tables):
        return tuple(
            lax.ppermute(m, BOTH, tables(mesh_rows, mesh_cols, first)) for first, m in enumerate((e, o))
        )

    params = pltpu.CompilerParams(vmem_limit_bytes=24 * 1024 * 1024)
    row_args, row_specs = [], []
    for a in (x, base, warm, via, feeder, amps):
        end = last_cell_row if a is warm else last_row
        row_args += [a, a]
        row_specs += [edge_rows(a, 0), edge_rows(a, end)]
    message = shape(2 * layers, SUB, cols)
    e, o = pl.pallas_call(
        pack_rows_kernel,
        grid=(1,),
        in_specs=row_specs,
        out_specs=(full(message), full(message)),
        out_shape=(message, message),
        compiler_params=pltpu.CompilerParams(vmem_limit_bytes=58 * 1024 * 1024),
        name="pack_rows",
    )(*row_args)
    row_e, row_o = swap(e, o, row_swaps)

    fields = (shape(layers, rows, cols),) * 10 + (shape(rows, LANE),) * 2
    node_scratch = pltpu.VMEM((layers, rows, cols), f32)
    g, inject, *mid = pl.pallas_call(
        bulk_first_kernel,
        out_shape=fields,
        scratch_shapes=[node_scratch],
        compiler_params=params,
        name="bulk_first",
        cost_estimate=pl.CostEstimate(flops=40 * x.size, bytes_accessed=60 * x.size, transcendentals=0),
    )(x, base, warm, via, feeder, amps)
    x_mid, w_mid, d_mid, inv_diag, g_diag, j_diag, edge_h, edge_v, own_e, own_o = mid

    col_args, col_specs = [], []
    for a in (x, g, inject, via):
        col_args += [a, a]
        col_specs += [edge_cols(a, 0), edge_cols(a, last_col)]
    message = shape(rows + 2 * SUB, LANE)
    e, o = pl.pallas_call(
        pack_cols_kernel,
        out_shape=(message, message),
        compiler_params=params,
        name="pack_cols",
    )(row_e, row_o, own_e, own_o, warm)
    col_e, col_o = swap(e, o, col_swaps)

    def strip_scratch(height, width):
        node = pltpu.VMEM((layers, height, width), f32)
        taller = pltpu.VMEM((layers, width // LANE, height + SUB, LANE), f32)
        return [node] * 3 + [pltpu.VMEM((layers - 1, height, width), f32)] + [node] * 9 + [taller] * 3 + [node] * 2

    def edge_deep(a, at):
        return pl.BlockSpec((a.shape[0], 2 * SUB, a.shape[2]), lambda _, at=at: (0, at, 0))

    deep_args, deep_specs = [], []
    for a in (x, g, inject, via):
        deep_args += [a, a]
        deep_specs += [edge_deep(a, 0), edge_deep(a, rows // (2 * SUB) - 1)]
    edge_x, edge_h2 = shape(layers, 4 * SUB, cols), shape(layers, SUB, cells)
    strip = shape(4 * layers - 1, rows + 2 * SUB, LANE)
    x_rows, heat_strip, strip = pl.pallas_call(
        row_strip_kernel,
        grid=(1,),
        in_specs=deep_specs + col_specs + [full(row_e), full(row_o)],
        out_specs=(full(edge_x), full(edge_h2), full(strip)),
        out_shape=(edge_x, edge_h2, strip),
        scratch_shapes=strip_scratch(6 * SUB, cols),
        compiler_params=params,
        name="row_strip",
        cost_estimate=pl.CostEstimate(flops=40 * x.size, bytes_accessed=20 * x.size, transcendentals=0),
    )(*deep_args, *col_args, row_e, row_o)

    x_cols, heat_cols, heat_edge = pl.pallas_call(
        col_strip_kernel,
        out_shape=(shape(layers, rows, LANE), shape(layers, cell_rows, cells), edge_h2),
        scratch_shapes=strip_scratch(rows + 2 * SUB, LANE),
        compiler_params=params,
        name="col_strip",
    )(strip, col_e, col_o, heat_strip)
    heat_row_e, heat_row_o = swap(heat_edge, heat_edge, row_swaps)

    assert SWEEPS == 3
    x_done = pl.pallas_call(
        bulk_mid_kernel,
        out_shape=shape(layers, rows, cols),
        scratch_shapes=[node_scratch] * 3,
        compiler_params=params,
        name="bulk_mid",
        cost_estimate=pl.CostEstimate(flops=20 * x.size, bytes_accessed=20 * x.size, transcendentals=0),
    )(x_mid, via, w_mid, d_mid, inv_diag, g_diag, j_diag, g)

    message = shape(cell_rows + 2 * SUB, LANE)
    e, o = pl.pallas_call(
        pack_heat_kernel,
        in_specs=[pl.BlockSpec(memory_space=pltpu.VMEM)] * 3 + [pl.BlockSpec(memory_space=pl.ANY)],
        out_shape=(message, message),
        compiler_params=params,
        name="pack_heat",
    )(heat_cols, heat_row_e, heat_row_o, x_done)
    heat_col_e, heat_col_o = swap(e, o, col_swaps)

    tall = pltpu.VMEM((layers, cols // LANE, rows + SUB, LANE), f32)
    voltage, heat = pl.pallas_call(
        bulk_last_kernel,
        out_shape=(shape(layers, rows, cols), shape(layers, cell_rows, cells)),
        out_specs=(pl.BlockSpec(memory_space=pl.ANY), pl.BlockSpec(memory_space=pltpu.VMEM)),
        scratch_shapes=[tall] * 3 + [node_scratch, pltpu.SemaphoreType.DMA],
        compiler_params=params,
        name="bulk_last",
        cost_estimate=pl.CostEstimate(flops=40 * x.size, bytes_accessed=60 * x.size, transcendentals=0),
    )(x_done, via, edge_h, edge_v, x_rows, x_cols)

    warmth = pl.pallas_call(
        warm_kernel,
        out_shape=shape(layers, cell_rows, cells),
        compiler_params=params,
        name="warm",
    )(warm, heat, heat_edge, heat_cols, row_e, row_o, col_e, col_o, heat_row_e, heat_row_o, heat_col_e, heat_col_o)
    return voltage, warmth


def solution(mesh):
    placed = P(None, "row", "col")
    return jax.shard_map(
        on_device,
        mesh=mesh,
        in_specs=(placed,) * 6,
        out_specs=(placed, placed),
        check_vma=False,
    )
```

```python
import jax
import jax.numpy as jnp
from jax import lax
from jax.experimental import pallas as pl
from jax.experimental.pallas import tpu as pltpu
from jax.sharding import PartitionSpec as P

REFINE = 4
SWEEPS = 3
HEAT_SWEEPS = 4

warmth_sensitivity = 0.5
leak_cond = 0.2
spectrum_low = 0.05
spectrum_high = 1.95
warming_weight = 0.3
heat_gain = 0.0625
interval_length = 0.12

SUB = 8
LANE = 128
REACH = 4
BOTH = ("row", "col")
HIGHEST = lax.Precision.HIGHEST


def row_swaps(rows, cols, first):
    pairs = []
    for r in range(rows):
        for c in range(cols):
            p = r + 1 if (r - first) % 2 == 0 else r - 1
            if 0 <= p < rows:
                pairs.append((r * cols + c, p * cols + c))
            elif c ^ 1 < cols:
                pairs.append((r * cols + c, r * cols + (c ^ 1)))
    return pairs


def col_swaps(rows, cols, first):
    pairs = []
    for r in range(rows):
        for c in range(cols):
            p = c + 1 if (c - first) % 2 == 0 else c - 1
            if 0 <= p < cols:
                pairs.append((r * cols + c, r * cols + p))
            elif r ^ 1 < rows:
                pairs.append((r * cols + c, (r ^ 1) * cols + c))
    return pairs


def iota(shape, dim):
    return lax.broadcasted_iota(jnp.int32, shape, dim)


def uniform(flag, shape):
    return jnp.full(shape, flag.astype(jnp.int32), jnp.int32) == 1


def place(axis):
    at = lax.axis_index(axis)
    return at % 2 == 0, at > 0, at < lax.axis_size(axis) - 1


def dot(a, b):
    return jnp.dot(a, b, precision=HIGHEST, preferred_element_type=jnp.float32)


def spread_lanes(cells, nodes):
    same = lax.shift_right_logical(iota((cells, nodes), 1), 2) == iota((cells, nodes), 0)
    return same.astype(jnp.float32)


def gather_lanes(nodes, cells):
    same = lax.shift_right_logical(iota((nodes, cells), 0), 2) == iota((nodes, cells), 1)
    return same.astype(jnp.float32)


def pack_rows_kernel(x_t, x_b, b_t, b_b, w_t, w_b, v_t, v_b, f_t, f_b, a_t, a_b, e_ref, o_ref):
    layers, _, cols = x_t.shape
    cells = w_t.shape[2]
    even, _, _ = place("row")
    low = iota((SUB, cols), 0) < REACH
    spread = spread_lanes(cells, cols)

    def planes(x, b, w, v, f, a, cell_row):
        warm = jnp.concatenate([w[l, cell_row : cell_row + 1, :] for l in range(layers)] * 2, 0)
        warm = dot(jnp.exp(-0.5 * warmth_sensitivity * warm), spread)
        xs = [x[l] for l in range(layers)]
        gs = [jnp.sqrt(b[l]) * warm[l : l + 1] for l in range(layers)]
        js = [f[l].astype(jnp.float32) * a[l] for l in range(layers)]
        vs = [v[l].astype(jnp.float32) for l in range(layers - 1)]
        ws = [jnp.concatenate([w[l] for l in range(layers)], axis=1)]
        return xs + gs, js + vs + ws

    top_a, top_b = planes(x_t, b_t, w_t, v_t, f_t, a_t, 0)
    bot_a, bot_b = planes(x_b, b_b, w_b, v_b, f_b, a_b, SUB - 1)
    pick = uniform(even, (SUB, cols))
    for k in range(2 * layers):
        top = jnp.where(low, top_a[k], pltpu.roll(top_b[k], REACH, 0))
        bot = jnp.where(low, pltpu.roll(bot_a[k], REACH, 0), bot_b[k])
        e_ref[k] = jnp.where(pick, bot, top)
        o_ref[k] = jnp.where(pick, top, bot)


def row_margin(e_ref, o_ref, plane, cols, half):
    even, above, below = place("row")
    k = plane % half
    e, o = e_ref[k, :, cols], o_ref[k, :, cols]
    pick = uniform(even, e.shape)
    top, bot = jnp.where(pick, o, e), jnp.where(pick, e, o)
    if plane < half:
        top = pltpu.roll(top, REACH, 0)
    else:
        bot = pltpu.roll(bot, REACH, 0)
    return (
        jnp.where(uniform(above, top.shape), top, 0.0),
        jnp.where(uniform(below, bot.shape), bot, 0.0),
    )


def packed(values, side, high, out):
    lane = iota(out.shape, 1)
    slot, upper = lax.shift_right_logical(lane, 3), lane % 8 >= REACH
    for p, value in enumerate(values):
        shift = (8 * p + REACH * (side + high)) % LANE
        value = pltpu.roll(value.astype(jnp.float32), shift, 1) if shift else value
        out = jnp.where((slot == p) & (upper if high else ~upper), value, out)
    return out


def end_tiles(width):
    return slice(0, LANE), slice(width - LANE, width)


def pack_own_columns(fields, w_ref, e_ref, o_ref):
    rows, cols = fields[0].shape[1:]
    layers, cell_rows, cells = w_ref.shape
    sides = []
    for side in range(2):
        tile, cell_tile = end_tiles(cols)[side], end_tiles(cells)[side]
        values = [ref[l, :, tile] for ref in fields for l in range(ref.shape[0])]
        out = packed(values, side, False, jnp.zeros((rows, LANE), jnp.float32))
        head = packed([w_ref[l, :, cell_tile] for l in range(layers)], side, True, out[:cell_rows])
        sides.append(jnp.concatenate([head, out[cell_rows:]], axis=0))
    even, _, _ = place("col")
    pick = uniform(even, (rows, LANE))
    e_ref[...] = jnp.where(pick, sides[1], sides[0])
    o_ref[...] = jnp.where(pick, sides[0], sides[1])


def pack_cols_kernel(re_ref, ro_ref, own_e, own_o, w_ref, e_ref, o_ref):
    rows, cols = own_e.shape[0], re_ref.shape[2]
    layers, cell_rows, cells = w_ref.shape
    half = 2 * layers
    even, _, _ = place("col")
    pick = uniform(even, (SUB, LANE))
    zero = jnp.zeros((SUB, LANE), jnp.float32)
    tops, bots, lows = [], [], []
    for side in range(2):
        tile, cell_tile = end_tiles(cols)[side], end_tiles(cells)[side]
        margins = [row_margin(re_ref, ro_ref, p, tile, half) for p in range(2 * half - 1)]
        warm = [
            row_margin(
                re_ref, ro_ref, 2 * half - 1,
                slice(l * cells + cell_tile.start, l * cells + cell_tile.stop), half,
            )
            for l in range(layers)
        ]
        tops.append(packed([m[0] for m in warm], side, True, packed([m[0] for m in margins], side, False, zero)))
        bots.append(packed([m[1] for m in margins], side, False, zero))
        lows.append(packed([m[1] for m in warm], side, True, zero))
    high = iota((SUB, LANE), 1) % 8 >= REACH
    at = SUB + cell_rows
    for ref, own, first in ((e_ref, own_e, 1), (o_ref, own_o, 0)):
        ref[SUB : SUB + rows, :] = own[...]
        ref[0:SUB, :] = jnp.where(pick, tops[first], tops[1 - first])
        ref[SUB + rows : 2 * SUB + rows, :] = jnp.where(pick, bots[first], bots[1 - first])
        low = jnp.where(pick, lows[first], lows[1 - first])
        ref[at : at + SUB, :] = jnp.where(high, low, own[cell_rows : cell_rows + SUB, :])


def col_margin(e, o, high, back):
    even, before, after = place("col")
    lane = iota(e.shape, 1)
    pick = uniform(even, e.shape)
    right, left = jnp.where(pick, e, o), jnp.where(pick, o, e)
    right = jnp.where(uniform(after, e.shape), right, 0.0)
    left = jnp.where(uniform(before, e.shape), left, 0.0)
    own_half = lane % 8 >= REACH if high else lane % 8 < REACH
    return jnp.where(own_half, right, pltpu.roll(left, LANE - back, 1))


def margin_tile(mixed, shift):
    lane = iota(mixed.shape, 1)
    value = mixed if shift == 0 else pltpu.roll(mixed, LANE - shift, 1)
    return jnp.where((lane < REACH) | (lane >= LANE - REACH), value, 0.0)


CENTER = 0.5 * (spectrum_high + spectrum_low)
HALF = 0.5 * (spectrum_high - spectrum_low)
SIGMA = CENTER / HALF


def sweep_gains():
    rho, gains = 1.0 / SIGMA, []
    for _ in range(SWEEPS - 1):
        rho_new = 1.0 / (2.0 * SIGMA - rho)
        gains.append((rho_new * rho, 2.0 * rho_new / HALF))
        rho = rho_new
    return gains


def tile_rows(i):
    return pl.ds(pl.multiple_of(i * SUB, SUB), SUB)


def each(first, last, unroll, body):
    if unroll >= last - first:
        for i in range(first, last):
            body(i)
    else:
        lax.fori_loop(first, last, lambda i, c: (body(i), c)[1], 0, unroll=unroll)


def before(i):
    return max(i - 1, 0) if isinstance(i, int) else jnp.maximum(i - 1, 0)


def after(i, groups):
    return min(i + 1, groups - 1) if isinstance(i, int) else jnp.minimum(i + 1, groups - 1)


def shifted_down(here, nxt):
    return jnp.where(
        iota(here.shape, 0) == SUB - 1, pltpu.roll(nxt, SUB - 1, 0), pltpu.roll(here, SUB - 1, 0)
    )


def shifted_up(prev, here):
    return jnp.where(iota(here.shape, 0) == 0, pltpu.roll(prev, 1, 0), pltpu.roll(here, 1, 0))


def around(ref, l, i, groups):
    here = ref[l, tile_rows(i), :]
    width = here.shape[1]
    up = shifted_up(ref[l, tile_rows(before(i)), :], here)
    down = shifted_down(here, ref[l, tile_rows(after(i, groups)), :])
    return up, down, pltpu.roll(here, 1, 1), pltpu.roll(here, width - 1, 1)


def added(four):
    return (four[0] + four[1]) + (four[2] + four[3])


def upright(l, xs, vs):
    layers = len(xs)
    if l == 0:
        return vs[0] * xs[1]
    if l == layers - 1:
        return vs[l - 1] * xs[l - 1]
    return vs[l] * xs[l + 1] + vs[l - 1] * xs[l - 1]


def load_vias(V, r):
    return [V[l, r, :].astype(jnp.float32) for l in range(V.shape[0])]


def first_sweep(unroll, skip, X, G, J, V, W0, XN, WN, D, DI, GD, JD, EH, EV):
    layers, height, _ = X.shape
    groups = height // SUB

    def start(i):
        r = tile_rows(i)
        for l in range(layers):
            W0[l, r, :] = G[l, r, :] * X[l, r, :]

    each(0, groups, unroll, start)

    def body(i):
        r = tile_rows(i)
        xs = [X[l, r, :] for l in range(layers)]
        vs = load_vias(V, r)
        for l in range(layers):
            g = G[l, r, :]
            four = around(G, l, i, groups)
            diag = leak_cond + g * added(four)
            EV[l, r, :] = g * four[1]
            EH[l, r, :] = g * four[3]
            if l < layers - 1:
                diag = diag + vs[l]
            if l > 0:
                diag = diag + vs[l - 1]
            inverse = 1.0 / diag
            gd, jd = g * inverse, J[l, r, :] * inverse
            near = added(around(W0, l, i, groups))
            d = (jd + gd * near + inverse * upright(l, xs, vs) - xs[l]) / CENTER
            x = xs[l] + d
            DI[l, r, :], GD[l, r, :], JD[l, r, :], D[l, r, :] = inverse, gd, jd, d
            XN[l, r, :] = x
            WN[l, r, :] = g * x

    each(skip, groups - skip, unroll, body)


def next_sweep(unroll, skip, keep, gain, X, V, W, D, DI, GD, JD, G, XN, WN=None, DN=None):
    layers, height, _ = X.shape
    groups = height // SUB

    def body(i):
        r = tile_rows(i)
        xs = [X[l, r, :] for l in range(layers)]
        vs = load_vias(V, r)
        for l in range(layers):
            near = added(around(W, l, i, groups))
            resid = (
                JD[l, r, :] + GD[l, r, :] * near + DI[l, r, :] * upright(l, xs, vs) - xs[l]
            )
            d = keep * D[l, r, :] + gain * resid
            x = xs[l] + d
            XN[l, r, :] = x
            if WN is not None:
                DN[l, r, :] = d
                WN[l, r, :] = G[l, r, :] * x

    each(skip, groups - skip, unroll, body)


def later_sweeps(unroll, X, V, W, D, DI, GD, JD, G, WN, XN, DN):
    gains = sweep_gains()
    x, w, d, other = X, W, D, WN
    for at, (keep, gain) in enumerate(gains):
        if at == len(gains) - 1:
            next_sweep(unroll, 0, keep, gain, x, V, w, d, DI, GD, JD, G, XN)
        else:
            next_sweep(unroll, 0, keep, gain, x, V, w, d, DI, GD, JD, G, XN, other, DN)
            assert len(gains) <= 2
            x, w, d = XN, other, DN


def power_rows(first, last, unroll, X, V, EH, EV, PA, PB, PD):
    layers, height, width = X.shape
    groups = height // SUB
    share = jnp.where(iota((SUB, width), 0) % REFINE == REFINE - 1, 0.5, 1.0)
    lane_share = jnp.where(iota((SUB, width), 1) % REFINE == REFINE - 1, 1.0, 2.0)

    def fold(v):
        v = v + pltpu.roll(v, SUB - 1, 0)
        return v + pltpu.roll(v, SUB - 2, 0)

    def body(i):
        r = tile_rows(i)
        out = tile_rows(i + 1)
        xs = [X[l, r, :] for l in range(layers)]
        vs = load_vias(V, r)
        drops = [0.5 * vs[l] * (xs[l] - xs[l + 1]) ** 2 for l in range(layers - 1)]
        for l in range(layers):
            x = xs[l]
            across = x - pltpu.roll(x, width - 1, 1)
            down = x - shifted_down(x, X[l, tile_rows(after(i, groups)), :])
            across = 0.5 * EH[l, r, :] * (across * across)
            down = EV[l, r, :] * (down * down)
            total = leak_cond * (x * x) + share * down + lane_share * across
            if l < layers - 1:
                total = total + drops[l]
            if l > 0:
                total = total + drops[l - 1]
            total, across = fold(total), fold(across)
            for t in range(width // LANE):
                tile = slice(t * LANE, (t + 1) * LANE)
                PA[l, t, out, :] = total[:, tile]
                PB[l, t, out, :] = across[:, tile]
                PD[l, t, out, :] = down[:, tile]

    each(first, last, unroll, body)


def fold_power(row, cells, PA, PB, PD, same, left):
    layers = PA.shape[0]
    at = pl.ds(row + SUB, cells, stride=REFINE)
    up = pl.ds(row + SUB - 1, cells, stride=REFINE)
    tiles = range(PA.shape[1])
    a = [
        jnp.concatenate([PA[l, t, at, :] + 0.5 * PD[l, t, up, :] for t in tiles], 1)
        for l in range(layers)
    ]
    b = [jnp.concatenate([PB[l, t, at, :] for t in tiles], 1) for l in range(layers)]
    a, b = jnp.concatenate(a, 0), jnp.concatenate(b, 0)
    heat = (dot(a, same) + dot(b, left)) * heat_gain
    return [heat[l * cells : (l + 1) * cells] for l in range(layers)]


def fold_matrices(nodes, cells):
    n, c = iota((nodes, cells), 0), iota((nodes, cells), 1)
    same = lax.shift_right_logical(n, 2) == c
    return same.astype(jnp.float32), (n == REFINE * c - 1).astype(jnp.float32)


def bulk_first_kernel(
    x_ref, b_ref, w_ref, v_ref, f_ref, a_ref,
    g_ref, j_ref, XN, WN, D, DI, GD, JD, EH, EV, own_e, own_o,
    W0,
):
    layers, rows, cols = x_ref.shape
    _, cell_rows, cells = w_ref.shape
    spread_rows = gather_lanes(rows, cell_rows)
    spread = spread_lanes(cells, cols)
    for l in range(layers):
        warm = jnp.exp(-0.5 * warmth_sensitivity * w_ref[l])
        g_ref[l] = jnp.sqrt(b_ref[l]) * dot(spread_rows, dot(warm, spread))
        j_ref[l] = f_ref[l].astype(jnp.float32) * a_ref[l]
    pack_own_columns((x_ref, g_ref, j_ref, v_ref), w_ref, own_e, own_o)
    first_sweep(2, 1, x_ref, g_ref, j_ref, v_ref, W0, XN, WN, D, DI, GD, JD, EH, EV)


def bulk_mid_kernel(X, V, W, D, DI, GD, JD, G, XL, WN, XN, DN):
    (keep, gain), (keep_last, gain_last) = sweep_gains()
    next_sweep(2, 1, keep, gain, X, V, W, D, DI, GD, JD, G, XN, WN, DN)
    next_sweep(2, 1, keep_last, gain_last, XN, V, WN, DN, DI, GD, JD, G, XL)


def bulk_last_kernel(
    XN, V, EH, EV, xr_ref, xc_ref,
    x_hbm, h_ref,
    PA, PB, PD, out, sem,
):
    layers, rows, cols = XN.shape
    cell_rows, cells = h_ref.shape[1:]
    groups = rows // SUB
    lane = iota((rows, LANE), 1)
    low = iota((SUB, LANE), 0) < REACH
    for l in range(layers):
        for t in range(cols // LANE):
            tile = slice(t * LANE, (t + 1) * LANE)
            x = jnp.concatenate(
                [
                    xr_ref[l, 0:SUB, tile],
                    jnp.where(low, xr_ref[l, SUB : 2 * SUB, tile], XN[l, SUB : 2 * SUB, tile]),
                    XN[l, 2 * SUB : rows - 2 * SUB, tile],
                    jnp.where(
                        low,
                        XN[l, rows - 2 * SUB : rows - SUB, tile],
                        xr_ref[l, 2 * SUB : 3 * SUB, tile],
                    ),
                    xr_ref[l, 3 * SUB : 4 * SUB, tile],
                ],
                0,
            )
            if t == 0:
                x = jnp.where(lane < SUB, xc_ref[l], x)
            if t == cols // LANE - 1:
                x = jnp.where(lane >= LANE - SUB, xc_ref[l], x)
            out[l, :, tile] = x
    copy = pltpu.make_async_copy(out, x_hbm, sem)
    copy.start()
    power_rows(1, groups - 1, 2, XN, V, EH, EV, PA, PB, PD)
    heat = fold_power(0, cell_rows, PA, PB, PD, *fold_matrices(cols, cells))
    for l in range(layers):
        h_ref[l] = heat[l]
    copy.wait()


def row_strip_kernel(
    x_t, x_b, g_t, g_b, j_t, j_b, v_t, v_b,
    x_l, x_r, g_l, g_r, j_l, j_r, v_l, v_r,
    re_ref, ro_ref,
    xr_ref, h_ref, strip_ref,
    X, G, J, V, W0, XN, WN, D, DI, GD, JD, EH, EV, PA, PB, PD, DN, XL,
):
    layers, deep, cols = x_t.shape
    rows = x_l.shape[1]
    cells = h_ref.shape[2]
    half = 2 * layers
    height = 2 * (SUB + deep)
    plane = 0
    tall = strip_ref.shape[1]
    lane = iota((tall, LANE), 1)
    for top_ref, bot_ref, left_ref, right_ref, pad in (
        (x_t, x_b, x_l, x_r, X), (g_t, g_b, g_l, g_r, G), (j_t, j_b, j_l, j_r, J), (v_t, v_b, v_l, v_r, V),
    ):
        for l in range(top_ref.shape[0]):
            top, bot = row_margin(re_ref, ro_ref, plane, slice(0, cols), half)
            pad[l, 0:SUB, :] = top
            pad[l, SUB : SUB + deep, :] = top_ref[l].astype(jnp.float32)
            pad[l, SUB + deep : SUB + 2 * deep, :] = bot_ref[l].astype(jnp.float32)
            pad[l, SUB + 2 * deep : height, :] = bot
            left = jnp.concatenate([top[:, :LANE], left_ref[l].astype(jnp.float32), bot[:, :LANE]], 0)
            right = jnp.concatenate(
                [top[:, cols - LANE :], right_ref[l].astype(jnp.float32), bot[:, cols - LANE :]], 0
            )
            strip_ref[plane] = jnp.where(
                lane < LANE // 2,
                jnp.where(lane < LANE // 4, left[:tall], pltpu.roll(right[:tall], 48, 1)),
                jnp.where(
                    lane < 3 * LANE // 4,
                    pltpu.roll(left[rows + 2 * SUB - tall :], 64, 1),
                    pltpu.roll(right[rows + 2 * SUB - tall :], 112, 1),
                ),
            )
            plane += 1
    first_sweep(6, 0, X, G, J, V, W0, XN, WN, D, DI, GD, JD, EH, EV)
    later_sweeps(6, XN, V, WN, D, DI, GD, JD, G, W0, XL, DN)
    groups = height // SUB
    power_rows(0, groups - 1, 6, XL, V, EH, EV, PA, PB, PD)
    heat = fold_power(SUB, 2 * SUB // 2, PA, PB, PD, *fold_matrices(cols, cells))
    for l in range(layers):
        h_ref[l] = heat[l]
        xr_ref[l] = XL[l, SUB : height - SUB, :]


def col_strip_kernel(
    strip_ref, ce_ref, co_ref, hr_ref,
    xc_ref, hc_ref, hm_ref,
    X, G, J, V, W0, XN, WN, D, DI, GD, JD, EH, EV, PA, PB, PD, DN, XL,
):
    layers, rows, _ = xc_ref.shape
    cell_rows, cells = hc_ref.shape[1:]
    tall = strip_ref.shape[1]
    mixed = col_margin(ce_ref[...], co_ref[...], False, 52)
    upper, lower = mixed[:tall], mixed[rows + 2 * SUB - tall :]
    lane = iota((tall, LANE), 1)
    in_upper = ((lane >= 48) & (lane < 48 + REACH)) | (lane >= LANE - REACH)
    in_lower = ((lane >= 112) & (lane < 112 + REACH)) | ((lane >= 64 - REACH) & (lane < 64))
    plane = 0
    for pad in (X, G, J, V):
        for l in range(pad.shape[0]):
            shift = (48 - 8 * plane) % LANE
            value = pltpu.roll(upper, shift, 1) if shift else upper
            shift = (112 - 8 * plane) % LANE
            other = pltpu.roll(lower, shift, 1) if shift else lower
            value = jnp.where(in_upper, value, strip_ref[plane])
            pad[l] = jnp.where(in_lower, other, value)
            plane += 1
    groups = tall // SUB
    first_sweep(groups, 0, X, G, J, V, W0, XN, WN, D, DI, GD, JD, EH, EV)
    later_sweeps(groups, XN, V, WN, D, DI, GD, JD, G, W0, XL, DN)
    power_rows(0, groups - 1, groups, XL, V, EH, EV, PA, PB, PD)
    n, c = iota((LANE, cells), 0), iota((LANE, cells), 1)
    at_edge = (c < REACH) | (c >= cells - REACH)
    halves = []
    for part in range(2):
        slot = jnp.where(c < cells // 2, c, c - cells + 12) + 16 * part
        same = at_edge & (lax.shift_right_logical(n, 2) == slot)
        left = at_edge & (n == jnp.where(slot == 0, LANE - 1, REFINE * slot - 1))
        halves.append(
            fold_power(
                SUB, cell_rows // 2, PA, PB, PD, same.astype(jnp.float32), left.astype(jnp.float32)
            )
        )
    lane = iota((rows // 2, LANE), 1)
    cell = iota((SUB, cells), 1)
    edge = (cell < REACH - 1) | (cell > cells - REACH)
    low = lane < LANE // 2
    for l in range(layers):
        first, final = halves[0][l], halves[1][l]
        hc_ref[l, 0 : cell_rows // 2, :] = first
        hc_ref[l, cell_rows // 2 : cell_rows, :] = final
        x = XL[l, SUB : SUB + rows // 2, :]
        xc_ref[l, 0 : rows // 2, :] = jnp.where(low, x, pltpu.roll(x, 80, 1))
        xc_ref[l, rows // 2 : rows, :] = jnp.where(low, pltpu.roll(x, 64, 1), pltpu.roll(x, 16, 1))
        own = jnp.concatenate([first[:REACH], final[cell_rows // 2 - REACH :]], 0)
        hm_ref[l] = jnp.where(edge, own, hr_ref[l])


def heat_rows(own, e_ref, o_ref, l):
    even, above, below = place("row")
    e, o = e_ref[l], o_ref[l]
    pick = uniform(even, e.shape)
    top = jnp.where(uniform(above, e.shape), jnp.where(pick, o, e), 0.0)
    bot = jnp.where(uniform(below, e.shape), jnp.where(pick, e, o), 0.0)
    return jnp.concatenate([top, own, bot], axis=0)


def pack_heat_kernel(h_ref, re_ref, ro_ref, _, e_ref, o_ref):
    layers, cell_rows, cells = h_ref.shape
    height = cell_rows + 2 * SUB
    even, _, _ = place("col")
    lane = iota((height, LANE), 1)
    slot, low = lax.shift_right_logical(lane, 3), lane % 8 < REACH
    left = right = jnp.zeros((height, LANE), jnp.float32)
    for l in range(layers):
        value = heat_rows(h_ref[l], re_ref, ro_ref, l)
        mine = (slot == l) & low
        left = jnp.where(mine, pltpu.roll(value[:, :LANE], 8 * l, 1) if l else value[:, :LANE], left)
        right = jnp.where(mine, pltpu.roll(value[:, cells - LANE :], 8 * l + REACH, 1), right)
    pick = uniform(even, (height, LANE))
    e_ref[...] = jnp.where(pick, right, left)
    o_ref[...] = jnp.where(pick, left, right)


def warm_kernel(
    w_ref, h_ref, hm_ref, hc_ref, re_ref, ro_ref, ce_ref, co_ref,
    hre_ref, hro_ref, hce_ref, hco_ref, out_ref,
):
    layers, cell_rows, cells = w_ref.shape
    half = 2 * layers
    height, width = cell_rows + 2 * SUB, cells + LANE
    warm_mixed = col_margin(ce_ref[0:height, :], co_ref[0:height, :], True, REACH)
    heat_mixed = col_margin(hce_ref[...], hco_ref[...], False, REACH)
    cell = iota((cell_rows, cells), 1)
    edge = (cell < REACH - 1) | (cell > cells - REACH)
    cell_row = iota((SUB, cells), 0)
    theta, heat = [], []
    for l in range(layers):
        top, bot = row_margin(
            re_ref, ro_ref, 2 * half - 1, slice(l * cells, (l + 1) * cells), half
        )
        own = jnp.concatenate([top, w_ref[l], bot], axis=0)
        theta.append(jnp.concatenate([own, margin_tile(warm_mixed, 8 * l + REACH)], axis=1))
        own = jnp.where(edge, hc_ref[l], h_ref[l])
        first, final = own[:SUB], own[cell_rows - SUB :]
        first = jnp.where(cell_row < REACH - 1, hm_ref[l], first)
        final = jnp.where(cell_row > SUB - REACH, hm_ref[l], final)
        own = jnp.concatenate([first, own[SUB : cell_rows - SUB], final], axis=0)
        own = heat_rows(own, hre_ref, hro_ref, l)
        heat.append(jnp.concatenate([own, margin_tile(heat_mixed, 8 * l)], axis=1))
    _, above, below = place("row")
    _, before, after = place("col")
    shape = (height, width)
    r, c = iota(shape, 0), iota(shape, 1)
    inside = (uniform(above, shape) | (r >= SUB)) & (uniform(below, shape) | (r < height - SUB))
    inside = inside & (uniform(after, shape) | (c < cells) | (c >= cells + LANE // 2))
    inside = inside & (uniform(before, shape) | (c < cells + LANE // 2))

    def around_cells(v):
        return (pltpu.roll(v, 1, 0) + pltpu.roll(v, height - 1, 0)) + (
            pltpu.roll(v, 1, 1) + pltpu.roll(v, width - 1, 1)
        )

    for _ in range(HEAT_SWEEPS):
        later = []
        for l in range(layers):
            t = theta[l]
            q = jnp.where(inside, jnp.exp(-0.5 * warming_weight * t), 0.0)
            change = q * (around_cells(q * t) - t * around_cells(q)) + heat[l]
            if l < layers - 1:
                change = change + (theta[l + 1] - t)
            if l > 0:
                change = change + (theta[l - 1] - t)
            if l == layers - 1:
                change = change - t
            later.append(t + interval_length * change)
        theta = later
    for l in range(layers):
        out_ref[l] = theta[l][SUB : SUB + cell_rows, :cells]


def on_device(x, base, warm, via, feeder, amps):
    layers, rows, cols = x.shape
    _, cell_rows, cells = warm.shape
    f32 = jnp.float32
    mesh_rows, mesh_cols = lax.axis_size("row"), lax.axis_size("col")
    last_row, last_cell_row, last_col = rows // SUB - 1, cell_rows // SUB - 1, cols // LANE - 1

    def shape(*dims):
        return jax.ShapeDtypeStruct(dims, f32)

    def edge_rows(a, at):
        return pl.BlockSpec((a.shape[0], SUB, a.shape[2]), lambda _, at=at: (0, at, 0))

    def edge_cols(a, at):
        return pl.BlockSpec((a.shape[0], a.shape[1], LANE), lambda _, at=at: (0, 0, at))

    def full(a):
        return pl.BlockSpec(a.shape, lambda _, n=len(a.shape): (0,) * n)

    def swap(e, o, tables):
        return tuple(
            lax.ppermute(m, BOTH, tables(mesh_rows, mesh_cols, first)) for first, m in enumerate((e, o))
        )

    params = pltpu.CompilerParams(vmem_limit_bytes=24 * 1024 * 1024)
    row_args, row_specs = [], []
    for a in (x, base, warm, via, feeder, amps):
        end = last_cell_row if a is warm else last_row
        row_args += [a, a]
        row_specs += [edge_rows(a, 0), edge_rows(a, end)]
    message = shape(2 * layers, SUB, cols)
    e, o = pl.pallas_call(
        pack_rows_kernel,
        grid=(1,),
        in_specs=row_specs,
        out_specs=(full(message), full(message)),
        out_shape=(message, message),
        compiler_params=pltpu.CompilerParams(vmem_limit_bytes=58 * 1024 * 1024),
        name="pack_rows",
    )(*row_args)
    row_e, row_o = swap(e, o, row_swaps)

    fields = (shape(layers, rows, cols),) * 10 + (shape(rows, LANE),) * 2
    node_scratch = pltpu.VMEM((layers, rows, cols), f32)
    g, inject, *mid = pl.pallas_call(
        bulk_first_kernel,
        out_shape=fields,
        scratch_shapes=[node_scratch],
        compiler_params=params,
        name="bulk_first",
        cost_estimate=pl.CostEstimate(flops=40 * x.size, bytes_accessed=60 * x.size, transcendentals=0),
    )(x, base, warm, via, feeder, amps)
    x_mid, w_mid, d_mid, inv_diag, g_diag, j_diag, edge_h, edge_v, own_e, own_o = mid

    col_args, col_specs = [], []
    for a in (x, g, inject, via):
        col_args += [a, a]
        col_specs += [edge_cols(a, 0), edge_cols(a, last_col)]
    message = shape(rows + 2 * SUB, LANE)
    e, o = pl.pallas_call(
        pack_cols_kernel,
        out_shape=(message, message),
        compiler_params=params,
        name="pack_cols",
    )(row_e, row_o, own_e, own_o, warm)
    col_e, col_o = swap(e, o, col_swaps)

    def strip_scratch(height, width):
        node = pltpu.VMEM((layers, height, width), f32)
        taller = pltpu.VMEM((layers, width // LANE, height + SUB, LANE), f32)
        return [node] * 3 + [pltpu.VMEM((layers - 1, height, width), f32)] + [node] * 9 + [taller] * 3 + [node] * 2

    def edge_deep(a, at):
        return pl.BlockSpec((a.shape[0], 2 * SUB, a.shape[2]), lambda _, at=at: (0, at, 0))

    deep_args, deep_specs = [], []
    for a in (x, g, inject, via):
        deep_args += [a, a]
        deep_specs += [edge_deep(a, 0), edge_deep(a, rows // (2 * SUB) - 1)]
    edge_x, edge_h2 = shape(layers, 4 * SUB, cols), shape(layers, SUB, cells)
    strip = shape(4 * layers - 1, rows // 2 + 2 * SUB, LANE)
    x_rows, heat_strip, strip = pl.pallas_call(
        row_strip_kernel,
        grid=(1,),
        in_specs=deep_specs + col_specs + [full(row_e), full(row_o)],
        out_specs=(full(edge_x), full(edge_h2), full(strip)),
        out_shape=(edge_x, edge_h2, strip),
        scratch_shapes=strip_scratch(6 * SUB, cols),
        compiler_params=params,
        name="row_strip",
        cost_estimate=pl.CostEstimate(flops=40 * x.size, bytes_accessed=20 * x.size, transcendentals=0),
    )(*deep_args, *col_args, row_e, row_o)

    x_cols, heat_cols, heat_edge = pl.pallas_call(
        col_strip_kernel,
        out_shape=(shape(layers, rows, LANE), shape(layers, cell_rows, cells), edge_h2),
        scratch_shapes=strip_scratch(rows // 2 + 2 * SUB, LANE),
        compiler_params=params,
        name="col_strip",
    )(strip, col_e, col_o, heat_strip)
    heat_row_e, heat_row_o = swap(heat_edge, heat_edge, row_swaps)

    assert SWEEPS == 3
    x_done = pl.pallas_call(
        bulk_mid_kernel,
        out_shape=shape(layers, rows, cols),
        scratch_shapes=[node_scratch] * 3,
        compiler_params=params,
        name="bulk_mid",
        cost_estimate=pl.CostEstimate(flops=20 * x.size, bytes_accessed=20 * x.size, transcendentals=0),
    )(x_mid, via, w_mid, d_mid, inv_diag, g_diag, j_diag, g)

    message = shape(cell_rows + 2 * SUB, LANE)
    e, o = pl.pallas_call(
        pack_heat_kernel,
        in_specs=[pl.BlockSpec(memory_space=pltpu.VMEM)] * 3 + [pl.BlockSpec(memory_space=pl.ANY)],
        out_shape=(message, message),
        compiler_params=params,
        name="pack_heat",
    )(heat_cols, heat_row_e, heat_row_o, x_done)
    heat_col_e, heat_col_o = swap(e, o, col_swaps)

    tall = pltpu.VMEM((layers, cols // LANE, rows + SUB, LANE), f32)
    voltage, heat = pl.pallas_call(
        bulk_last_kernel,
        out_shape=(shape(layers, rows, cols), shape(layers, cell_rows, cells)),
        out_specs=(pl.BlockSpec(memory_space=pl.ANY), pl.BlockSpec(memory_space=pltpu.VMEM)),
        scratch_shapes=[tall] * 3 + [node_scratch, pltpu.SemaphoreType.DMA],
        compiler_params=params,
        name="bulk_last",
        cost_estimate=pl.CostEstimate(flops=40 * x.size, bytes_accessed=60 * x.size, transcendentals=0),
    )(x_done, via, edge_h, edge_v, x_rows, x_cols)

    warmth = pl.pallas_call(
        warm_kernel,
        out_shape=shape(layers, cell_rows, cells),
        compiler_params=params,
        name="warm",
    )(warm, heat, heat_edge, heat_cols, row_e, row_o, col_e, col_o, heat_row_e, heat_row_o, heat_col_e, heat_col_o)
    return voltage, warmth


def solution(mesh):
    placed = P(None, "row", "col")
    return jax.shard_map(
        on_device,
        mesh=mesh,
        in_specs=(placed,) * 6,
        out_specs=(placed, placed),
        check_vma=False,
    )
```

```python
import jax
import jax.numpy as jnp
from jax import lax
from jax.experimental import pallas as pl
from jax.experimental.pallas import tpu as pltpu
from jax.sharding import PartitionSpec as P

REFINE = 4
SWEEPS = 3
HEAT_SWEEPS = 4

warmth_sensitivity = 0.5
leak_cond = 0.2
spectrum_low = 0.05
spectrum_high = 1.95
warming_weight = 0.3
heat_gain = 0.0625
interval_length = 0.12

SUB = 8
LANE = 128
REACH = 4
BOTH = ("row", "col")
HIGHEST = lax.Precision.HIGHEST


def row_swaps(rows, cols, first):
    pairs = []
    for r in range(rows):
        for c in range(cols):
            p = r + 1 if (r - first) % 2 == 0 else r - 1
            if 0 <= p < rows:
                pairs.append((r * cols + c, p * cols + c))
            elif c ^ 1 < cols:
                pairs.append((r * cols + c, r * cols + (c ^ 1)))
    return pairs


def col_swaps(rows, cols, first):
    pairs = []
    for r in range(rows):
        for c in range(cols):
            p = c + 1 if (c - first) % 2 == 0 else c - 1
            if 0 <= p < cols:
                pairs.append((r * cols + c, r * cols + p))
            elif r ^ 1 < rows:
                pairs.append((r * cols + c, (r ^ 1) * cols + c))
    return pairs


def iota(shape, dim):
    return lax.broadcasted_iota(jnp.int32, shape, dim)


def uniform(flag, shape):
    return jnp.full(shape, flag.astype(jnp.int32), jnp.int32) == 1


def place(axis):
    at = lax.axis_index(axis)
    return at % 2 == 0, at > 0, at < lax.axis_size(axis) - 1


def dot(a, b):
    return jnp.dot(a, b, precision=HIGHEST, preferred_element_type=jnp.float32)


def spread_lanes(cells, nodes):
    same = lax.shift_right_logical(iota((cells, nodes), 1), 2) == iota((cells, nodes), 0)
    return same.astype(jnp.float32)


def gather_lanes(nodes, cells):
    same = lax.shift_right_logical(iota((nodes, cells), 0), 2) == iota((nodes, cells), 1)
    return same.astype(jnp.float32)


def pack_rows_kernel(x_t, x_b, b_t, b_b, w_t, w_b, v_t, v_b, f_t, f_b, a_t, a_b, e_ref, o_ref):
    layers, _, cols = x_t.shape
    cells = w_t.shape[2]
    even, _, _ = place("row")
    low = iota((SUB, cols), 0) < REACH
    spread = spread_lanes(cells, cols)

    def planes(x, b, w, v, f, a, cell_row):
        warm = jnp.concatenate([w[l, cell_row : cell_row + 1, :] for l in range(layers)] * 2, 0)
        warm = dot(jnp.exp(-0.5 * warmth_sensitivity * warm), spread)
        xs = [x[l] for l in range(layers)]
        gs = [jnp.sqrt(b[l]) * warm[l : l + 1] for l in range(layers)]
        js = [f[l].astype(jnp.float32) * a[l] for l in range(layers)]
        vs = [v[l].astype(jnp.float32) for l in range(layers - 1)]
        ws = [jnp.concatenate([w[l] for l in range(layers)], axis=1)]
        return xs + gs, js + vs + ws

    top_a, top_b = planes(x_t, b_t, w_t, v_t, f_t, a_t, 0)
    bot_a, bot_b = planes(x_b, b_b, w_b, v_b, f_b, a_b, SUB - 1)
    pick = uniform(even, (SUB, cols))
    for k in range(2 * layers):
        top = jnp.where(low, top_a[k], pltpu.roll(top_b[k], REACH, 0))
        bot = jnp.where(low, pltpu.roll(bot_a[k], REACH, 0), bot_b[k])
        e_ref[k] = jnp.where(pick, bot, top)
        o_ref[k] = jnp.where(pick, top, bot)


def row_margin(e_ref, o_ref, plane, cols, half):
    even, above, below = place("row")
    k = plane % half
    e, o = e_ref[k, :, cols], o_ref[k, :, cols]
    pick = uniform(even, e.shape)
    top, bot = jnp.where(pick, o, e), jnp.where(pick, e, o)
    if plane < half:
        top = pltpu.roll(top, REACH, 0)
    else:
        bot = pltpu.roll(bot, REACH, 0)
    return (
        jnp.where(uniform(above, top.shape), top, 0.0),
        jnp.where(uniform(below, bot.shape), bot, 0.0),
    )


def put(out, value, at, side):
    at = at % LANE
    shift = (at + REACH * side) % LANE
    lane, value = iota(out.shape, 1), value.astype(jnp.float32)
    value = pltpu.roll(value, shift, 1) if shift else value
    return jnp.where((lane >= at) & (lane < at + REACH), value, out)


def end_tiles(width):
    return slice(0, LANE), slice(width - LANE, width)


LOWER = LANE // 2 + REACH


def pack_own_columns(fields, w_ref, e_ref, o_ref):
    rows, cols = fields[0].shape[1:]
    layers, cell_rows, cells = w_ref.shape
    part = rows // 2 + SUB
    zero = jnp.zeros((SUB, LANE), jnp.float32)
    sides = []
    for side in range(2):
        tile, cell_tile = end_tiles(cols)[side], end_tiles(cells)[side]
        values = [ref[l, :, tile] for ref in fields for l in range(ref.shape[0])]
        out = jnp.zeros((part + SUB, LANE), jnp.float32)
        for p, value in enumerate(values):
            value = value.astype(jnp.float32)
            out = put(out, jnp.concatenate([zero, value[:part]], 0), 8 * p, side)
            out = put(out, jnp.concatenate([value[rows - part :], zero], 0), 8 * p + LOWER, side)
        warm = zero
        for l in range(layers):
            for k in range(cell_rows // SUB):
                value = w_ref[l, k * SUB : (k + 1) * SUB, cell_tile]
                warm = put(warm, value, 16 * (k + 1) + REACH * l, side)
        sides.append(jnp.concatenate([out, warm], axis=0))
    even, _, _ = place("col")
    pick = uniform(even, sides[0].shape)
    e_ref[...] = jnp.where(pick, sides[1], sides[0])
    o_ref[...] = jnp.where(pick, sides[0], sides[1])


def pack_cols_kernel(re_ref, ro_ref, own_e, own_o, w_ref, e_ref, o_ref):
    cols = re_ref.shape[2]
    tall = own_e.shape[0] - SUB
    layers, cell_rows, cells = w_ref.shape
    half = 2 * layers
    final = 16 * (cell_rows // SUB + 1)
    even, _, _ = place("col")
    pick = uniform(even, (SUB, LANE))
    zero = jnp.zeros((SUB, LANE), jnp.float32)
    parts = []
    for side in range(2):
        tile, cell_tile = end_tiles(cols)[side], end_tiles(cells)[side]
        above = below = warm = zero
        for p in range(2 * half - 1):
            top, bot = row_margin(re_ref, ro_ref, p, tile, half)
            above = put(above, top, 8 * p, side)
            below = put(below, bot, 8 * p + LOWER, side)
        for l in range(layers):
            at = slice(l * cells + cell_tile.start, l * cells + cell_tile.stop)
            top, bot = row_margin(re_ref, ro_ref, 2 * half - 1, at, half)
            warm = put(put(warm, top, REACH * l, side), bot, final + REACH * l, side)
        parts.append((above, below, warm))
    lane = iota((SUB, LANE), 1)
    low = lane % 8 < REACH
    ends = (lane < 16) | ((lane >= final) & (lane < final + 16))
    for ref, own, first in ((e_ref, own_e, 1), (o_ref, own_o, 0)):
        above, below, warm = (jnp.where(pick, a, b) for a, b in zip(parts[first], parts[1 - first]))
        ref[SUB : tall - SUB, :] = own[SUB : tall - SUB, :]
        ref[0:SUB, :] = jnp.where(low, above, own[0:SUB, :])
        ref[tall - SUB : tall, :] = jnp.where(low, own[tall - SUB : tall, :], below)
        ref[tall : tall + SUB, :] = jnp.where(ends, warm, own[tall : tall + SUB, :])


def col_sides(e, o):
    even, before, after = place("col")
    pick = uniform(even, e.shape)
    right, left = jnp.where(pick, e, o), jnp.where(pick, o, e)
    return (
        jnp.where(uniform(after, e.shape), right, 0.0),
        jnp.where(uniform(before, e.shape), left, 0.0),
    )


def turned(value, shift):
    shift = shift % LANE
    return pltpu.roll(value, shift, 1) if shift else value


def col_margin(e, o, high, back):
    even, before, after = place("col")
    lane = iota(e.shape, 1)
    pick = uniform(even, e.shape)
    right, left = jnp.where(pick, e, o), jnp.where(pick, o, e)
    right = jnp.where(uniform(after, e.shape), right, 0.0)
    left = jnp.where(uniform(before, e.shape), left, 0.0)
    own_half = lane % 8 >= REACH if high else lane % 8 < REACH
    return jnp.where(own_half, right, pltpu.roll(left, LANE - back, 1))


def margin_tile(mixed, shift):
    lane = iota(mixed.shape, 1)
    value = mixed if shift == 0 else pltpu.roll(mixed, LANE - shift, 1)
    return jnp.where((lane < REACH) | (lane >= LANE - REACH), value, 0.0)


CENTER = 0.5 * (spectrum_high + spectrum_low)
HALF = 0.5 * (spectrum_high - spectrum_low)
SIGMA = CENTER / HALF


def sweep_gains():
    rho, gains = 1.0 / SIGMA, []
    for _ in range(SWEEPS - 1):
        rho_new = 1.0 / (2.0 * SIGMA - rho)
        gains.append((rho_new * rho, 2.0 * rho_new / HALF))
        rho = rho_new
    return gains


def tile_rows(i):
    return pl.ds(pl.multiple_of(i * SUB, SUB), SUB)


def each(first, last, unroll, body):
    if unroll >= last - first:
        for i in range(first, last):
            body(i)
    else:
        lax.fori_loop(first, last, lambda i, c: (body(i), c)[1], 0, unroll=unroll)


def before(i):
    return max(i - 1, 0) if isinstance(i, int) else jnp.maximum(i - 1, 0)


def after(i, groups):
    return min(i + 1, groups - 1) if isinstance(i, int) else jnp.minimum(i + 1, groups - 1)


def shifted_down(here, nxt):
    return jnp.where(
        iota(here.shape, 0) == SUB - 1, pltpu.roll(nxt, SUB - 1, 0), pltpu.roll(here, SUB - 1, 0)
    )


def shifted_up(prev, here):
    return jnp.where(iota(here.shape, 0) == 0, pltpu.roll(prev, 1, 0), pltpu.roll(here, 1, 0))


def around(ref, l, i, groups):
    here = ref[l, tile_rows(i), :]
    width = here.shape[1]
    up = shifted_up(ref[l, tile_rows(before(i)), :], here)
    down = shifted_down(here, ref[l, tile_rows(after(i, groups)), :])
    return up, down, pltpu.roll(here, 1, 1), pltpu.roll(here, width - 1, 1)


def added(four):
    return (four[0] + four[1]) + (four[2] + four[3])


def upright(l, xs, vs):
    layers = len(xs)
    if l == 0:
        return vs[0] * xs[1]
    if l == layers - 1:
        return vs[l - 1] * xs[l - 1]
    return vs[l] * xs[l + 1] + vs[l - 1] * xs[l - 1]


def load_vias(V, r):
    return [V[l, r, :].astype(jnp.float32) for l in range(V.shape[0])]


def first_sweep(unroll, skip, X, G, J, V, W0, XN, WN, D, DI, GD, JD, EH, EV):
    layers, height, _ = X.shape
    groups = height // SUB

    def start(i):
        r = tile_rows(i)
        for l in range(layers):
            W0[l, r, :] = G[l, r, :] * X[l, r, :]

    each(0, groups, unroll, start)

    def body(i):
        r = tile_rows(i)
        xs = [X[l, r, :] for l in range(layers)]
        vs = load_vias(V, r)
        for l in range(layers):
            g = G[l, r, :]
            four = around(G, l, i, groups)
            diag = leak_cond + g * added(four)
            EV[l, r, :] = g * four[1]
            EH[l, r, :] = g * four[3]
            if l < layers - 1:
                diag = diag + vs[l]
            if l > 0:
                diag = diag + vs[l - 1]
            inverse = 1.0 / diag
            gd, jd = g * inverse, J[l, r, :] * inverse
            near = added(around(W0, l, i, groups))
            d = (jd + gd * near + inverse * upright(l, xs, vs) - xs[l]) / CENTER
            x = xs[l] + d
            DI[l, r, :], GD[l, r, :], JD[l, r, :], D[l, r, :] = inverse, gd, jd, d
            XN[l, r, :] = x
            WN[l, r, :] = g * x

    each(skip, groups - skip, unroll, body)


def next_sweep(unroll, skip, keep, gain, X, V, W, D, DI, GD, JD, G, XN, WN=None, DN=None):
    layers, height, _ = X.shape
    groups = height // SUB

    def body(i):
        r = tile_rows(i)
        xs = [X[l, r, :] for l in range(layers)]
        vs = load_vias(V, r)
        for l in range(layers):
            near = added(around(W, l, i, groups))
            resid = (
                JD[l, r, :] + GD[l, r, :] * near + DI[l, r, :] * upright(l, xs, vs) - xs[l]
            )
            d = keep * D[l, r, :] + gain * resid
            x = xs[l] + d
            XN[l, r, :] = x
            if WN is not None:
                DN[l, r, :] = d
                WN[l, r, :] = G[l, r, :] * x

    each(skip, groups - skip, unroll, body)


def later_sweeps(unroll, X, V, W, D, DI, GD, JD, G, WN, XN, DN):
    gains = sweep_gains()
    x, w, d, other = X, W, D, WN
    for at, (keep, gain) in enumerate(gains):
        if at == len(gains) - 1:
            next_sweep(unroll, 0, keep, gain, x, V, w, d, DI, GD, JD, G, XN)
        else:
            next_sweep(unroll, 0, keep, gain, x, V, w, d, DI, GD, JD, G, XN, other, DN)
            assert len(gains) <= 2
            x, w, d = XN, other, DN


def power_rows(first, last, unroll, X, V, EH, EV, PA, PB, PD):
    layers, height, width = X.shape
    groups = height // SUB
    share = jnp.where(iota((SUB, width), 0) % REFINE == REFINE - 1, 0.5, 1.0)
    lane_share = jnp.where(iota((SUB, width), 1) % REFINE == REFINE - 1, 1.0, 2.0)

    def fold(v):
        v = v + pltpu.roll(v, SUB - 1, 0)
        return v + pltpu.roll(v, SUB - 2, 0)

    def body(i):
        r = tile_rows(i)
        out = tile_rows(i + 1)
        xs = [X[l, r, :] for l in range(layers)]
        vs = load_vias(V, r)
        drops = [0.5 * vs[l] * (xs[l] - xs[l + 1]) ** 2 for l in range(layers - 1)]
        for l in range(layers):
            x = xs[l]
            across = x - pltpu.roll(x, width - 1, 1)
            down = x - shifted_down(x, X[l, tile_rows(after(i, groups)), :])
            across = 0.5 * EH[l, r, :] * (across * across)
            down = EV[l, r, :] * (down * down)
            total = leak_cond * (x * x) + share * down + lane_share * across
            if l < layers - 1:
                total = total + drops[l]
            if l > 0:
                total = total + drops[l - 1]
            total, across = fold(total), fold(across)
            for t in range(width // LANE):
                tile = slice(t * LANE, (t + 1) * LANE)
                PA[l, t, out, :] = total[:, tile]
                PB[l, t, out, :] = across[:, tile]
                PD[l, t, out, :] = down[:, tile]

    each(first, last, unroll, body)


def fold_power(row, cells, PA, PB, PD, same, left):
    layers = PA.shape[0]
    at = pl.ds(row + SUB, cells, stride=REFINE)
    up = pl.ds(row + SUB - 1, cells, stride=REFINE)
    tiles = range(PA.shape[1])
    a = [
        jnp.concatenate([PA[l, t, at, :] + 0.5 * PD[l, t, up, :] for t in tiles], 1)
        for l in range(layers)
    ]
    b = [jnp.concatenate([PB[l, t, at, :] for t in tiles], 1) for l in range(layers)]
    a, b = jnp.concatenate(a, 0), jnp.concatenate(b, 0)
    heat = (dot(a, same) + dot(b, left)) * heat_gain
    return [heat[l * cells : (l + 1) * cells] for l in range(layers)]


def fold_matrices(nodes, cells):
    n, c = iota((nodes, cells), 0), iota((nodes, cells), 1)
    same = lax.shift_right_logical(n, 2) == c
    return same.astype(jnp.float32), (n == REFINE * c - 1).astype(jnp.float32)


def bulk_first_kernel(
    x_ref, b_ref, w_ref, v_ref, f_ref, a_ref,
    g_ref, j_ref, XN, WN, D, DI, GD, JD, EH, EV, own_e, own_o,
    W0,
):
    layers, rows, cols = x_ref.shape
    _, cell_rows, cells = w_ref.shape
    spread_rows = gather_lanes(rows, cell_rows)
    spread = spread_lanes(cells, cols)
    for l in range(layers):
        warm = jnp.exp(-0.5 * warmth_sensitivity * w_ref[l])
        g_ref[l] = jnp.sqrt(b_ref[l]) * dot(spread_rows, dot(warm, spread))
        j_ref[l] = f_ref[l].astype(jnp.float32) * a_ref[l]
    pack_own_columns((x_ref, g_ref, j_ref, v_ref), w_ref, own_e, own_o)
    first_sweep(2, 1, x_ref, g_ref, j_ref, v_ref, W0, XN, WN, D, DI, GD, JD, EH, EV)


def bulk_mid_kernel(X, V, W, D, DI, GD, JD, G, XL, WN, XN, DN):
    (keep, gain), (keep_last, gain_last) = sweep_gains()
    next_sweep(2, 1, keep, gain, X, V, W, D, DI, GD, JD, G, XN, WN, DN)
    next_sweep(2, 1, keep_last, gain_last, XN, V, WN, DN, DI, GD, JD, G, XL)


def bulk_last_kernel(
    XN, V, EH, EV, xr_ref, xc_ref,
    x_hbm, h_ref,
    PA, PB, PD, out, sem,
):
    layers, rows, cols = XN.shape
    cell_rows, cells = h_ref.shape[1:]
    groups = rows // SUB
    lane = iota((rows, LANE), 1)
    low = iota((SUB, LANE), 0) < REACH
    for l in range(layers):
        for t in range(cols // LANE):
            tile = slice(t * LANE, (t + 1) * LANE)
            x = jnp.concatenate(
                [
                    xr_ref[l, 0:SUB, tile],
                    jnp.where(low, xr_ref[l, SUB : 2 * SUB, tile], XN[l, SUB : 2 * SUB, tile]),
                    XN[l, 2 * SUB : rows - 2 * SUB, tile],
                    jnp.where(
                        low,
                        XN[l, rows - 2 * SUB : rows - SUB, tile],
                        xr_ref[l, 2 * SUB : 3 * SUB, tile],
                    ),
                    xr_ref[l, 3 * SUB : 4 * SUB, tile],
                ],
                0,
            )
            if t == 0:
                x = jnp.where(lane < SUB, xc_ref[l], x)
            if t == cols // LANE - 1:
                x = jnp.where(lane >= LANE - SUB, xc_ref[l], x)
            out[l, :, tile] = x
    copy = pltpu.make_async_copy(out, x_hbm, sem)
    copy.start()
    power_rows(1, groups - 1, 2, XN, V, EH, EV, PA, PB, PD)
    heat = fold_power(0, cell_rows, PA, PB, PD, *fold_matrices(cols, cells))
    for l in range(layers):
        h_ref[l] = heat[l]
    copy.wait()


def row_strip_kernel(
    x_t, x_b, g_t, g_b, j_t, j_b, v_t, v_b,
    x_l, x_r, g_l, g_r, j_l, j_r, v_l, v_r,
    re_ref, ro_ref,
    xr_ref, h_ref, strip_ref,
    X, G, J, V, W0, XN, WN, D, DI, GD, JD, EH, EV, PA, PB, PD, DN, XL,
):
    layers, deep, cols = x_t.shape
    rows = x_l.shape[1]
    cells = h_ref.shape[2]
    half = 2 * layers
    height = 2 * (SUB + deep)
    plane = 0
    tall = strip_ref.shape[1]
    lane = iota((tall, LANE), 1)
    for top_ref, bot_ref, left_ref, right_ref, pad in (
        (x_t, x_b, x_l, x_r, X), (g_t, g_b, g_l, g_r, G), (j_t, j_b, j_l, j_r, J), (v_t, v_b, v_l, v_r, V),
    ):
        for l in range(top_ref.shape[0]):
            top, bot = row_margin(re_ref, ro_ref, plane, slice(0, cols), half)
            pad[l, 0:SUB, :] = top
            pad[l, SUB : SUB + deep, :] = top_ref[l].astype(jnp.float32)
            pad[l, SUB + deep : SUB + 2 * deep, :] = bot_ref[l].astype(jnp.float32)
            pad[l, SUB + 2 * deep : height, :] = bot
            left = jnp.concatenate([top[:, :LANE], left_ref[l].astype(jnp.float32), bot[:, :LANE]], 0)
            right = jnp.concatenate(
                [top[:, cols - LANE :], right_ref[l].astype(jnp.float32), bot[:, cols - LANE :]], 0
            )
            strip_ref[plane] = jnp.where(
                lane < LANE // 2,
                jnp.where(lane < LANE // 4, left[:tall], pltpu.roll(right[:tall], 48, 1)),
                jnp.where(
                    lane < 3 * LANE // 4,
                    pltpu.roll(left[rows + 2 * SUB - tall :], LOWER, 1),
                    pltpu.roll(right[rows + 2 * SUB - tall :], 48 + LOWER, 1),
                ),
            )
            plane += 1
    first_sweep(6, 0, X, G, J, V, W0, XN, WN, D, DI, GD, JD, EH, EV)
    later_sweeps(6, XN, V, WN, D, DI, GD, JD, G, W0, XL, DN)
    groups = height // SUB
    power_rows(0, groups - 1, 6, XL, V, EH, EV, PA, PB, PD)
    heat = fold_power(SUB, 2 * SUB // 2, PA, PB, PD, *fold_matrices(cols, cells))
    for l in range(layers):
        h_ref[l] = heat[l]
        xr_ref[l] = XL[l, SUB : height - SUB, :]


def col_strip_kernel(
    strip_ref, ce_ref, co_ref, hr_ref,
    xc_ref, hc_ref, hm_ref,
    X, G, J, V, W0, XN, WN, D, DI, GD, JD, EH, EV, PA, PB, PD, DN, XL,
):
    layers, rows, _ = xc_ref.shape
    cell_rows, cells = hc_ref.shape[1:]
    tall = strip_ref.shape[1]
    right, left = col_sides(ce_ref[0:tall, :], co_ref[0:tall, :])
    lane = iota((tall, LANE), 1)
    in_right = ((lane >= 48) & (lane < 48 + REACH)) | ((lane >= 48 + LOWER) & (lane < 48 + LOWER + REACH))
    in_left = (lane >= LANE - REACH) | ((lane >= LOWER - REACH) & (lane < LOWER))
    plane = 0
    for pad in (X, G, J, V):
        for l in range(pad.shape[0]):
            value = jnp.where(in_right, turned(right, 48 - 8 * plane), strip_ref[plane])
            pad[l] = jnp.where(in_left, turned(left, LANE - REACH - 8 * plane), value)
            plane += 1
    groups = tall // SUB
    first_sweep(groups, 0, X, G, J, V, W0, XN, WN, D, DI, GD, JD, EH, EV)
    later_sweeps(groups, XN, V, WN, D, DI, GD, JD, G, W0, XL, DN)
    power_rows(0, groups - 1, groups, XL, V, EH, EV, PA, PB, PD)
    n, c = iota((LANE, cells), 0), iota((LANE, cells), 1)
    at_edge = (c < REACH) | (c >= cells - REACH)
    halves = []
    for part in range(2):
        slot = jnp.where(c < cells // 2, c, c - cells + 12) + LOWER // REFINE * part
        same = at_edge & (lax.shift_right_logical(n, 2) == slot)
        left = at_edge & (n == jnp.where(slot == 0, LANE - 1, REFINE * slot - 1))
        halves.append(
            fold_power(
                SUB, cell_rows // 2, PA, PB, PD, same.astype(jnp.float32), left.astype(jnp.float32)
            )
        )
    lane = iota((rows // 2, LANE), 1)
    cell = iota((SUB, cells), 1)
    edge = (cell < REACH - 1) | (cell > cells - REACH)
    low = lane < LANE // 2
    for l in range(layers):
        first, final = halves[0][l], halves[1][l]
        hc_ref[l, 0 : cell_rows // 2, :] = first
        hc_ref[l, cell_rows // 2 : cell_rows, :] = final
        x = XL[l, SUB : SUB + rows // 2, :]
        xc_ref[l, 0 : rows // 2, :] = jnp.where(low, x, pltpu.roll(x, 80, 1))
        xc_ref[l, rows // 2 : rows, :] = jnp.where(low, turned(x, -LOWER), turned(x, 80 - LOWER))
        own = jnp.concatenate([first[:REACH], final[cell_rows // 2 - REACH :]], 0)
        hm_ref[l] = jnp.where(edge, own, hr_ref[l])


def heat_rows(own, e_ref, o_ref, l):
    even, above, below = place("row")
    e, o = e_ref[l], o_ref[l]
    pick = uniform(even, e.shape)
    top = jnp.where(uniform(above, e.shape), jnp.where(pick, o, e), 0.0)
    bot = jnp.where(uniform(below, e.shape), jnp.where(pick, e, o), 0.0)
    return jnp.concatenate([top, own, bot], axis=0)


def pack_heat_kernel(h_ref, re_ref, ro_ref, _, e_ref, o_ref):
    layers, cell_rows, cells = h_ref.shape
    height = cell_rows + 2 * SUB
    even, _, _ = place("col")
    lane = iota((height, LANE), 1)
    slot, low = lax.shift_right_logical(lane, 3), lane % 8 < REACH
    left = right = jnp.zeros((height, LANE), jnp.float32)
    for l in range(layers):
        value = heat_rows(h_ref[l], re_ref, ro_ref, l)
        mine = (slot == l) & low
        left = jnp.where(mine, pltpu.roll(value[:, :LANE], 8 * l, 1) if l else value[:, :LANE], left)
        right = jnp.where(mine, pltpu.roll(value[:, cells - LANE :], 8 * l + REACH, 1), right)
    pick = uniform(even, (height, LANE))
    e_ref[...] = jnp.where(pick, right, left)
    o_ref[...] = jnp.where(pick, left, right)


def warm_kernel(
    w_ref, h_ref, hm_ref, hc_ref, re_ref, ro_ref, ce_ref, co_ref,
    hre_ref, hro_ref, hce_ref, hco_ref, out_ref,
):
    layers, cell_rows, cells = w_ref.shape
    half = 2 * layers
    height, width = cell_rows + 2 * SUB, cells + LANE
    tall = ce_ref.shape[0]
    right, left = col_sides(ce_ref[tall - SUB : tall, :], co_ref[tall - SUB : tall, :])
    lane = iota((SUB, LANE), 1)
    heat_mixed = col_margin(hce_ref[...], hco_ref[...], False, REACH)
    cell = iota((cell_rows, cells), 1)
    edge = (cell < REACH - 1) | (cell > cells - REACH)
    cell_row = iota((SUB, cells), 0)
    theta, heat = [], []
    for l in range(layers):
        top, bot = row_margin(
            re_ref, ro_ref, 2 * half - 1, slice(l * cells, (l + 1) * cells), half
        )
        own = jnp.concatenate([top, w_ref[l], bot], axis=0)
        pieces = []
        for k in range(height // SUB):
            at = 16 * k + REACH * l
            value = jnp.where(lane < REACH, turned(right, -at), 0.0)
            pieces.append(jnp.where(lane >= LANE - REACH, turned(left, -REACH - at), value))
        theta.append(jnp.concatenate([own, jnp.concatenate(pieces, axis=0)], axis=1))
        own = jnp.where(edge, hc_ref[l], h_ref[l])
        first, final = own[:SUB], own[cell_rows - SUB :]
        first = jnp.where(cell_row < REACH - 1, hm_ref[l], first)
        final = jnp.where(cell_row > SUB - REACH, hm_ref[l], final)
        own = jnp.concatenate([first, own[SUB : cell_rows - SUB], final], axis=0)
        own = heat_rows(own, hre_ref, hro_ref, l)
        heat.append(jnp.concatenate([own, margin_tile(heat_mixed, 8 * l)], axis=1))
    _, above, below = place("row")
    _, before, after = place("col")
    shape = (height, width)
    r, c = iota(shape, 0), iota(shape, 1)
    inside = (uniform(above, shape) | (r >= SUB)) & (uniform(below, shape) | (r < height - SUB))
    inside = inside & (uniform(after, shape) | (c < cells) | (c >= cells + LANE // 2))
    inside = inside & (uniform(before, shape) | (c < cells + LANE // 2))

    def around_cells(v):
        return (pltpu.roll(v, 1, 0) + pltpu.roll(v, height - 1, 0)) + (
            pltpu.roll(v, 1, 1) + pltpu.roll(v, width - 1, 1)
        )

    for _ in range(HEAT_SWEEPS):
        later = []
        for l in range(layers):
            t = theta[l]
            q = jnp.where(inside, jnp.exp(-0.5 * warming_weight * t), 0.0)
            change = q * (around_cells(q * t) - t * around_cells(q)) + heat[l]
            if l < layers - 1:
                change = change + (theta[l + 1] - t)
            if l > 0:
                change = change + (theta[l - 1] - t)
            if l == layers - 1:
                change = change - t
            later.append(t + interval_length * change)
        theta = later
    for l in range(layers):
        out_ref[l] = theta[l][SUB : SUB + cell_rows, :cells]


def on_device(x, base, warm, via, feeder, amps):
    layers, rows, cols = x.shape
    _, cell_rows, cells = warm.shape
    f32 = jnp.float32
    mesh_rows, mesh_cols = lax.axis_size("row"), lax.axis_size("col")
    last_row, last_cell_row, last_col = rows // SUB - 1, cell_rows // SUB - 1, cols // LANE - 1

    def shape(*dims):
        return jax.ShapeDtypeStruct(dims, f32)

    def edge_rows(a, at):
        return pl.BlockSpec((a.shape[0], SUB, a.shape[2]), lambda _, at=at: (0, at, 0))

    def edge_cols(a, at):
        return pl.BlockSpec((a.shape[0], a.shape[1], LANE), lambda _, at=at: (0, 0, at))

    def full(a):
        return pl.BlockSpec(a.shape, lambda _, n=len(a.shape): (0,) * n)

    def swap(e, o, tables):
        return tuple(
            lax.ppermute(m, BOTH, tables(mesh_rows, mesh_cols, first)) for first, m in enumerate((e, o))
        )

    params = pltpu.CompilerParams(vmem_limit_bytes=24 * 1024 * 1024)
    row_args, row_specs = [], []
    for a in (x, base, warm, via, feeder, amps):
        end = last_cell_row if a is warm else last_row
        row_args += [a, a]
        row_specs += [edge_rows(a, 0), edge_rows(a, end)]
    message = shape(2 * layers, SUB, cols)
    e, o = pl.pallas_call(
        pack_rows_kernel,
        grid=(1,),
        in_specs=row_specs,
        out_specs=(full(message), full(message)),
        out_shape=(message, message),
        compiler_params=pltpu.CompilerParams(vmem_limit_bytes=58 * 1024 * 1024),
        name="pack_rows",
    )(*row_args)
    row_e, row_o = swap(e, o, row_swaps)

    fields = (shape(layers, rows, cols),) * 10 + (shape(rows // 2 + 3 * SUB, LANE),) * 2
    node_scratch = pltpu.VMEM((layers, rows, cols), f32)
    g, inject, *mid = pl.pallas_call(
        bulk_first_kernel,
        out_shape=fields,
        scratch_shapes=[node_scratch],
        compiler_params=params,
        name="bulk_first",
        cost_estimate=pl.CostEstimate(flops=40 * x.size, bytes_accessed=60 * x.size, transcendentals=0),
    )(x, base, warm, via, feeder, amps)
    x_mid, w_mid, d_mid, inv_diag, g_diag, j_diag, edge_h, edge_v, own_e, own_o = mid

    col_args, col_specs = [], []
    for a in (x, g, inject, via):
        col_args += [a, a]
        col_specs += [edge_cols(a, 0), edge_cols(a, last_col)]
    message = shape(rows // 2 + 3 * SUB, LANE)
    e, o = pl.pallas_call(
        pack_cols_kernel,
        out_shape=(message, message),
        compiler_params=params,
        name="pack_cols",
    )(row_e, row_o, own_e, own_o, warm)
    col_e, col_o = swap(e, o, col_swaps)

    def strip_scratch(height, width):
        node = pltpu.VMEM((layers, height, width), f32)
        taller = pltpu.VMEM((layers, width // LANE, height + SUB, LANE), f32)
        return [node] * 3 + [pltpu.VMEM((layers - 1, height, width), f32)] + [node] * 9 + [taller] * 3 + [node] * 2

    def edge_deep(a, at):
        return pl.BlockSpec((a.shape[0], 2 * SUB, a.shape[2]), lambda _, at=at: (0, at, 0))

    deep_args, deep_specs = [], []
    for a in (x, g, inject, via):
        deep_args += [a, a]
        deep_specs += [edge_deep(a, 0), edge_deep(a, rows // (2 * SUB) - 1)]
    edge_x, edge_h2 = shape(layers, 4 * SUB, cols), shape(layers, SUB, cells)
    strip = shape(4 * layers - 1, rows // 2 + 2 * SUB, LANE)
    x_rows, heat_strip, strip = pl.pallas_call(
        row_strip_kernel,
        grid=(1,),
        in_specs=deep_specs + col_specs + [full(row_e), full(row_o)],
        out_specs=(full(edge_x), full(edge_h2), full(strip)),
        out_shape=(edge_x, edge_h2, strip),
        scratch_shapes=strip_scratch(6 * SUB, cols),
        compiler_params=params,
        name="row_strip",
        cost_estimate=pl.CostEstimate(flops=40 * x.size, bytes_accessed=20 * x.size, transcendentals=0),
    )(*deep_args, *col_args, row_e, row_o)

    x_cols, heat_cols, heat_edge = pl.pallas_call(
        col_strip_kernel,
        out_shape=(shape(layers, rows, LANE), shape(layers, cell_rows, cells), edge_h2),
        scratch_shapes=strip_scratch(rows // 2 + 2 * SUB, LANE),
        compiler_params=params,
        name="col_strip",
    )(strip, col_e, col_o, heat_strip)
    heat_row_e, heat_row_o = swap(heat_edge, heat_edge, row_swaps)

    assert SWEEPS == 3
    x_done = pl.pallas_call(
        bulk_mid_kernel,
        out_shape=shape(layers, rows, cols),
        scratch_shapes=[node_scratch] * 3,
        compiler_params=params,
        name="bulk_mid",
        cost_estimate=pl.CostEstimate(flops=20 * x.size, bytes_accessed=20 * x.size, transcendentals=0),
    )(x_mid, via, w_mid, d_mid, inv_diag, g_diag, j_diag, g)

    message = shape(cell_rows + 2 * SUB, LANE)
    e, o = pl.pallas_call(
        pack_heat_kernel,
        in_specs=[pl.BlockSpec(memory_space=pltpu.VMEM)] * 3 + [pl.BlockSpec(memory_space=pl.ANY)],
        out_shape=(message, message),
        compiler_params=params,
        name="pack_heat",
    )(heat_cols, heat_row_e, heat_row_o, x_done)
    heat_col_e, heat_col_o = swap(e, o, col_swaps)

    tall = pltpu.VMEM((layers, cols // LANE, rows + SUB, LANE), f32)
    voltage, heat = pl.pallas_call(
        bulk_last_kernel,
        out_shape=(shape(layers, rows, cols), shape(layers, cell_rows, cells)),
        out_specs=(pl.BlockSpec(memory_space=pl.ANY), pl.BlockSpec(memory_space=pltpu.VMEM)),
        scratch_shapes=[tall] * 3 + [node_scratch, pltpu.SemaphoreType.DMA],
        compiler_params=params,
        name="bulk_last",
        cost_estimate=pl.CostEstimate(flops=40 * x.size, bytes_accessed=60 * x.size, transcendentals=0),
    )(x_done, via, edge_h, edge_v, x_rows, x_cols)

    warmth = pl.pallas_call(
        warm_kernel,
        out_shape=shape(layers, cell_rows, cells),
        compiler_params=params,
        name="warm",
    )(warm, heat, heat_edge, heat_cols, row_e, row_o, col_e, col_o, heat_row_e, heat_row_o, heat_col_e, heat_col_o)
    return voltage, warmth


def solution(mesh):
    placed = P(None, "row", "col")
    return jax.shard_map(
        on_device,
        mesh=mesh,
        in_specs=(placed,) * 6,
        out_specs=(placed, placed),
        check_vma=False,
    )
```

```python
import jax
import jax.numpy as jnp
from jax import lax
from jax.experimental import pallas as pl
from jax.experimental.pallas import tpu as pltpu
from jax.sharding import PartitionSpec as P

REFINE = 4
SWEEPS = 3
HEAT_SWEEPS = 4

warmth_sensitivity = 0.5
leak_cond = 0.2
spectrum_low = 0.05
spectrum_high = 1.95
warming_weight = 0.3
heat_gain = 0.0625
interval_length = 0.12

SUB = 8
LANE = 128
REACH = 4
BOTH = ("row", "col")
HIGHEST = lax.Precision.HIGHEST


def row_swaps(rows, cols, first):
    pairs = []
    for r in range(rows):
        for c in range(cols):
            p = r + 1 if (r - first) % 2 == 0 else r - 1
            if 0 <= p < rows:
                pairs.append((r * cols + c, p * cols + c))
            elif c ^ 1 < cols:
                pairs.append((r * cols + c, r * cols + (c ^ 1)))
    return pairs


def col_swaps(rows, cols, first):
    pairs = []
    for r in range(rows):
        for c in range(cols):
            p = c + 1 if (c - first) % 2 == 0 else c - 1
            if 0 <= p < cols:
                pairs.append((r * cols + c, r * cols + p))
            elif r ^ 1 < rows:
                pairs.append((r * cols + c, (r ^ 1) * cols + c))
    return pairs


def iota(shape, dim):
    return lax.broadcasted_iota(jnp.int32, shape, dim)


def uniform(flag, shape):
    return jnp.full(shape, flag.astype(jnp.int32), jnp.int32) == 1


def place(axis):
    at = lax.axis_index(axis)
    return at % 2 == 0, at > 0, at < lax.axis_size(axis) - 1


def dot(a, b):
    return jnp.dot(a, b, precision=HIGHEST, preferred_element_type=jnp.float32)


def spread_lanes(cells, nodes):
    same = lax.shift_right_logical(iota((cells, nodes), 1), 2) == iota((cells, nodes), 0)
    return same.astype(jnp.float32)


def gather_lanes(nodes, cells):
    same = lax.shift_right_logical(iota((nodes, cells), 0), 2) == iota((nodes, cells), 1)
    return same.astype(jnp.float32)


def pack_rows_kernel(x_t, x_b, b_t, b_b, w_t, w_b, v_t, v_b, f_t, f_b, a_t, a_b, e_ref, o_ref):
    layers, _, cols = x_t.shape
    cells = w_t.shape[2]
    even, _, _ = place("row")
    low = iota((SUB, cols), 0) < REACH
    spread = spread_lanes(cells, cols)

    def planes(x, b, w, v, f, a, cell_row):
        warm = jnp.concatenate([w[l, cell_row : cell_row + 1, :] for l in range(layers)] * 2, 0)
        warm = dot(jnp.exp(-0.5 * warmth_sensitivity * warm), spread)
        xs = [x[l] for l in range(layers)]
        gs = [jnp.sqrt(b[l]) * warm[l : l + 1] for l in range(layers)]
        js = [f[l].astype(jnp.float32) * a[l] for l in range(layers)]
        vs = [v[l].astype(jnp.float32) for l in range(layers - 1)]
        ws = [jnp.concatenate([w[l] for l in range(layers)], axis=1)]
        return xs + gs, js + vs + ws

    top_a, top_b = planes(x_t, b_t, w_t, v_t, f_t, a_t, 0)
    bot_a, bot_b = planes(x_b, b_b, w_b, v_b, f_b, a_b, SUB - 1)
    pick = uniform(even, (SUB, cols))
    for k in range(2 * layers):
        top = jnp.where(low, top_a[k], pltpu.roll(top_b[k], REACH, 0))
        bot = jnp.where(low, pltpu.roll(bot_a[k], REACH, 0), bot_b[k])
        e_ref[k] = jnp.where(pick, bot, top)
        o_ref[k] = jnp.where(pick, top, bot)


def row_margin(e_ref, o_ref, plane, cols, half):
    even, above, below = place("row")
    k = plane % half
    e, o = e_ref[k, :, cols], o_ref[k, :, cols]
    pick = uniform(even, e.shape)
    top, bot = jnp.where(pick, o, e), jnp.where(pick, e, o)
    if plane < half:
        top = pltpu.roll(top, REACH, 0)
    else:
        bot = pltpu.roll(bot, REACH, 0)
    return (
        jnp.where(uniform(above, top.shape), top, 0.0),
        jnp.where(uniform(below, bot.shape), bot, 0.0),
    )


def put(out, value, at, side):
    at = at % LANE
    shift = (at + REACH * side) % LANE
    lane, value = iota(out.shape, 1), value.astype(jnp.float32)
    value = pltpu.roll(value, shift, 1) if shift else value
    return jnp.where((lane >= at) & (lane < at + REACH), value, out)


def end_tiles(width):
    return slice(0, LANE), slice(width - LANE, width)


LOWER = LANE // 2 + REACH


def pack_own_columns(fields, w_ref, e_ref, o_ref):
    rows, cols = fields[0].shape[1:]
    layers, cell_rows, cells = w_ref.shape
    part = rows // 2 + SUB
    zero = jnp.zeros((SUB, LANE), jnp.float32)
    sides = []
    for side in range(2):
        tile, cell_tile = end_tiles(cols)[side], end_tiles(cells)[side]
        values = [ref[l, :, tile] for ref in fields for l in range(ref.shape[0])]
        out = jnp.zeros((part + SUB, LANE), jnp.float32)
        for p, value in enumerate(values):
            value = value.astype(jnp.float32)
            out = put(out, jnp.concatenate([zero, value[:part]], 0), 8 * p, side)
            out = put(out, jnp.concatenate([value[rows - part :], zero], 0), 8 * p + LOWER, side)
        warm = zero
        for l in range(layers):
            for k in range(cell_rows // SUB):
                value = w_ref[l, k * SUB : (k + 1) * SUB, cell_tile]
                warm = put(warm, value, 16 * (k + 1) + REACH * l, side)
        sides.append(jnp.concatenate([out, warm], axis=0))
    even, _, _ = place("col")
    pick = uniform(even, sides[0].shape)
    e_ref[...] = jnp.where(pick, sides[1], sides[0])
    o_ref[...] = jnp.where(pick, sides[0], sides[1])


def pack_cols_kernel(re_ref, ro_ref, own_e, own_o, w_ref, e_ref, o_ref):
    cols = re_ref.shape[2]
    tall = own_e.shape[0] - SUB
    layers, cell_rows, cells = w_ref.shape
    half = 2 * layers
    final = 16 * (cell_rows // SUB + 1)
    even, _, _ = place("col")
    pick = uniform(even, (SUB, LANE))
    zero = jnp.zeros((SUB, LANE), jnp.float32)
    parts = []
    for side in range(2):
        tile, cell_tile = end_tiles(cols)[side], end_tiles(cells)[side]
        above = below = warm = zero
        for p in range(2 * half - 1):
            top, bot = row_margin(re_ref, ro_ref, p, tile, half)
            above = put(above, top, 8 * p, side)
            below = put(below, bot, 8 * p + LOWER, side)
        for l in range(layers):
            at = slice(l * cells + cell_tile.start, l * cells + cell_tile.stop)
            top, bot = row_margin(re_ref, ro_ref, 2 * half - 1, at, half)
            warm = put(put(warm, top, REACH * l, side), bot, final + REACH * l, side)
        parts.append((above, below, warm))
    lane = iota((SUB, LANE), 1)
    low = lane % 8 < REACH
    ends = (lane < 16) | ((lane >= final) & (lane < final + 16))
    for ref, own, first in ((e_ref, own_e, 1), (o_ref, own_o, 0)):
        above, below, warm = (jnp.where(pick, a, b) for a, b in zip(parts[first], parts[1 - first]))
        ref[SUB : tall - SUB, :] = own[SUB : tall - SUB, :]
        ref[0:SUB, :] = jnp.where(low, above, own[0:SUB, :])
        ref[tall - SUB : tall, :] = jnp.where(low, own[tall - SUB : tall, :], below)
        ref[tall : tall + SUB, :] = jnp.where(ends, warm, own[tall : tall + SUB, :])


def col_sides(e, o):
    even, before, after = place("col")
    pick = uniform(even, e.shape)
    right, left = jnp.where(pick, e, o), jnp.where(pick, o, e)
    return (
        jnp.where(uniform(after, e.shape), right, 0.0),
        jnp.where(uniform(before, e.shape), left, 0.0),
    )


def turned(value, shift):
    shift = shift % LANE
    return pltpu.roll(value, shift, 1) if shift else value


def col_margin(e, o, high, back):
    even, before, after = place("col")
    lane = iota(e.shape, 1)
    pick = uniform(even, e.shape)
    right, left = jnp.where(pick, e, o), jnp.where(pick, o, e)
    right = jnp.where(uniform(after, e.shape), right, 0.0)
    left = jnp.where(uniform(before, e.shape), left, 0.0)
    own_half = lane % 8 >= REACH if high else lane % 8 < REACH
    return jnp.where(own_half, right, pltpu.roll(left, LANE - back, 1))


def margin_tile(mixed, shift):
    lane = iota(mixed.shape, 1)
    value = mixed if shift == 0 else pltpu.roll(mixed, LANE - shift, 1)
    return jnp.where((lane < REACH) | (lane >= LANE - REACH), value, 0.0)


CENTER = 0.5 * (spectrum_high + spectrum_low)
HALF = 0.5 * (spectrum_high - spectrum_low)
SIGMA = CENTER / HALF


def sweep_gains():
    rho, gains = 1.0 / SIGMA, []
    for _ in range(SWEEPS - 1):
        rho_new = 1.0 / (2.0 * SIGMA - rho)
        gains.append((rho_new * rho, 2.0 * rho_new / HALF))
        rho = rho_new
    return gains


def tile_rows(i):
    return pl.ds(pl.multiple_of(i * SUB, SUB), SUB)


def each(first, last, unroll, body):
    if unroll >= last - first:
        for i in range(first, last):
            body(i)
    else:
        lax.fori_loop(first, last, lambda i, c: (body(i), c)[1], 0, unroll=unroll)


def before(i):
    return max(i - 1, 0) if isinstance(i, int) else jnp.maximum(i - 1, 0)


def after(i, groups):
    return min(i + 1, groups - 1) if isinstance(i, int) else jnp.minimum(i + 1, groups - 1)


def shifted_down(here, nxt):
    return jnp.where(
        iota(here.shape, 0) == SUB - 1, pltpu.roll(nxt, SUB - 1, 0), pltpu.roll(here, SUB - 1, 0)
    )


def shifted_up(prev, here):
    return jnp.where(iota(here.shape, 0) == 0, pltpu.roll(prev, 1, 0), pltpu.roll(here, 1, 0))


def around(ref, l, i, groups):
    here = ref[l, tile_rows(i), :]
    width = here.shape[1]
    up = shifted_up(ref[l, tile_rows(before(i)), :], here)
    down = shifted_down(here, ref[l, tile_rows(after(i, groups)), :])
    return up, down, pltpu.roll(here, 1, 1), pltpu.roll(here, width - 1, 1)


def added(four):
    return (four[0] + four[1]) + (four[2] + four[3])


def upright(l, xs, vs):
    layers = len(xs)
    if l == 0:
        return vs[0] * xs[1]
    if l == layers - 1:
        return vs[l - 1] * xs[l - 1]
    return vs[l] * xs[l + 1] + vs[l - 1] * xs[l - 1]


def load_vias(V, r):
    return [V[l, r, :].astype(jnp.float32) for l in range(V.shape[0])]


def first_sweep(unroll, skip, X, G, J, V, W0, XN, WN, D, DI, GD, JD, EH, EV):
    layers, height, _ = X.shape
    groups = height // SUB

    def start(i):
        r = tile_rows(i)
        for l in range(layers):
            W0[l, r, :] = G[l, r, :] * X[l, r, :]

    each(0, groups, unroll, start)

    def body(i):
        r = tile_rows(i)
        xs = [X[l, r, :] for l in range(layers)]
        vs = load_vias(V, r)
        for l in range(layers):
            g = G[l, r, :]
            four = around(G, l, i, groups)
            diag = leak_cond + g * added(four)
            EV[l, r, :] = g * four[1]
            EH[l, r, :] = g * four[3]
            if l < layers - 1:
                diag = diag + vs[l]
            if l > 0:
                diag = diag + vs[l - 1]
            inverse = 1.0 / diag
            gd, jd = g * inverse, J[l, r, :] * inverse
            near = added(around(W0, l, i, groups))
            d = (jd + gd * near + inverse * upright(l, xs, vs) - xs[l]) / CENTER
            x = xs[l] + d
            DI[l, r, :], GD[l, r, :], JD[l, r, :], D[l, r, :] = inverse, gd, jd, d
            XN[l, r, :] = x
            WN[l, r, :] = g * x

    each(skip, groups - skip, unroll, body)


def next_sweep(unroll, skip, keep, gain, X, V, W, D, DI, GD, JD, G, XN, WN=None, DN=None):
    layers, height, _ = X.shape
    groups = height // SUB

    def body(i):
        r = tile_rows(i)
        xs = [X[l, r, :] for l in range(layers)]
        vs = load_vias(V, r)
        for l in range(layers):
            near = added(around(W, l, i, groups))
            resid = (
                JD[l, r, :] + GD[l, r, :] * near + DI[l, r, :] * upright(l, xs, vs) - xs[l]
            )
            d = keep * D[l, r, :] + gain * resid
            x = xs[l] + d
            XN[l, r, :] = x
            if WN is not None:
                DN[l, r, :] = d
                WN[l, r, :] = G[l, r, :] * x

    each(skip, groups - skip, unroll, body)


def later_sweeps(unroll, X, V, W, D, DI, GD, JD, G, WN, XN, DN):
    gains = sweep_gains()
    x, w, d, other = X, W, D, WN
    for at, (keep, gain) in enumerate(gains):
        if at == len(gains) - 1:
            next_sweep(unroll, 0, keep, gain, x, V, w, d, DI, GD, JD, G, XN)
        else:
            next_sweep(unroll, 0, keep, gain, x, V, w, d, DI, GD, JD, G, XN, other, DN)
            assert len(gains) <= 2
            x, w, d = XN, other, DN


def power_rows(first, last, unroll, X, V, EH, EV, PA, PB, PD):
    layers, height, width = X.shape
    groups = height // SUB
    share = jnp.where(iota((SUB, width), 0) % REFINE == REFINE - 1, 0.5, 1.0)
    lane_share = jnp.where(iota((SUB, width), 1) % REFINE == REFINE - 1, 1.0, 2.0)

    def fold(v):
        v = v + pltpu.roll(v, SUB - 1, 0)
        return v + pltpu.roll(v, SUB - 2, 0)

    def body(i):
        r = tile_rows(i)
        out = tile_rows(i + 1)
        xs = [X[l, r, :] for l in range(layers)]
        vs = load_vias(V, r)
        drops = [0.5 * vs[l] * (xs[l] - xs[l + 1]) ** 2 for l in range(layers - 1)]
        for l in range(layers):
            x = xs[l]
            across = x - pltpu.roll(x, width - 1, 1)
            down = x - shifted_down(x, X[l, tile_rows(after(i, groups)), :])
            across = 0.5 * EH[l, r, :] * (across * across)
            down = EV[l, r, :] * (down * down)
            total = leak_cond * (x * x) + share * down + lane_share * across
            if l < layers - 1:
                total = total + drops[l]
            if l > 0:
                total = total + drops[l - 1]
            total, across = fold(total), fold(across)
            for t in range(width // LANE):
                tile = slice(t * LANE, (t + 1) * LANE)
                PA[l, t, out, :] = total[:, tile]
                PB[l, t, out, :] = across[:, tile]
                PD[l, t, out, :] = down[:, tile]

    each(first, last, unroll, body)


def fold_power(row, cells, PA, PB, PD, same, left):
    layers = PA.shape[0]
    at = pl.ds(row + SUB, cells, stride=REFINE)
    up = pl.ds(row + SUB - 1, cells, stride=REFINE)
    tiles = range(PA.shape[1])
    a = [
        jnp.concatenate([PA[l, t, at, :] + 0.5 * PD[l, t, up, :] for t in tiles], 1)
        for l in range(layers)
    ]
    b = [jnp.concatenate([PB[l, t, at, :] for t in tiles], 1) for l in range(layers)]
    a, b = jnp.concatenate(a, 0), jnp.concatenate(b, 0)
    heat = (dot(a, same) + dot(b, left)) * heat_gain
    return [heat[l * cells : (l + 1) * cells] for l in range(layers)]


def fold_matrices(nodes, cells):
    n, c = iota((nodes, cells), 0), iota((nodes, cells), 1)
    same = lax.shift_right_logical(n, 2) == c
    return same.astype(jnp.float32), (n == REFINE * c - 1).astype(jnp.float32)


def bulk_first_kernel(
    x_ref, b_ref, w_ref, v_ref, f_ref, a_ref,
    g_ref, j_ref, XN, WN, D, DI, GD, JD, EH, EV, own_e, own_o,
    W0,
):
    layers, rows, cols = x_ref.shape
    _, cell_rows, cells = w_ref.shape
    spread_rows = gather_lanes(rows, cell_rows)
    spread = spread_lanes(cells, cols)
    for l in range(layers):
        warm = jnp.exp(-0.5 * warmth_sensitivity * w_ref[l])
        g_ref[l] = jnp.sqrt(b_ref[l]) * dot(spread_rows, dot(warm, spread))
        j_ref[l] = f_ref[l].astype(jnp.float32) * a_ref[l]
    pack_own_columns((x_ref, g_ref, j_ref, v_ref), w_ref, own_e, own_o)
    first_sweep(7, 1, x_ref, g_ref, j_ref, v_ref, W0, XN, WN, D, DI, GD, JD, EH, EV)


def bulk_mid_kernel(X, V, W, D, DI, GD, JD, G, XL, WN, XN, DN):
    (keep, gain), (keep_last, gain_last) = sweep_gains()
    next_sweep(7, 1, keep, gain, X, V, W, D, DI, GD, JD, G, XN, WN, DN)
    next_sweep(7, 1, keep_last, gain_last, XN, V, WN, DN, DI, GD, JD, G, XL)


def bulk_last_kernel(
    XN, V, EH, EV, xr_ref, xc_ref,
    x_hbm, h_ref,
    PA, PB, PD, out, sem,
):
    layers, rows, cols = XN.shape
    cell_rows, cells = h_ref.shape[1:]
    groups = rows // SUB
    lane = iota((rows, LANE), 1)
    low = iota((SUB, LANE), 0) < REACH
    for l in range(layers):
        for t in range(cols // LANE):
            tile = slice(t * LANE, (t + 1) * LANE)
            x = jnp.concatenate(
                [
                    xr_ref[l, 0:SUB, tile],
                    jnp.where(low, xr_ref[l, SUB : 2 * SUB, tile], XN[l, SUB : 2 * SUB, tile]),
                    XN[l, 2 * SUB : rows - 2 * SUB, tile],
                    jnp.where(
                        low,
                        XN[l, rows - 2 * SUB : rows - SUB, tile],
                        xr_ref[l, 2 * SUB : 3 * SUB, tile],
                    ),
                    xr_ref[l, 3 * SUB : 4 * SUB, tile],
                ],
                0,
            )
            if t == 0:
                x = jnp.where(lane < SUB, xc_ref[l], x)
            if t == cols // LANE - 1:
                x = jnp.where(lane >= LANE - SUB, xc_ref[l], x)
            out[l, :, tile] = x
    copy = pltpu.make_async_copy(out, x_hbm, sem)
    copy.start()
    power_rows(1, groups - 1, 7, XN, V, EH, EV, PA, PB, PD)
    heat = fold_power(0, cell_rows, PA, PB, PD, *fold_matrices(cols, cells))
    for l in range(layers):
        h_ref[l] = heat[l]
    copy.wait()


def row_strip_kernel(
    x_t, x_b, g_t, g_b, j_t, j_b, v_t, v_b,
    x_l, x_r, g_l, g_r, j_l, j_r, v_l, v_r,
    re_ref, ro_ref,
    xr_ref, h_ref, strip_ref,
    X, G, J, V, W0, XN, WN, D, DI, GD, JD, EH, EV, PA, PB, PD, DN, XL,
):
    layers, deep, cols = x_t.shape
    rows = x_l.shape[1]
    cells = h_ref.shape[2]
    half = 2 * layers
    height = 2 * (SUB + deep)
    plane = 0
    tall = strip_ref.shape[1]
    lane = iota((tall, LANE), 1)
    for top_ref, bot_ref, left_ref, right_ref, pad in (
        (x_t, x_b, x_l, x_r, X), (g_t, g_b, g_l, g_r, G), (j_t, j_b, j_l, j_r, J), (v_t, v_b, v_l, v_r, V),
    ):
        for l in range(top_ref.shape[0]):
            top, bot = row_margin(re_ref, ro_ref, plane, slice(0, cols), half)
            pad[l, 0:SUB, :] = top
            pad[l, SUB : SUB + deep, :] = top_ref[l].astype(jnp.float32)
            pad[l, SUB + deep : SUB + 2 * deep, :] = bot_ref[l].astype(jnp.float32)
            pad[l, SUB + 2 * deep : height, :] = bot
            left = jnp.concatenate([top[:, :LANE], left_ref[l].astype(jnp.float32), bot[:, :LANE]], 0)
            right = jnp.concatenate(
                [top[:, cols - LANE :], right_ref[l].astype(jnp.float32), bot[:, cols - LANE :]], 0
            )
            strip_ref[plane] = jnp.where(
                lane < LANE // 2,
                jnp.where(lane < LANE // 4, left[:tall], pltpu.roll(right[:tall], 48, 1)),
                jnp.where(
                    lane < 3 * LANE // 4,
                    pltpu.roll(left[rows + 2 * SUB - tall :], LOWER, 1),
                    pltpu.roll(right[rows + 2 * SUB - tall :], 48 + LOWER, 1),
                ),
            )
            plane += 1
    first_sweep(6, 0, X, G, J, V, W0, XN, WN, D, DI, GD, JD, EH, EV)
    later_sweeps(6, XN, V, WN, D, DI, GD, JD, G, W0, XL, DN)
    groups = height // SUB
    power_rows(0, groups - 1, 6, XL, V, EH, EV, PA, PB, PD)
    heat = fold_power(SUB, 2 * SUB // 2, PA, PB, PD, *fold_matrices(cols, cells))
    for l in range(layers):
        h_ref[l] = heat[l]
        xr_ref[l] = XL[l, SUB : height - SUB, :]


def col_strip_kernel(
    strip_ref, ce_ref, co_ref, hr_ref,
    xc_ref, hc_ref, hm_ref,
    X, G, J, V, W0, XN, WN, D, DI, GD, JD, EH, EV, PA, PB, PD, DN, XL,
):
    layers, rows, _ = xc_ref.shape
    cell_rows, cells = hc_ref.shape[1:]
    tall = strip_ref.shape[1]
    right, left = col_sides(ce_ref[0:tall, :], co_ref[0:tall, :])
    lane = iota((tall, LANE), 1)
    in_right = ((lane >= 48) & (lane < 48 + REACH)) | ((lane >= 48 + LOWER) & (lane < 48 + LOWER + REACH))
    in_left = (lane >= LANE - REACH) | ((lane >= LOWER - REACH) & (lane < LOWER))
    plane = 0
    for pad in (X, G, J, V):
        for l in range(pad.shape[0]):
            value = jnp.where(in_right, turned(right, 48 - 8 * plane), strip_ref[plane])
            pad[l] = jnp.where(in_left, turned(left, LANE - REACH - 8 * plane), value)
            plane += 1
    groups = tall // SUB
    first_sweep(groups, 0, X, G, J, V, W0, XN, WN, D, DI, GD, JD, EH, EV)
    later_sweeps(groups, XN, V, WN, D, DI, GD, JD, G, W0, XL, DN)
    power_rows(0, groups - 1, groups, XL, V, EH, EV, PA, PB, PD)
    n, c = iota((LANE, cells), 0), iota((LANE, cells), 1)
    at_edge = (c < REACH) | (c >= cells - REACH)
    halves = []
    for part in range(2):
        slot = jnp.where(c < cells // 2, c, c - cells + 12) + LOWER // REFINE * part
        same = at_edge & (lax.shift_right_logical(n, 2) == slot)
        left = at_edge & (n == jnp.where(slot == 0, LANE - 1, REFINE * slot - 1))
        halves.append(
            fold_power(
                SUB, cell_rows // 2, PA, PB, PD, same.astype(jnp.float32), left.astype(jnp.float32)
            )
        )
    lane = iota((rows // 2, LANE), 1)
    cell = iota((SUB, cells), 1)
    edge = (cell < REACH - 1) | (cell > cells - REACH)
    low = lane < LANE // 2
    for l in range(layers):
        first, final = halves[0][l], halves[1][l]
        hc_ref[l, 0 : cell_rows // 2, :] = first
        hc_ref[l, cell_rows // 2 : cell_rows, :] = final
        x = XL[l, SUB : SUB + rows // 2, :]
        xc_ref[l, 0 : rows // 2, :] = jnp.where(low, x, pltpu.roll(x, 80, 1))
        xc_ref[l, rows // 2 : rows, :] = jnp.where(low, turned(x, -LOWER), turned(x, 80 - LOWER))
        own = jnp.concatenate([first[:REACH], final[cell_rows // 2 - REACH :]], 0)
        hm_ref[l] = jnp.where(edge, own, hr_ref[l])


def heat_rows(own, e_ref, o_ref, l):
    even, above, below = place("row")
    e, o = e_ref[l], o_ref[l]
    pick = uniform(even, e.shape)
    top = jnp.where(uniform(above, e.shape), jnp.where(pick, o, e), 0.0)
    bot = jnp.where(uniform(below, e.shape), jnp.where(pick, e, o), 0.0)
    return jnp.concatenate([top, own, bot], axis=0)


def pack_heat_kernel(h_ref, re_ref, ro_ref, _, e_ref, o_ref):
    layers, cell_rows, cells = h_ref.shape
    height = cell_rows + 2 * SUB
    even, _, _ = place("col")
    lane = iota((height, LANE), 1)
    slot, low = lax.shift_right_logical(lane, 3), lane % 8 < REACH
    left = right = jnp.zeros((height, LANE), jnp.float32)
    for l in range(layers):
        value = heat_rows(h_ref[l], re_ref, ro_ref, l)
        mine = (slot == l) & low
        left = jnp.where(mine, pltpu.roll(value[:, :LANE], 8 * l, 1) if l else value[:, :LANE], left)
        right = jnp.where(mine, pltpu.roll(value[:, cells - LANE :], 8 * l + REACH, 1), right)
    pick = uniform(even, (height, LANE))
    e_ref[...] = jnp.where(pick, right, left)
    o_ref[...] = jnp.where(pick, left, right)


def warm_kernel(
    w_ref, h_ref, hm_ref, hc_ref, re_ref, ro_ref, ce_ref, co_ref,
    hre_ref, hro_ref, hce_ref, hco_ref, out_ref,
):
    layers, cell_rows, cells = w_ref.shape
    half = 2 * layers
    height, width = cell_rows + 2 * SUB, cells + LANE
    tall = ce_ref.shape[0]
    right, left = col_sides(ce_ref[tall - SUB : tall, :], co_ref[tall - SUB : tall, :])
    lane = iota((SUB, LANE), 1)
    heat_mixed = col_margin(hce_ref[...], hco_ref[...], False, REACH)
    cell = iota((cell_rows, cells), 1)
    edge = (cell < REACH - 1) | (cell > cells - REACH)
    cell_row = iota((SUB, cells), 0)
    theta, heat = [], []
    for l in range(layers):
        top, bot = row_margin(
            re_ref, ro_ref, 2 * half - 1, slice(l * cells, (l + 1) * cells), half
        )
        own = jnp.concatenate([top, w_ref[l], bot], axis=0)
        pieces = []
        for k in range(height // SUB):
            at = 16 * k + REACH * l
            value = jnp.where(lane < REACH, turned(right, -at), 0.0)
            pieces.append(jnp.where(lane >= LANE - REACH, turned(left, -REACH - at), value))
        theta.append(jnp.concatenate([own, jnp.concatenate(pieces, axis=0)], axis=1))
        own = jnp.where(edge, hc_ref[l], h_ref[l])
        first, final = own[:SUB], own[cell_rows - SUB :]
        first = jnp.where(cell_row < REACH - 1, hm_ref[l], first)
        final = jnp.where(cell_row > SUB - REACH, hm_ref[l], final)
        own = jnp.concatenate([first, own[SUB : cell_rows - SUB], final], axis=0)
        own = heat_rows(own, hre_ref, hro_ref, l)
        heat.append(jnp.concatenate([own, margin_tile(heat_mixed, 8 * l)], axis=1))
    _, above, below = place("row")
    _, before, after = place("col")
    shape = (height, width)
    r, c = iota(shape, 0), iota(shape, 1)
    inside = (uniform(above, shape) | (r >= SUB)) & (uniform(below, shape) | (r < height - SUB))
    inside = inside & (uniform(after, shape) | (c < cells) | (c >= cells + LANE // 2))
    inside = inside & (uniform(before, shape) | (c < cells + LANE // 2))

    def around_cells(v):
        return (pltpu.roll(v, 1, 0) + pltpu.roll(v, height - 1, 0)) + (
            pltpu.roll(v, 1, 1) + pltpu.roll(v, width - 1, 1)
        )

    for _ in range(HEAT_SWEEPS):
        later = []
        for l in range(layers):
            t = theta[l]
            q = jnp.where(inside, jnp.exp(-0.5 * warming_weight * t), 0.0)
            change = q * (around_cells(q * t) - t * around_cells(q)) + heat[l]
            if l < layers - 1:
                change = change + (theta[l + 1] - t)
            if l > 0:
                change = change + (theta[l - 1] - t)
            if l == layers - 1:
                change = change - t
            later.append(t + interval_length * change)
        theta = later
    for l in range(layers):
        out_ref[l] = theta[l][SUB : SUB + cell_rows, :cells]


def on_device(x, base, warm, via, feeder, amps):
    layers, rows, cols = x.shape
    _, cell_rows, cells = warm.shape
    f32 = jnp.float32
    mesh_rows, mesh_cols = lax.axis_size("row"), lax.axis_size("col")
    last_row, last_cell_row, last_col = rows // SUB - 1, cell_rows // SUB - 1, cols // LANE - 1

    def shape(*dims):
        return jax.ShapeDtypeStruct(dims, f32)

    def edge_rows(a, at):
        return pl.BlockSpec((a.shape[0], SUB, a.shape[2]), lambda _, at=at: (0, at, 0))

    def edge_cols(a, at):
        return pl.BlockSpec((a.shape[0], a.shape[1], LANE), lambda _, at=at: (0, 0, at))

    def full(a):
        return pl.BlockSpec(a.shape, lambda _, n=len(a.shape): (0,) * n)

    def swap(e, o, tables):
        return tuple(
            lax.ppermute(m, BOTH, tables(mesh_rows, mesh_cols, first)) for first, m in enumerate((e, o))
        )

    params = pltpu.CompilerParams(vmem_limit_bytes=24 * 1024 * 1024)
    row_args, row_specs = [], []
    for a in (x, base, warm, via, feeder, amps):
        end = last_cell_row if a is warm else last_row
        row_args += [a, a]
        row_specs += [edge_rows(a, 0), edge_rows(a, end)]
    message = shape(2 * layers, SUB, cols)
    e, o = pl.pallas_call(
        pack_rows_kernel,
        grid=(1,),
        in_specs=row_specs,
        out_specs=(full(message), full(message)),
        out_shape=(message, message),
        compiler_params=pltpu.CompilerParams(vmem_limit_bytes=58 * 1024 * 1024),
        name="pack_rows",
    )(*row_args)
    row_e, row_o = swap(e, o, row_swaps)

    fields = (shape(layers, rows, cols),) * 10 + (shape(rows // 2 + 3 * SUB, LANE),) * 2
    node_scratch = pltpu.VMEM((layers, rows, cols), f32)
    g, inject, *mid = pl.pallas_call(
        bulk_first_kernel,
        out_shape=fields,
        scratch_shapes=[node_scratch],
        compiler_params=params,
        name="bulk_first",
        cost_estimate=pl.CostEstimate(flops=40 * x.size, bytes_accessed=60 * x.size, transcendentals=0),
    )(x, base, warm, via, feeder, amps)
    x_mid, w_mid, d_mid, inv_diag, g_diag, j_diag, edge_h, edge_v, own_e, own_o = mid

    col_args, col_specs = [], []
    for a in (x, g, inject, via):
        col_args += [a, a]
        col_specs += [edge_cols(a, 0), edge_cols(a, last_col)]
    message = shape(rows // 2 + 3 * SUB, LANE)
    e, o = pl.pallas_call(
        pack_cols_kernel,
        out_shape=(message, message),
        compiler_params=params,
        name="pack_cols",
    )(row_e, row_o, own_e, own_o, warm)
    col_e, col_o = swap(e, o, col_swaps)

    def strip_scratch(height, width):
        node = pltpu.VMEM((layers, height, width), f32)
        taller = pltpu.VMEM((layers, width // LANE, height + SUB, LANE), f32)
        return [node] * 3 + [pltpu.VMEM((layers - 1, height, width), f32)] + [node] * 9 + [taller] * 3 + [node] * 2

    def edge_deep(a, at):
        return pl.BlockSpec((a.shape[0], 2 * SUB, a.shape[2]), lambda _, at=at: (0, at, 0))

    deep_args, deep_specs = [], []
    for a in (x, g, inject, via):
        deep_args += [a, a]
        deep_specs += [edge_deep(a, 0), edge_deep(a, rows // (2 * SUB) - 1)]
    edge_x, edge_h2 = shape(layers, 4 * SUB, cols), shape(layers, SUB, cells)
    strip = shape(4 * layers - 1, rows // 2 + 2 * SUB, LANE)
    x_rows, heat_strip, strip = pl.pallas_call(
        row_strip_kernel,
        grid=(1,),
        in_specs=deep_specs + col_specs + [full(row_e), full(row_o)],
        out_specs=(full(edge_x), full(edge_h2), full(strip)),
        out_shape=(edge_x, edge_h2, strip),
        scratch_shapes=strip_scratch(6 * SUB, cols),
        compiler_params=params,
        name="row_strip",
        cost_estimate=pl.CostEstimate(flops=40 * x.size, bytes_accessed=20 * x.size, transcendentals=0),
    )(*deep_args, *col_args, row_e, row_o)

    x_cols, heat_cols, heat_edge = pl.pallas_call(
        col_strip_kernel,
        out_shape=(shape(layers, rows, LANE), shape(layers, cell_rows, cells), edge_h2),
        scratch_shapes=strip_scratch(rows // 2 + 2 * SUB, LANE),
        compiler_params=params,
        name="col_strip",
    )(strip, col_e, col_o, heat_strip)
    heat_row_e, heat_row_o = swap(heat_edge, heat_edge, row_swaps)

    assert SWEEPS == 3
    x_done = pl.pallas_call(
        bulk_mid_kernel,
        out_shape=shape(layers, rows, cols),
        scratch_shapes=[node_scratch] * 3,
        compiler_params=params,
        name="bulk_mid",
        cost_estimate=pl.CostEstimate(flops=20 * x.size, bytes_accessed=20 * x.size, transcendentals=0),
    )(x_mid, via, w_mid, d_mid, inv_diag, g_diag, j_diag, g)

    message = shape(cell_rows + 2 * SUB, LANE)
    e, o = pl.pallas_call(
        pack_heat_kernel,
        in_specs=[pl.BlockSpec(memory_space=pltpu.VMEM)] * 3 + [pl.BlockSpec(memory_space=pl.ANY)],
        out_shape=(message, message),
        compiler_params=params,
        name="pack_heat",
    )(heat_cols, heat_row_e, heat_row_o, x_done)
    heat_col_e, heat_col_o = swap(e, o, col_swaps)

    tall = pltpu.VMEM((layers, cols // LANE, rows + SUB, LANE), f32)
    voltage, heat = pl.pallas_call(
        bulk_last_kernel,
        out_shape=(shape(layers, rows, cols), shape(layers, cell_rows, cells)),
        out_specs=(pl.BlockSpec(memory_space=pl.ANY), pl.BlockSpec(memory_space=pltpu.VMEM)),
        scratch_shapes=[tall] * 3 + [node_scratch, pltpu.SemaphoreType.DMA],
        compiler_params=params,
        name="bulk_last",
        cost_estimate=pl.CostEstimate(flops=40 * x.size, bytes_accessed=60 * x.size, transcendentals=0),
    )(x_done, via, edge_h, edge_v, x_rows, x_cols)

    warmth = pl.pallas_call(
        warm_kernel,
        out_shape=shape(layers, cell_rows, cells),
        compiler_params=params,
        name="warm",
    )(warm, heat, heat_edge, heat_cols, row_e, row_o, col_e, col_o, heat_row_e, heat_row_o, heat_col_e, heat_col_o)
    return voltage, warmth


def solution(mesh):
    placed = P(None, "row", "col")
    return jax.shard_map(
        on_device,
        mesh=mesh,
        in_specs=(placed,) * 6,
        out_specs=(placed, placed),
        check_vma=False,
    )
```
